128 devices in a mesh: grp: 8 (over z, x_lo), sp: 16 (over y, x_hi, core).
Axes of the slice: x: 4 (x_hi: 2, x_lo: 2; x = x_hi * 2 + x_lo), y: 4, z: 4, core: 2. Of those that a mesh axis runs over, the one named last changes fastest.
Arguments:
- patches: bfloat16 [8, 64, 128, 1280], P('grp', 'sp'), may hold values from -9 to 9, as said below
- conv_w: bfloat16 [3, 3, 1280], replicated, may hold values from -3 to 3
- w_qkv: bfloat16 [1280, 3840], replicated, as said below
- w_out: bfloat16 [1280, 1280], replicated, may hold values from -0.15625 to 0.15625
- cotangent: bfloat16 [8, 64, 128, 1280], P('grp', 'sp'), may hold values from -6 to 6
Outputs:
- layer_out: bfloat16 [8, 64, 128, 1280], P('grp', 'sp')
- grad_patches: bfloat16 [8, 64, 128, 1280], P('grp', 'sp')
- dw_qkv: float32 [1280, 3840], P(None, ('grp', 'sp'))
- dw_out: float32 [1280, 1280], P(None, ('grp', 'sp'))
- grad_conv: float32 [3, 3, 1280], P(None, None, ('grp', 'sp'))
The draws below stay inside these ranges and needn't reach their ends.
Inputs may be any that keep to these rules, and one draw needn't show every extreme that they name: `patches`: patch embeddings of order one. `w_qkv`: entries within 7 / sqrt(1280) in magnitude.
All inputs are finite; a program needn't handle non-finite values.
Results may differ from the reference program's by a relative error of at most 0.013.
The reference program's roundings to bfloat16 on the way count: a program that leaves them out, or rounds other values in their place, can miss the bound.
Values may be sent and summed in bfloat16 or wider, within the bound.
No kernel may reach another device: no remote copies, remote signals or barrier semaphores. Data moves between devices by JAX's collectives and lax.ppermute only.
A program may use at most 128 MiB of HBM per device.

```python
import math
import jax
import jax.numpy as jnp
from jax import lax

HEADS = 16
HDIM = 80
D = 1280
WIDTH = 128
ROWS = 64
SCENES = 8


def draw_patches(key, part):
    key = jax.random.fold_in(key, 101)
    values = jnp.clip(jax.random.normal(key, (SCENES, ROWS, WIDTH, D), jnp.float32), -6.0, 6.0)
    return jnp.clip(values, -9.0, 9.0).astype(jnp.bfloat16)


def draw_w_qkv(key, part):
    key = jax.random.fold_in(key, 202)
    values = jnp.clip(jax.random.normal(key, (D, 3 * D), jnp.float32), -3.0, 3.0) * D ** (-0.5)
    return values.astype(jnp.bfloat16)


def with_spikes(values, rng, source, target, shards_of, factor):
    def block_of(position):
        return (jnp.arange(values.shape[position]) // (values.shape[position] // shards_of)).reshape((-1,) + (1,) * (values.ndim - 1 - position))

    first = jax.random.permutation(rng, shards_of)[block_of(target)]
    far = (block_of(target) + shards_of // 2) % shards_of
    return jnp.where((block_of(source) == first) | (block_of(source) == far), factor * values, values)


def block_scale(rng, extent, pieces, least, top_value):
    gain, own = 1.0, jax.random.fold_in(rng, 6)
    for dim, shards_of in pieces:
        heights = jnp.exp(jax.random.uniform(jax.random.fold_in(own, dim), (shards_of,), jnp.float32, least / len(pieces), top_value / len(pieces)))
        gain = gain * jnp.repeat(heights, extent[dim] // shards_of).reshape([-1 if axis == dim else 1 for axis in range(len(extent))])
    return gain


def normal_values(own_key, dims, scale, reach, pieces=(), kind=jnp.bfloat16):
    values = jax.random.normal(own_key, dims, jnp.float32) * scale
    if len(pieces) > 0:
        values = block_scale(own_key, dims, pieces, -0.22, 0.18) * values
    return jnp.clip(values, min=-reach, max=reach).astype(kind)


def bell_draw_with(key, extent, deviation, reach, pieces, heavy, kind=jnp.bfloat16):
    array = deviation * jax.random.normal(key, extent, jnp.float32)
    if pieces:
        array = array * block_scale(key, extent, pieces, -0.22, 0.18)
    return jnp.clip(with_spikes(array, jax.random.fold_in(key, 3), *heavy), -reach, reach).astype(kind)


def setup_inputs(seed: int = 0) -> dict:
    splits = jax.random.split(jax.random.key(seed), 6)
    return {
        "patches": draw_patches(jax.random.fold_in(splits[5], 71), 0),
        "conv_w": normal_values(splits[1], (3, 3, D), 0.25, 3.0),
        "w_qkv": draw_w_qkv(jax.random.fold_in(splits[5], 71), 0),
        "w_out": normal_values(splits[3], (D, D), D ** -0.5, 0.15625),
        "cotangent": bell_draw_with(splits[4], (SCENES, ROWS, WIDTH, D), 1.0, 6.0, ((0, 8), (1, 16)), (1, 3, 16, 2.0)),
    }


def frequencies():
    half = HDIM // 2
    base = 10000.0 * 4.0 ** (HDIM / (HDIM - 2.0))
    steps = jnp.arange(half, dtype=jnp.float32)
    return jnp.exp(-(2.0 * steps / HDIM) * math.log(base))

def tables(count):
    angle = jnp.arange(count, dtype=jnp.float32)[:, None] * frequencies()[None, :]
    return (jnp.cos(angle), jnp.sin(angle))

def rotate(value, cosine, sine, sign):
    half = HDIM // 2
    first = value[..., :half]
    second = value[..., half:]
    return jnp.concatenate([first * cosine - sign * second * sine, second * cosine + sign * first * sine], axis=-1)

def forms(seq_first):
    if seq_first:
        left, right = ('ibhd', 'jbhd')
    else:
        left, right = ('bihd', 'bjhd')
    return (left + ',' + right + '->bhij', 'bhij,' + right + '->' + left, 'bhij,' + left + '->' + right)

def matmul(form, first, second):
    first = lax.optimization_barrier(first).astype(jnp.float32)
    second = lax.optimization_barrier(second).astype(jnp.float32)
    return jnp.einsum(form, first, second)

def probs(query, key, seq_first):
    scores = matmul(forms(seq_first)[0], query, key) / math.sqrt(HDIM)
    top = lax.optimization_barrier(jnp.max(scores, axis=-1, keepdims=True))
    expo = jnp.exp(scores - top)
    return expo / lax.optimization_barrier(jnp.sum(expo, axis=-1, keepdims=True))

def attend(weights, value, seq_first):
    return matmul(forms(seq_first)[1], weights.astype(jnp.bfloat16), value).astype(jnp.bfloat16)

def backward(weights, query, key, value, grad_o, seq_first):
    form_s, form_o, form_t = forms(seq_first)
    grad_v = matmul(form_t, weights.astype(jnp.bfloat16), grad_o).astype(jnp.bfloat16)
    grad_p = matmul(form_s, grad_o, value)
    delta = lax.optimization_barrier(jnp.sum(weights * grad_p, axis=-1, keepdims=True))
    grad_s = (weights * (grad_p - delta) / math.sqrt(HDIM)).astype(jnp.bfloat16)
    return (matmul(form_o, grad_s, key), matmul(form_t, grad_s, query), grad_v)

def scene(x_one, cot_one, conv_w, w_qkv, w_out):
    rows, width = (x_one.shape[0], x_one.shape[1])
    heads_half = HEADS // 2
    kernel = conv_w.astype(jnp.float32)
    x_float = x_one.astype(jnp.float32)
    padded = jnp.pad(x_float, ((1, 1), (1, 1), (0, 0)))
    mixed = x_float
    for row_off in range(3):
        for col_off in range(3):
            mixed = mixed + kernel[row_off, col_off] * padded[row_off:row_off + rows, col_off:col_off + width]
    y_val = mixed.astype(jnp.bfloat16)
    y_flat = y_val.reshape(rows * width, D)
    qkv = jnp.dot(y_flat, w_qkv, preferred_element_type=jnp.float32).astype(jnp.bfloat16)
    qkv = qkv.reshape(rows, width, 3, HEADS, HDIM)
    cos_w, sin_w = tables(width)
    cos_h, sin_h = tables(rows)

    def turn(value, sign):
        row_part = rotate(value[:, :, :heads_half], cos_w[None, :, None], sin_w[None, :, None], sign)
        col_part = rotate(value[:, :, heads_half:], cos_h[:, None, None], sin_h[:, None, None], sign)
        return (row_part.astype(jnp.bfloat16), col_part.astype(jnp.bfloat16))
    q_row, q_col = turn(qkv[:, :, 0].astype(jnp.float32), 1.0)
    k_row, k_col = turn(qkv[:, :, 1].astype(jnp.float32), 1.0)
    v_row = qkv[:, :, 2, :heads_half]
    v_col = qkv[:, :, 2, heads_half:]
    p_row = probs(q_row, k_row, False)
    p_col = probs(q_col, k_col, True)
    o_row = attend(p_row, v_row, False)
    o_col = attend(p_col, v_col, True)
    attn = jnp.concatenate([o_row, o_col], axis=2).reshape(rows * width, D)
    result = (y_flat.astype(jnp.float32) + jnp.dot(attn, w_out, preferred_element_type=jnp.float32)).astype(jnp.bfloat16)
    grad_flat = cot_one.reshape(rows * width, D)
    d_attn = jnp.dot(grad_flat, w_out.T, preferred_element_type=jnp.float32).astype(jnp.bfloat16)
    gw_out = jnp.dot(attn.T, grad_flat, preferred_element_type=jnp.float32)
    d_attn = d_attn.reshape(rows, width, HEADS, HDIM)
    dq_row, dk_row, dv_row = backward(p_row, q_row, k_row, v_row, d_attn[:, :, :heads_half], False)
    dq_col, dk_col, dv_col = backward(p_col, q_col, k_col, v_col, d_attn[:, :, heads_half:], True)

    def unturn(row_part, col_part):
        row_back = rotate(row_part, cos_w[None, :, None], sin_w[None, :, None], -1.0)
        col_back = rotate(col_part, cos_h[:, None, None], sin_h[:, None, None], -1.0)
        return jnp.concatenate([row_back, col_back], axis=2).astype(jnp.bfloat16)
    grad_q = unturn(dq_row, dq_col)
    grad_k = unturn(dk_row, dk_col)
    grad_v = jnp.concatenate([dv_row, dv_col], axis=2)
    dqkv = jnp.stack([grad_q, grad_k, grad_v], axis=2).reshape(rows * width, 3 * D)
    gw_qkv = jnp.dot(y_flat.T, dqkv, preferred_element_type=jnp.float32)
    d_y = (grad_flat.astype(jnp.float32) + jnp.dot(dqkv, w_qkv.T, preferred_element_type=jnp.float32)).astype(jnp.bfloat16)
    d_y = d_y.reshape(rows, width, D)
    dy_float = d_y.astype(jnp.float32)
    grad_pad = jnp.pad(dy_float, ((1, 1), (1, 1), (0, 0)))
    grad_x = dy_float
    for row_off in range(3):
        for col_off in range(3):
            grad_x = grad_x + kernel[row_off, col_off] * grad_pad[2 - row_off:2 - row_off + rows, 2 - col_off:2 - col_off + width]
    gconv = jnp.stack([jnp.stack([lax.optimization_barrier(jnp.sum(padded[row_off:row_off + rows, col_off:col_off + width] * dy_float, axis=(0, 1))) for col_off in range(3)]) for row_off in range(3)])
    return (result.reshape(rows, width, D), grad_x.astype(jnp.bfloat16), gw_qkv, gw_out, gconv)

def reference(patches, conv_w, w_qkv, w_out, cotangent):

    def step(carry, pair):
        result, grad_x, gw_qkv, gw_out, gconv = scene(pair[0], pair[1], conv_w, w_qkv, w_out)
        return ((carry[0] + gw_qkv, carry[1] + gw_out, carry[2] + gconv), (result, grad_x))
    start = (jnp.zeros((D, 3 * D), jnp.float32), jnp.zeros((D, D), jnp.float32), jnp.zeros((3, 3, D), jnp.float32))
    sums, stacked = lax.scan(step, start, (patches, cotangent))
    factor = 1.0 / math.sqrt(patches.shape[0] * patches.shape[1] * patches.shape[2])
    return (stacked[0], stacked[1], sums[0] * factor, sums[1] * factor, sums[2] * factor)
```

```python
import functools
import math

import jax
import jax.numpy as jnp
import numpy as np
from jax import lax
from jax.experimental import pallas as pl
from jax.experimental.pallas import tpu as pltpu
from jax.sharding import PartitionSpec as P

HEADS = 16
HDIM = 80
D = 1280
HALF = 640
ROWS = 4
WIDTH = 128
TOK = ROWS * WIDTH
AXES = ("grp", "sp")
BF = jnp.bfloat16
F32 = jnp.float32
MIB = 1024 * 1024

CHUNK = 40
PARTS = (512, 384, 384)
ORDERS = ("xyz", "yzx", "zxy")


def place(index):
    return {
        "z": index // 32,
        "y": (index // 4) % 4,
        "x": ((index // 2) % 2) * 2 + (index // 16) % 2,
        "c": index % 2,
    }


def pairs(axis, offset):
    count = 2 if axis == "c" else 4
    out = []
    for index in range(128):
        to = place(index)
        to[axis] = (to[axis] + offset) % count
        target = to["z"] * 32 + (to["x"] % 2) * 16 + to["y"] * 4 + (to["x"] // 2) * 2 + to["c"]
        out.append((index, target))
    return out


def hop(value, axis, offset):
    return lax.ppermute(value, AXES, pairs(axis, offset))


def dot(a, b):
    return lax.dot_general(a, b, (((1,), (0,)), ((), ())), preferred_element_type=F32)


def dot_nt(a, b):
    return lax.dot_general(a, b, (((1,), (1,)), ((), ())), preferred_element_type=F32)


def dot_tn(a, b):
    return lax.dot_general(a, b, (((0,), (0,)), ((), ())), preferred_element_type=F32)


def params(limit):
    return pltpu.CompilerParams(vmem_limit_bytes=limit * MIB)


def shifted(value, step):
    index = lax.broadcasted_iota(jnp.int32, value.shape, 0)
    moved = pltpu.roll(value, step % WIDTH, axis=0)
    edge = 0 if step == 1 else WIDTH - 1
    return jnp.where(index == edge, 0.0, moved)


def conv_kernel(x_ref, top_ref, bot_ref, k_ref, y_ref, send_ref):
    taps = k_ref[...].astype(F32)
    rows = [top_ref[0].astype(F32)]
    rows += [x_ref[r].astype(F32) for r in range(ROWS)]
    rows += [bot_ref[0].astype(F32)]
    for r in range(ROWS):
        sums = []
        for b in range(3):
            total = taps[b : b + 1] * rows[r]
            total += taps[3 + b : 4 + b] * rows[r + 1]
            total += taps[6 + b : 7 + b] * rows[r + 2]
            sums.append(total)
        out = rows[r + 1] + sums[1] + shifted(sums[0], 1) + shifted(sums[2], -1)
        y_ref[r] = out.astype(BF)
        send_ref[:, r] = out.reshape(16, 8, out.shape[-1]).astype(BF)


def conv_forward(x, top, bot, taps):
    block = 256
    grid = (D // block,)
    row = pl.BlockSpec((1, WIDTH, block), lambda i: (0, 0, i))
    return pl.pallas_call(
        conv_kernel,
        grid=grid,
        in_specs=[
            pl.BlockSpec((ROWS, WIDTH, block), lambda i: (0, 0, i)),
            row,
            row,
            pl.BlockSpec((9, block), lambda i: (0, i)),
        ],
        out_specs=[
            pl.BlockSpec((ROWS, WIDTH, block), lambda i: (0, 0, i)),
            pl.BlockSpec((16, ROWS, 8, block), lambda i: (0, 0, 0, i)),
        ],
        out_shape=[
            jax.ShapeDtypeStruct((ROWS, WIDTH, D), BF),
            jax.ShapeDtypeStruct((16, ROWS, 8, D), BF),
        ],
        compiler_params=params(32),
    )(x, top, bot, taps)


def conv_back_kernel(x_ref, top_ref, bot_ref, dy_ref, dtop_ref, dbot_ref, k_ref, gx_ref, gk_ref):
    taps = k_ref[...].astype(F32)
    rows = [top_ref[0].astype(F32)]
    rows += [x_ref[r].astype(F32) for r in range(ROWS)]
    rows += [bot_ref[0].astype(F32)]
    grads = [dtop_ref[0].astype(F32)]
    grads += [dy_ref[r].astype(F32) for r in range(ROWS)]
    grads += [dbot_ref[0].astype(F32)]
    gains = [None] * 9
    for r in range(ROWS):
        sums = []
        for b in range(3):
            total = taps[b : b + 1] * grads[r + 2]
            total += taps[3 + b : 4 + b] * grads[r + 1]
            total += taps[6 + b : 7 + b] * grads[r]
            sums.append(total)
        mid = grads[r + 1]
        gx_ref[r] = (mid + sums[1] + shifted(sums[0], -1) + shifted(sums[2], 1)).astype(BF)
        near = (shifted(mid, -1), mid, shifted(mid, 1))
        for a in range(3):
            for b in range(3):
                term = rows[r + a] * near[b]
                slot = a * 3 + b
                gains[slot] = term if gains[slot] is None else gains[slot] + term
    for slot in range(9):
        gk_ref[slot : slot + 1] = jnp.sum(gains[slot], axis=0, keepdims=True)


def conv_backward(x, top, bot, dy, dtop, dbot, taps):
    block = 128
    grid = (D // block,)
    row = pl.BlockSpec((1, WIDTH, block), lambda i: (0, 0, i))
    slab = pl.BlockSpec((ROWS, WIDTH, block), lambda i: (0, 0, i))
    small = pl.BlockSpec((9, block), lambda i: (0, i))
    return pl.pallas_call(
        conv_back_kernel,
        grid=grid,
        in_specs=[slab, row, row, slab, row, row, small],
        out_specs=[slab, small],
        out_shape=[
            jax.ShapeDtypeStruct((ROWS, WIDTH, D), BF),
            jax.ShapeDtypeStruct((9, D), F32),
        ],
        compiler_params=params(32),
    )(x, top, bot, dy, dtop, dbot, taps)


def attention(block, q_s, k_s, v_s, d_s, cos, sin, mask, both, o_ref, g_ref):
    scale = 1.0 / math.sqrt(HDIM)
    toks = pl.ds(pl.multiple_of(block * 128, 128), 128)
    for h in range(HEADS // 2):
        cols = slice(h * HDIM, (h + 1) * HDIM)
        q = q_s[toks, cols]
        k = k_s[toks, cols]
        v = v_s[toks, cols]
        d_o = d_s[toks, cols]
        q2 = dot(q, both)
        k2 = dot(k, both)
        qr = (q2[:, :HDIM] * cos + q2[:, 128 : 128 + HDIM] * sin).astype(BF)
        kr = (k2[:, :HDIM] * cos + k2[:, 128 : 128 + HDIM] * sin).astype(BF)
        qq = dot(qr, both).astype(BF)
        kk = dot(kr, both).astype(BF)
        scores = dot_nt(qr, kr) * scale
        if mask is not None:
            scores = scores + mask
        top = jnp.max(scores, axis=-1, keepdims=True)
        expo = jnp.exp(scores - top)
        prob = expo / jnp.sum(expo, axis=-1, keepdims=True)
        prob_b = prob.astype(BF)
        o_ref[toks, cols] = dot(prob_b, v).astype(BF)
        g_ref[toks, slice(2 * HALF + h * HDIM, 2 * HALF + (h + 1) * HDIM)] = dot_tn(
            prob_b, d_o
        ).astype(BF)
        d_p = dot_nt(d_o, v)
        delta = jnp.sum(prob * d_p, axis=-1, keepdims=True)
        d_s_b = (prob * (d_p - delta) * scale).astype(BF)
        dq = dot(d_s_b, kk)
        g_ref[toks, cols] = (dq[:, :HDIM] * cos - dq[:, 128 : 128 + HDIM] * sin).astype(BF)
        dk = dot_tn(d_s_b, qq)
        g_ref[toks, slice(HALF + h * HDIM, HALF + (h + 1) * HDIM)] = (
            dk[:, :HDIM] * cos - dk[:, 128 : 128 + HDIM] * sin
        ).astype(BF)


def row_kernel(
    y_ref, c_ref, wq_ref, wk_ref, wv_ref, wo_ref, cos_ref, sin_ref, both_ref,
    o_ref, g_ref, out_ref, dy_ref, q_s, k_s, v_s, d_s,
):
    y = y_ref[...]
    cot = c_ref[...]
    q_s[...] = dot(y, wq_ref[...]).astype(BF)
    k_s[...] = dot(y, wk_ref[...]).astype(BF)
    v_s[...] = dot(y, wv_ref[...]).astype(BF)
    d_s[...] = dot_nt(cot, wo_ref[...]).astype(BF)

    @pl.loop(0, TOK // 128)
    def _(block):
        attention(
            block, q_s, k_s, v_s, d_s, cos_ref[...], sin_ref[...], None, both_ref[...], o_ref, g_ref
        )

    out_ref[...] = y.astype(F32) + dot(o_ref[...], wo_ref[...])
    dy_ref[...] = (
        cot.astype(F32)
        + dot_nt(g_ref[:, :HALF], wq_ref[...])
        + dot_nt(g_ref[:, HALF : 2 * HALF], wk_ref[...])
        + dot_nt(g_ref[:, 2 * HALF :], wv_ref[...])
    )


def col_kernel(
    y_ref, c_ref, wq_ref, wk_ref, wv_ref, wo_ref, cos_ref, sin_ref, both_ref, mask_ref, perm_ref,
    yp_ref, cp_ref, o_ref, g_ref, back_ref, q_s, k_s, v_s, d_s,
):
    yp_ref[...] = dot(perm_ref[...], y_ref[...]).astype(BF)
    cp_ref[...] = dot(perm_ref[...], c_ref[...]).astype(BF)
    y = yp_ref[...]
    q_s[...] = dot(y, wq_ref[...]).astype(BF)
    k_s[...] = dot(y, wk_ref[...]).astype(BF)
    v_s[...] = dot(y, wv_ref[...]).astype(BF)
    d_s[...] = dot_nt(cp_ref[...], wo_ref[...]).astype(BF)

    @pl.loop(0, TOK // 128)
    def _(block):
        attention(
            block, q_s, k_s, v_s, d_s, cos_ref[...], sin_ref[...], mask_ref[...], both_ref[...],
            o_ref, g_ref,
        )

    part = (
        dot_nt(g_ref[:, :HALF], wq_ref[...])
        + dot_nt(g_ref[:, HALF : 2 * HALF], wk_ref[...])
        + dot_nt(g_ref[:, 2 * HALF :], wv_ref[...])
    ).astype(BF)
    back_ref[:, :HALF] = dot_tn(perm_ref[...], o_ref[...]).astype(BF)
    back_ref[:, HALF:] = dot_tn(perm_ref[...], part).astype(BF)


def whole(shape):
    return pl.BlockSpec(shape, lambda i: (0,) * len(shape))


def attention_call(kernel, half, y, cot, w_qkv, w_out, tables, outs):
    def columns(which):
        return pl.BlockSpec((D, HALF), lambda i: (0, 2 * which + half))

    return pl.pallas_call(
        kernel,
        grid=(1,),
        in_specs=[
            whole((TOK, D)),
            whole((TOK, D)),
            columns(0),
            columns(1),
            columns(2),
            pl.BlockSpec((HALF, D), lambda i: (half, 0)),
        ]
        + [whole(t.shape) for t in tables],
        out_specs=[whole(s) for s, _ in outs],
        out_shape=[jax.ShapeDtypeStruct(s, t) for s, t in outs],
        scratch_shapes=[pltpu.VMEM((TOK, HALF), BF)] * 4,
        compiler_params=params(60),
    )(y, cot, w_qkv, w_qkv, w_qkv, w_out, *tables)


def angle_tables(positions):
    half = HDIM // 2
    base = 10000.0 * 4.0 ** (HDIM / (HDIM - 2.0))
    steps = np.arange(half, dtype=np.float32)
    freq = np.exp(-(2.0 * steps / HDIM) * np.float32(math.log(base))).astype(np.float32)
    angle = positions.astype(np.float32)[:, None] * freq[None, :]
    cos = np.cos(angle).astype(np.float32)
    sin = np.sin(angle).astype(np.float32)
    return jnp.asarray(np.concatenate([cos, cos], 1)), jnp.asarray(np.concatenate([sin, sin], 1))


def turn_matrix():
    half = HDIM // 2
    out = np.zeros((HDIM, 256), np.float32)
    for j in range(HDIM):
        out[j, j] = 1.0
    for j in range(half):
        out[j + half, 128 + j] = -1.0
        out[j, 128 + half + j] = 1.0
    return jnp.asarray(out, BF)


def col_order():
    order = np.zeros((TOK, TOK), np.float32)
    for pair in range(4):
        for src in range(16):
            for c in range(2):
                for r in range(ROWS):
                    order[pair * 128 + src * 8 + c * 4 + r, src * 32 + r * 8 + pair * 2 + c] = 1.0
    token = np.arange(128)
    positions = (token // 8) * 4 + token % 4
    column = (token // 4) % 2
    mask = np.where(column[:, None] == column[None, :], 0.0, -1e30).astype(np.float32)
    return jnp.asarray(order, BF), positions, jnp.asarray(mask)


def grads_kernel(
    yr_ref, yc_ref, gr_ref, gc_ref, or_ref, oc_ref, cr_ref, cc_ref, pick_ref, pick_o_ref, *outs
):
    step = pl.program_id(0)
    keep, send = outs[:3], outs[3:]
    pick = pick_ref[...]
    pick_o = pick_o_ref[...]

    def lhs(ref, lo, hi, start):
        return dot(ref[:, lo:hi], pick[start : start + hi - lo]).astype(BF)

    for z in range(4):

        @pl.when(step == z)
        def _():
            for sub in range(4):
                group = z * 4 + sub
                xl, y_hi = sub // 2, sub % 2
                lo, hi = 240 * group, 240 * group + 240
                total = None
                for which in range(3):
                    for half in range(2):
                        base = which * D + half * HALF
                        a, b = max(lo, base), min(hi, base + HALF)
                        if a >= b:
                            continue
                        shift = which * HALF - base
                        g_ref, y_ref = ((gr_ref, yr_ref), (gc_ref, yc_ref))[half]
                        left = lhs(g_ref, a + shift, b + shift, a - lo)
                        term = dot_tn(left, y_ref[...])
                        total = term if total is None else total + term
                cols = slice(80 * group, 80 * group + 80)
                row_left = dot(cr_ref[:, cols], pick_o).astype(BF)
                col_left = dot(cc_ref[:, cols], pick_o).astype(BF)
                extra = jnp.concatenate(
                    [dot_tn(row_left, or_ref[...]), dot_tn(col_left, oc_ref[...])], axis=1
                )
                for j in range(8):
                    other, y_lo, xh = j // 4, (j // 2) % 2, j % 2
                    x = xh * 2 + xl
                    y = y_hi * 2 + y_lo
                    main = total[32 * j : 32 * j + 32]
                    more = extra[16 * j : 16 * j + 16]
                    block = jnp.concatenate([main[:24], main[24:] + more[:8], more[8:]], axis=0)
                    block = block.astype(BF)
                    refs = send if other else keep
                    refs[0][x, y, 0] = block[:, : PARTS[0]]
                    refs[1][y, 0, x] = block[:, PARTS[0] : PARTS[0] + PARTS[1]]
                    refs[2][0, x, y] = block[:, PARTS[0] + PARTS[1] :]


def weight_grads(y_row, y_col, g_row, g_col, o_row, o_col, c_row, c_col):
    core = lax.axis_index("sp") % 2
    lane = jnp.arange(256)[None, :]
    j = lane // 32
    source = ((j // 2) % 2) * 4 + (j % 2) * 2 + ((j // 4) ^ core)
    pick = ((jnp.arange(240)[:, None] == source * 30 + lane % 32) & (lane % 32 < 30)).astype(BF)
    lane = jnp.arange(128)[None, :]
    j = lane // 16
    source = ((j // 2) % 2) * 4 + (j % 2) * 2 + ((j // 4) ^ core)
    pick_o = (
        (jnp.arange(80)[:, None] == source * 10 + lane % 16 - 6) & (lane % 16 >= 6)
    ).astype(BF)
    ins = (y_row, y_col, g_row, g_col, o_row, o_col, c_row, c_col, pick, pick_o)
    shapes = [(4, 4, 4, CHUNK, part) for part in PARTS]
    specs = [
        pl.BlockSpec((4, 4, 1, CHUNK, PARTS[0]), lambda z: (0, 0, z, 0, 0)),
        pl.BlockSpec((4, 1, 4, CHUNK, PARTS[1]), lambda z: (0, z, 0, 0, 0)),
        pl.BlockSpec((1, 4, 4, CHUNK, PARTS[2]), lambda z: (z, 0, 0, 0, 0)),
    ]
    outs = pl.pallas_call(
        grads_kernel,
        grid=(4,),
        in_specs=[whole(v.shape) for v in ins],
        out_specs=specs * 2,
        out_shape=[jax.ShapeDtypeStruct(s, BF) for s in shapes] * 2,
        compiler_params=params(60),
    )(*ins)
    return outs[:3], outs[3:]


def reduce_scatter(keep, send):
    me = place(lax.axis_index(AXES))
    got = [hop(part, "c", 1) for part in send]

    def slot(value, index):
        return lax.dynamic_index_in_dim(value, index, 0, keepdims=False)

    pieces = []
    for mine, theirs, order in zip(keep, got, ORDERS):
        at = me[order[0]]
        pieces.append(
            [
                (
                    slot(mine, (at + off) % 4).astype(F32) + slot(theirs, (at + off) % 4).astype(F32)
                ).astype(BF)
                for off in range(4)
            ]
        )
    for level in range(3):
        sums = []
        for four, order in zip(pieces, ORDERS):
            axis = order[level]
            total = four[0].astype(F32)
            for off in (2, 1, 3):
                total = total + hop(four[off], axis, off).astype(F32)
            sums.append(total)
        if level == 2:
            return jnp.concatenate(sums, axis=-1)
        pieces = []
        for total, order in zip(sums, ORDERS):
            at = me[order[level + 1]]
            pieces.append([slot(total, (at + off) % 4).astype(BF) for off in range(4)])


def join_kernel(back_ref, part_ref, dpart_ref, wo_ref, out_ref, dy_ref):
    wo = wo_ref[...]
    for r in range(ROWS):
        toks = slice(r * WIDTH, (r + 1) * WIDTH)
        back = back_ref[:, r].reshape(WIDTH, 3 * HALF)
        out_ref[toks] = (part_ref[toks] + dot(back[:, :HALF], wo)).astype(BF)
        dy_ref[toks] = (dpart_ref[toks] + back[:, HALF:].astype(F32)).astype(BF)


def join(back, part, dpart, w_out):
    return pl.pallas_call(
        join_kernel,
        grid=(1,),
        in_specs=[
            whole((16, ROWS, 8, 3 * HALF)),
            whole((TOK, D)),
            whole((TOK, D)),
            pl.BlockSpec((HALF, D), lambda i: (1, 0)),
        ],
        out_specs=[whole((TOK, D))] * 2,
        out_shape=[jax.ShapeDtypeStruct((TOK, D), BF)] * 2,
        compiler_params=params(60),
    )(back, part, dpart, w_out)


def neighbours(cells):
    last = lax.axis_size("sp") - 1
    down = [(i, i + 1) for i in range(last)]
    up = [(i + 1, i) for i in range(last)]
    return (lax.ppermute(cells[ROWS - 1 :], "sp", down), lax.ppermute(cells[:1], "sp", up))


def spread(value):
    return lax.all_to_all(value, "sp", split_axis=0, concat_axis=0, tiled=True)


def shards(patches, conv_w, w_qkv, w_out, cotangent):
    x = patches[0]
    cot = cotangent[0]
    taps = conv_w.reshape(9, D)
    cot_flat = cot.reshape(TOK, D)
    cot_send = cot.reshape(ROWS, 16, 8, D).transpose(1, 0, 2, 3).reshape(16, ROWS * 8, D)
    cot_col = spread(cot_send).reshape(TOK, D)
    top, bot = neighbours(x)
    y, y_send = conv_forward(x, top, bot, taps)
    y_flat = y.reshape(TOK, D)
    y_col = spread(y_send.reshape(16, ROWS * 8, D)).reshape(TOK, D)

    both = turn_matrix()
    cos_w, sin_w = angle_tables(np.arange(WIDTH))
    o_row, g_row, part, dpart = attention_call(
        row_kernel, 0, y_flat, cot_flat, w_qkv, w_out, (cos_w, sin_w, both),
        [((TOK, HALF), BF), ((TOK, 3 * HALF), BF), ((TOK, D), F32), ((TOK, D), F32)],
    )
    order, positions, mask = col_order()
    cos_h, sin_h = angle_tables(positions)
    yp_col, cp_col, o_col, g_col, back = attention_call(
        col_kernel, 1, y_col, cot_col, w_qkv, w_out, (cos_h, sin_h, both, mask, order),
        [
            ((TOK, D), BF), ((TOK, D), BF), ((TOK, HALF), BF), ((TOK, 3 * HALF), BF),
            ((TOK, 3 * HALF), BF),
        ],
    )
    returned = spread(back.reshape(16, ROWS * 8, 3 * HALF)).reshape(16, ROWS, 8, 3 * HALF)
    keep, send = weight_grads(
        y_flat, yp_col, g_row, g_col, o_row, o_col, cot_flat, cp_col
    )
    layer_out, dy = join(returned, part, dpart, w_out)
    dy = dy.reshape(ROWS, WIDTH, D)
    dtop, dbot = neighbours(dy)
    grad_x, gconv = conv_backward(x, top, bot, dy, dtop, dbot, taps)
    factor = 1.0 / math.sqrt(8 * 64 * 128)
    gconv = lax.psum(gconv * factor, AXES)
    index = lax.axis_index(AXES)
    gconv = lax.dynamic_slice_in_dim(gconv, index * 10, 10, axis=1).reshape(3, 3, 10)
    total = reduce_scatter(keep, send) * factor
    total = total.T
    return (
        layer_out.reshape(1, ROWS, WIDTH, D),
        grad_x[None],
        total[:, :30],
        total[:, 30:],
        gconv,
    )


def solution(mesh):
    slab = P("grp", "sp", None, None)
    return jax.shard_map(
        shards,
        mesh=mesh,
        in_specs=(slab, P(), P(), P(), slab),
        out_specs=(slab, slab, P(None, AXES), P(None, AXES), P(None, None, AXES)),
        check_vma=False,
    )
```

```python
import functools
import math

import jax
import jax.numpy as jnp
import numpy as np
from jax import lax
from jax.experimental import pallas as pl
from jax.experimental.pallas import tpu as pltpu
from jax.sharding import PartitionSpec as P

HEADS = 16
HDIM = 80
D = 1280
HALF = 640
ROWS = 4
WIDTH = 128
TOK = ROWS * WIDTH
AXES = ("grp", "sp")
BF = jnp.bfloat16
F32 = jnp.float32
MIB = 1024 * 1024

CHUNK = 40
CHIPS = 64


def dot(a, b):
    return lax.dot_general(a, b, (((1,), (0,)), ((), ())), preferred_element_type=F32)


def dot_nt(a, b):
    return lax.dot_general(a, b, (((1,), (1,)), ((), ())), preferred_element_type=F32)


def dot_tn(a, b):
    return lax.dot_general(a, b, (((0,), (0,)), ((), ())), preferred_element_type=F32)


def params(limit):
    return pltpu.CompilerParams(vmem_limit_bytes=limit * MIB)


def cost(micros):
    return pl.CostEstimate(flops=int(micros * 1.1535e9), bytes_accessed=0, transcendentals=0)


def shifted(value, step):
    index = lax.broadcasted_iota(jnp.int32, value.shape, 0)
    moved = pltpu.roll(value, step % WIDTH, axis=0)
    edge = 0 if step == 1 else WIDTH - 1
    return jnp.where(index == edge, 0.0, moved)


def conv_kernel(x_ref, top_ref, bot_ref, k_ref, y_ref, send_ref):
    taps = k_ref[...].astype(F32)
    rows = [top_ref[0].astype(F32)]
    rows += [x_ref[r].astype(F32) for r in range(ROWS)]
    rows += [bot_ref[0].astype(F32)]
    for r in range(ROWS):
        sums = []
        for b in range(3):
            total = taps[b : b + 1] * rows[r]
            total += taps[3 + b : 4 + b] * rows[r + 1]
            total += taps[6 + b : 7 + b] * rows[r + 2]
            sums.append(total)
        out = rows[r + 1] + sums[1] + shifted(sums[0], 1) + shifted(sums[2], -1)
        y_ref[r] = out.astype(BF)
        send_ref[:, r] = out.reshape(16, 8, out.shape[-1]).astype(BF)


def conv_forward(x, top, bot, taps):
    block = 256
    grid = (D // block,)
    row = pl.BlockSpec((1, WIDTH, block), lambda i: (0, 0, i))
    return pl.pallas_call(
        conv_kernel,
        grid=grid,
        in_specs=[
            pl.BlockSpec((ROWS, WIDTH, block), lambda i: (0, 0, i)),
            row,
            row,
            pl.BlockSpec((9, block), lambda i: (0, i)),
        ],
        out_specs=[
            pl.BlockSpec((ROWS, WIDTH, block), lambda i: (0, 0, i)),
            pl.BlockSpec((16, ROWS, 8, block), lambda i: (0, 0, 0, i)),
        ],
        out_shape=[
            jax.ShapeDtypeStruct((ROWS, WIDTH, D), BF),
            jax.ShapeDtypeStruct((16, ROWS, 8, D), BF),
        ],
        compiler_params=params(32),
        cost_estimate=cost(4),
    )(x, top, bot, taps)


def conv_back_kernel(x_ref, top_ref, bot_ref, dy_ref, dtop_ref, dbot_ref, k_ref, gx_ref, gk_ref):
    taps = k_ref[...].astype(F32)
    rows = [top_ref[0].astype(F32)]
    rows += [x_ref[r].astype(F32) for r in range(ROWS)]
    rows += [bot_ref[0].astype(F32)]
    grads = [dtop_ref[0].astype(F32)]
    grads += [dy_ref[r].astype(F32) for r in range(ROWS)]
    grads += [dbot_ref[0].astype(F32)]
    gains = [None] * 9
    for r in range(ROWS):
        sums = []
        for b in range(3):
            total = taps[b : b + 1] * grads[r + 2]
            total += taps[3 + b : 4 + b] * grads[r + 1]
            total += taps[6 + b : 7 + b] * grads[r]
            sums.append(total)
        mid = grads[r + 1]
        gx_ref[r] = (mid + sums[1] + shifted(sums[0], -1) + shifted(sums[2], 1)).astype(BF)
        near = (shifted(mid, -1), mid, shifted(mid, 1))
        for a in range(3):
            for b in range(3):
                term = rows[r + a] * near[b]
                slot = a * 3 + b
                gains[slot] = term if gains[slot] is None else gains[slot] + term
    for slot in range(9):
        gk_ref[slot : slot + 1] = jnp.sum(gains[slot], axis=0, keepdims=True)


def conv_backward(x, top, bot, dy, dtop, dbot, taps):
    block = 128
    grid = (D // block,)
    row = pl.BlockSpec((1, WIDTH, block), lambda i: (0, 0, i))
    slab = pl.BlockSpec((ROWS, WIDTH, block), lambda i: (0, 0, i))
    small = pl.BlockSpec((9, block), lambda i: (0, i))
    return pl.pallas_call(
        conv_back_kernel,
        grid=grid,
        in_specs=[slab, row, row, slab, row, row, small],
        out_specs=[slab, small],
        out_shape=[
            jax.ShapeDtypeStruct((ROWS, WIDTH, D), BF),
            jax.ShapeDtypeStruct((9, D), F32),
        ],
        compiler_params=params(32),
        cost_estimate=cost(7),
    )(x, top, bot, dy, dtop, dbot, taps)


def turn(value, cos, sin, first, sign):
    moved = jnp.where(
        first, pltpu.roll(value, HALF - HDIM // 2, axis=1), pltpu.roll(value, HDIM // 2, axis=1)
    )
    return value * cos + moved * sin if sign > 0 else value * cos - moved * sin


def attention(block, q_s, k_s, v_s, d_s, dq_s, dk_s, cos_ref, sin_ref, mask, o_ref, g_ref):
    scale = 1.0 / math.sqrt(HDIM)
    toks = pl.ds(pl.multiple_of(block * 128, 128), 128)
    cos = cos_ref[...]
    sin = sin_ref[...]
    first = lax.broadcasted_iota(jnp.int32, (128, HALF), 1) % HDIM < HDIM // 2
    q_s[toks] = turn(q_s[toks].astype(F32), cos, sin, first, 1).astype(BF)
    k_s[toks] = turn(k_s[toks].astype(F32), cos, sin, first, 1).astype(BF)
    cols = [slice(h * HDIM, (h + 1) * HDIM) for h in range(HEADS // 2)]
    q = [q_s[toks, c] for c in cols]
    k = [k_s[toks, c] for c in cols]
    v = [v_s[toks, c] for c in cols]
    d_o = [d_s[toks, c] for c in cols]
    scores = [dot_nt(a, b) * scale for a, b in zip(q, k)]
    d_p = [dot_nt(a, b) for a, b in zip(d_o, v)]
    if mask is not None:
        scores = [s + mask for s in scores]
    expo = [jnp.exp(s - jnp.max(s, axis=-1, keepdims=True)) for s in scores]
    prob = [e * (1.0 / jnp.sum(e, axis=-1, keepdims=True)) for e in expo]
    prob_b = [p.astype(BF) for p in prob]
    d_s_b = [
        (p * (x - jnp.sum(p * x, axis=-1, keepdims=True)) * scale).astype(BF)
        for p, x in zip(prob, d_p)
    ]
    for h, c in enumerate(cols):
        o_ref[toks, c] = dot(prob_b[h], v[h]).astype(BF)
    for h, c in enumerate(cols):
        g_ref[toks, slice(2 * HALF + c.start, 2 * HALF + c.stop)] = dot_tn(
            prob_b[h], d_o[h]
        ).astype(BF)
    for h, c in enumerate(cols):
        dq_s[:, c] = dot(d_s_b[h], k[h])
    for h, c in enumerate(cols):
        dk_s[:, c] = dot_tn(d_s_b[h], q[h])
    g_ref[toks, slice(0, HALF)] = turn(dq_s[...], cos, sin, first, -1).astype(BF)
    g_ref[toks, slice(HALF, 2 * HALF)] = turn(dk_s[...], cos, sin, first, -1).astype(BF)


def row_kernel(
    y_ref, c_ref, wq_ref, wk_ref, wv_ref, wo_ref, cos_ref, sin_ref,
    o_ref, g_ref, out_ref, dy_ref, q_s, k_s, v_s, d_s, dq_s, dk_s,
):
    y = y_ref[...]
    cot = c_ref[...]
    q_s[...] = dot(y, wq_ref[...]).astype(BF)
    k_s[...] = dot(y, wk_ref[...]).astype(BF)
    v_s[...] = dot(y, wv_ref[...]).astype(BF)
    d_s[...] = dot_nt(cot, wo_ref[...]).astype(BF)

    @pl.loop(0, TOK // 128)
    def _(block):
        attention(block, q_s, k_s, v_s, d_s, dq_s, dk_s, cos_ref, sin_ref, None, o_ref, g_ref)

    out_ref[...] = y.astype(F32) + dot(o_ref[...], wo_ref[...])
    dy_ref[...] = (
        cot.astype(F32)
        + dot_nt(g_ref[:, :HALF], wq_ref[...])
        + dot_nt(g_ref[:, HALF : 2 * HALF], wk_ref[...])
        + dot_nt(g_ref[:, 2 * HALF :], wv_ref[...])
    )


def col_kernel(
    y_ref, c_ref, wq_ref, wk_ref, wv_ref, wo_ref, cos_ref, sin_ref, mask_ref, perm_ref,
    yp_ref, cp_ref, o_ref, g_ref, back_ref, q_s, k_s, v_s, d_s, dq_s, dk_s,
):
    yp_ref[...] = dot(perm_ref[...], y_ref[...]).astype(BF)
    cp_ref[...] = dot(perm_ref[...], c_ref[...]).astype(BF)
    y = yp_ref[...]
    q_s[...] = dot(y, wq_ref[...]).astype(BF)
    k_s[...] = dot(y, wk_ref[...]).astype(BF)
    v_s[...] = dot(y, wv_ref[...]).astype(BF)
    d_s[...] = dot_nt(cp_ref[...], wo_ref[...]).astype(BF)

    @pl.loop(0, TOK // 128)
    def _(block):
        attention(
            block, q_s, k_s, v_s, d_s, dq_s, dk_s, cos_ref, sin_ref, mask_ref[...], o_ref, g_ref
        )

    part = (
        dot_nt(g_ref[:, :HALF], wq_ref[...])
        + dot_nt(g_ref[:, HALF : 2 * HALF], wk_ref[...])
        + dot_nt(g_ref[:, 2 * HALF :], wv_ref[...])
    ).astype(BF)
    back_ref[:, :HALF] = dot_tn(perm_ref[...], o_ref[...]).astype(BF)
    back_ref[:, HALF:] = dot_tn(perm_ref[...], part).astype(BF)


def whole(shape):
    return pl.BlockSpec(shape, lambda i: (0,) * len(shape))


def attention_call(kernel, half, y, cot, w_qkv, w_out, tables, outs):
    def columns(which):
        return pl.BlockSpec((D, HALF), lambda i: (0, 2 * which + half))

    return pl.pallas_call(
        kernel,
        grid=(1,),
        in_specs=[
            whole((TOK, D)),
            whole((TOK, D)),
            columns(0),
            columns(1),
            columns(2),
            pl.BlockSpec((HALF, D), lambda i: (half, 0)),
        ]
        + [whole(t.shape) for t in tables],
        out_specs=[whole(s) for s, _ in outs],
        out_shape=[jax.ShapeDtypeStruct(s, t) for s, t in outs],
        scratch_shapes=[pltpu.VMEM((TOK, HALF), BF)] * 4 + [pltpu.VMEM((128, HALF), F32)] * 2,
        compiler_params=params(60),
        cost_estimate=cost(30),
    )(y, cot, w_qkv, w_qkv, w_qkv, w_out, *tables)


def angle_tables(positions):
    half = HDIM // 2
    base = 10000.0 * 4.0 ** (HDIM / (HDIM - 2.0))
    steps = np.arange(half, dtype=np.float32)
    freq = np.exp(-(2.0 * steps / HDIM) * np.float32(math.log(base))).astype(np.float32)
    angle = positions.astype(np.float32)[:, None] * freq[None, :]
    cos = np.cos(angle).astype(np.float32)
    sin = np.sin(angle).astype(np.float32)
    cos = np.tile(np.concatenate([cos, cos], 1), (1, HEADS // 2))
    sin = np.tile(np.concatenate([-sin, sin], 1), (1, HEADS // 2))
    return jnp.asarray(cos), jnp.asarray(sin)


def col_order():
    order = np.zeros((TOK, TOK), np.float32)
    for pair in range(4):
        for src in range(16):
            for c in range(2):
                for r in range(ROWS):
                    order[pair * 128 + src * 8 + c * 4 + r, src * 32 + r * 8 + pair * 2 + c] = 1.0
    token = np.arange(128)
    positions = (token // 8) * 4 + token % 4
    column = (token // 4) % 2
    mask = np.where(column[:, None] == column[None, :], 0.0, -1e30).astype(np.float32)
    return jnp.asarray(order, BF), positions, jnp.asarray(mask)


def grads_kernel(
    yr_ref, yc_ref, gr_ref, gc_ref, or_ref, oc_ref, cr_ref, cc_ref, pick_ref, pick_o_ref, *outs
):
    step = pl.program_id(0)

    for z in range(4):

        @pl.when(step == z)
        def _():
            lefts = ([], [])
            rows = ([], [])
            for sub in range(4):
                lo, hi = 240 * (z * 4 + sub), 240 * (z * 4 + sub) + 240
                for which in range(3):
                    for half in range(2):
                        base = which * D + half * HALF
                        a, b = max(lo, base), min(hi, base + HALF)
                        if a >= b:
                            continue
                        shift = which * HALF - base
                        g_ref = (gr_ref, gc_ref)[half]
                        lefts[half].append(
                            dot_nt(pick_ref[:, a - lo : b - lo], g_ref[:, a + shift : b + shift]).astype(BF)
                        )
                        rows[half].append(sub)
            totals = [None] * 4
            for half in range(2):
                y_ref = (yr_ref, yc_ref)[half]
                product = dot(jnp.concatenate(lefts[half], axis=0), y_ref[...])
                for i, sub in enumerate(rows[half]):
                    term = product[256 * i : 256 * i + 256]
                    totals[sub] = term if totals[sub] is None else totals[sub] + term
            extra = []
            for c_ref, o_ref in ((cr_ref, or_ref), (cc_ref, oc_ref)):
                left = [
                    dot_nt(pick_o_ref[...], c_ref[:, 320 * z + 80 * s : 320 * z + 80 * s + 80]).astype(BF)
                    for s in range(4)
                ]
                extra.append(dot(jnp.concatenate(left, axis=0), o_ref[...]))
            extra = jnp.concatenate(extra, axis=1)
            for sub in range(4):
                for j in range(8):
                    ref = outs[j // 4]
                    main = totals[sub][32 * j : 32 * j + 32]
                    more = extra[128 * sub + 16 * j : 128 * sub + 16 * j + 16]
                    block = jnp.concatenate([main[:24], main[24:] + more[:8], more[8:]], axis=0)
                    ref[4 * sub + j % 4] = block.astype(BF)


def weight_grads(y_row, y_col, g_row, g_col, o_row, o_col, c_row, c_col):
    core = lax.axis_index("sp") % 2
    lane = jnp.arange(256)[:, None]
    j = lane // 32
    source = (j % 4) * 2 + ((j // 4) ^ core)
    pick = ((jnp.arange(240)[None, :] == source * 30 + lane % 32) & (lane % 32 < 30)).astype(BF)
    lane = jnp.arange(128)[:, None]
    j = lane // 16
    source = (j % 4) * 2 + ((j // 4) ^ core)
    pick_o = (
        (jnp.arange(80)[None, :] == source * 10 + lane % 16 - 6) & (lane % 16 >= 6)
    ).astype(BF)
    ins = (y_row, y_col, g_row, g_col, o_row, o_col, c_row, c_col, pick, pick_o)
    return pl.pallas_call(
        grads_kernel,
        grid=(4,),
        in_specs=[whole(v.shape) for v in ins],
        out_specs=[pl.BlockSpec((CHIPS // 4, CHUNK, D), lambda z: (z, 0, 0))] * 2,
        out_shape=[jax.ShapeDtypeStruct((CHIPS, CHUNK, D), BF)] * 2,
        compiler_params=params(60),
        cost_estimate=cost(16),
    )(*ins)


def chip_sum(keep, send):
    swap = [(i, i ^ 1) for i in range(16)]
    return (keep.astype(F32) + lax.ppermute(send, "sp", swap).astype(F32)).astype(BF)


def reduce_scatter(chip):
    same_core = [[2 * i + core for i in range(CHIPS)] for core in range(2)]
    got = lax.all_to_all(
        chip, AXES, split_axis=0, concat_axis=0, axis_index_groups=same_core, tiled=True
    )
    return jnp.sum(got.astype(F32), axis=0)


def all_sum(value):
    for axis, bits in (("sp", 4), ("grp", 3)):
        for bit in range(bits):
            swap = [(i, i ^ (1 << bit)) for i in range(1 << bits)]
            value = value + lax.ppermute(value, axis, swap)
    return value


def join_kernel(back_ref, part_ref, dpart_ref, wo_ref, out_ref, dy_ref):
    wo = wo_ref[...]
    for r in range(ROWS):
        toks = slice(r * WIDTH, (r + 1) * WIDTH)
        back = back_ref[:, r].reshape(WIDTH, 3 * HALF)
        out_ref[toks] = (part_ref[toks] + dot(back[:, :HALF], wo)).astype(BF)
        dy_ref[toks] = (dpart_ref[toks] + back[:, HALF:].astype(F32)).astype(BF)


def join(back, part, dpart, w_out):
    return pl.pallas_call(
        join_kernel,
        grid=(1,),
        in_specs=[
            whole((16, ROWS, 8, 3 * HALF)),
            whole((TOK, D)),
            whole((TOK, D)),
            pl.BlockSpec((HALF, D), lambda i: (1, 0)),
        ],
        out_specs=[whole((TOK, D))] * 2,
        out_shape=[jax.ShapeDtypeStruct((TOK, D), BF)] * 2,
        compiler_params=params(60),
        cost_estimate=cost(6),
    )(back, part, dpart, w_out)


def neighbours(cells):
    last = lax.axis_size("sp") - 1
    down = [(i, i + 1) for i in range(last)]
    up = [(i + 1, i) for i in range(last)]
    return (lax.ppermute(cells[ROWS - 1 :], "sp", down), lax.ppermute(cells[:1], "sp", up))


def spread(value):
    return lax.all_to_all(value, "sp", split_axis=0, concat_axis=0, tiled=True)


def shards(patches, conv_w, w_qkv, w_out, cotangent):
    x = patches[0]
    cot = cotangent[0]
    taps = conv_w.reshape(9, D)
    cot_flat = cot.reshape(TOK, D)
    cot_send = cot.reshape(ROWS, 16, 8, D).transpose(1, 0, 2, 3).reshape(16, ROWS * 8, D)
    cot_col = spread(cot_send).reshape(TOK, D)
    top, bot = neighbours(x)
    y, y_send = conv_forward(x, top, bot, taps)
    y_flat = y.reshape(TOK, D)
    y_send, cot_col = lax.optimization_barrier((y_send, cot_col))
    y_col = spread(y_send.reshape(16, ROWS * 8, D)).reshape(TOK, D)

    cos_w, sin_w = angle_tables(np.arange(WIDTH))
    o_row, g_row, part, dpart = attention_call(
        row_kernel, 0, y_flat, cot_flat, w_qkv, w_out, (cos_w, sin_w),
        [((TOK, HALF), BF), ((TOK, 3 * HALF), BF), ((TOK, D), F32), ((TOK, D), F32)],
    )
    y_col, g_row = lax.optimization_barrier((y_col, g_row))
    order, positions, mask = col_order()
    cos_h, sin_h = angle_tables(positions)
    yp_col, cp_col, o_col, g_col, back = attention_call(
        col_kernel, 1, y_col, cot_col, w_qkv, w_out, (cos_h, sin_h, mask, order),
        [
            ((TOK, D), BF), ((TOK, D), BF), ((TOK, HALF), BF), ((TOK, 3 * HALF), BF),
            ((TOK, 3 * HALF), BF),
        ],
    )
    returned = spread(back.reshape(16, ROWS * 8, 3 * HALF)).reshape(16, ROWS, 8, 3 * HALF)
    keep, send = weight_grads(
        y_flat, yp_col, g_row, g_col, o_row, o_col, cot_flat, cp_col
    )
    returned, keep, send = lax.optimization_barrier((returned, keep, send))
    chip = chip_sum(keep, send)
    layer_out, dy = join(returned, part, dpart, w_out)
    dy = dy.reshape(ROWS, WIDTH, D)
    dtop, dbot = neighbours(dy)
    grad_x, gconv = conv_backward(x, top, bot, dy, dtop, dbot, taps)
    factor = 1.0 / math.sqrt(8 * 64 * 128)
    gconv = all_sum(gconv * factor)
    index = lax.axis_index(AXES)
    gconv = lax.dynamic_slice_in_dim(gconv, index * 10, 10, axis=1).reshape(3, 3, 10)
    total = reduce_scatter(chip) * factor
    total = total.T
    return (
        layer_out.reshape(1, ROWS, WIDTH, D),
        grad_x[None],
        total[:, :30],
        total[:, 30:],
        gconv,
    )


def solution(mesh):
    slab = P("grp", "sp", None, None)
    return jax.shard_map(
        shards,
        mesh=mesh,
        in_specs=(slab, P(), P(), P(), slab),
        out_specs=(slab, slab, P(None, AXES), P(None, AXES), P(None, None, AXES)),
        check_vma=False,
    )
```

```python
import functools
import math

import jax
import jax.numpy as jnp
import numpy as np
from jax import lax
from jax.experimental import pallas as pl
from jax.experimental.pallas import tpu as pltpu
from jax.sharding import PartitionSpec as P

HEADS = 16
HDIM = 80
D = 1280
HALF = 640
ROWS = 4
WIDTH = 128
TOK = ROWS * WIDTH
AXES = ("grp", "sp")
BF = jnp.bfloat16
F32 = jnp.float32
MIB = 1024 * 1024

CHUNK = 40
CHIPS = 64


def dot(a, b):
    return lax.dot_general(a, b, (((1,), (0,)), ((), ())), preferred_element_type=F32)


def dot_nt(a, b):
    return lax.dot_general(a, b, (((1,), (1,)), ((), ())), preferred_element_type=F32)


def dot_tn(a, b):
    return lax.dot_general(a, b, (((0,), (0,)), ((), ())), preferred_element_type=F32)


def params(limit):
    return pltpu.CompilerParams(vmem_limit_bytes=limit * MIB)


def cost(micros):
    return pl.CostEstimate(flops=int(micros * 1.1535e9), bytes_accessed=0, transcendentals=0)


def shifted(value, step):
    index = lax.broadcasted_iota(jnp.int32, value.shape, 0)
    moved = pltpu.roll(value, step % WIDTH, axis=0)
    edge = 0 if step == 1 else WIDTH - 1
    return jnp.where(index == edge, 0.0, moved)


def conv_kernel(x_ref, top_ref, bot_ref, c_ref, k_ref, y_ref, send_ref):
    taps = k_ref[...].astype(F32)
    rows = [top_ref[0].astype(F32)]
    rows += [x_ref[r].astype(F32) for r in range(ROWS)]
    rows += [bot_ref[0].astype(F32)]
    for r in range(ROWS):
        sums = []
        for b in range(3):
            total = taps[b : b + 1] * rows[r]
            total += taps[3 + b : 4 + b] * rows[r + 1]
            total += taps[6 + b : 7 + b] * rows[r + 2]
            sums.append(total)
        out = rows[r + 1] + sums[1] + shifted(sums[0], 1) + shifted(sums[2], -1)
        y_ref[r] = out.astype(BF)
        send_ref[:, 0, r] = out.reshape(16, 8, out.shape[-1]).astype(BF)
        send_ref[:, 1, r] = c_ref[r].reshape(16, 8, out.shape[-1])


def conv_forward(x, top, bot, cot, taps):
    block = 256
    grid = (D // block,)
    row = pl.BlockSpec((1, WIDTH, block), lambda i: (0, 0, i))
    return pl.pallas_call(
        conv_kernel,
        grid=grid,
        in_specs=[
            pl.BlockSpec((ROWS, WIDTH, block), lambda i: (0, 0, i)),
            row,
            row,
            pl.BlockSpec((ROWS, WIDTH, block), lambda i: (0, 0, i)),
            pl.BlockSpec((9, block), lambda i: (0, i)),
        ],
        out_specs=[
            pl.BlockSpec((ROWS, WIDTH, block), lambda i: (0, 0, i)),
            pl.BlockSpec((16, 2, ROWS, 8, block), lambda i: (0, 0, 0, 0, i)),
        ],
        out_shape=[
            jax.ShapeDtypeStruct((ROWS, WIDTH, D), BF),
            jax.ShapeDtypeStruct((16, 2, ROWS, 8, D), BF),
        ],
        compiler_params=params(32),
        cost_estimate=cost(5),
    )(x, top, bot, cot, taps)


def conv_back_kernel(x_ref, top_ref, bot_ref, dy_ref, dtop_ref, dbot_ref, k_ref, gx_ref, gk_ref):
    taps = k_ref[...].astype(F32)
    rows = [top_ref[0].astype(F32)]
    rows += [x_ref[r].astype(F32) for r in range(ROWS)]
    rows += [bot_ref[0].astype(F32)]
    grads = [dtop_ref[0].astype(F32)]
    grads += [dy_ref[r].astype(F32) for r in range(ROWS)]
    grads += [dbot_ref[0].astype(F32)]
    gains = [None] * 9
    for r in range(ROWS):
        sums = []
        for b in range(3):
            total = taps[b : b + 1] * grads[r + 2]
            total += taps[3 + b : 4 + b] * grads[r + 1]
            total += taps[6 + b : 7 + b] * grads[r]
            sums.append(total)
        mid = grads[r + 1]
        gx_ref[r] = (mid + sums[1] + shifted(sums[0], -1) + shifted(sums[2], 1)).astype(BF)
        near = (shifted(mid, -1), mid, shifted(mid, 1))
        for a in range(3):
            for b in range(3):
                term = rows[r + a] * near[b]
                slot = a * 3 + b
                gains[slot] = term if gains[slot] is None else gains[slot] + term
    for slot in range(9):
        gk_ref[slot : slot + 1] = jnp.sum(gains[slot], axis=0, keepdims=True)


def conv_backward(x, top, bot, dy, dtop, dbot, taps):
    block = 128
    grid = (D // block,)
    row = pl.BlockSpec((1, WIDTH, block), lambda i: (0, 0, i))
    slab = pl.BlockSpec((ROWS, WIDTH, block), lambda i: (0, 0, i))
    small = pl.BlockSpec((9, block), lambda i: (0, i))
    return pl.pallas_call(
        conv_back_kernel,
        grid=grid,
        in_specs=[slab, row, row, slab, row, row, small],
        out_specs=[slab, small],
        out_shape=[
            jax.ShapeDtypeStruct((ROWS, WIDTH, D), BF),
            jax.ShapeDtypeStruct((9, D), F32),
        ],
        compiler_params=params(32),
        cost_estimate=cost(7),
    )(x, top, bot, dy, dtop, dbot, taps)


def turn(value, cos, sin, first, sign):
    moved = jnp.where(
        first, pltpu.roll(value, HALF - HDIM // 2, axis=1), pltpu.roll(value, HDIM // 2, axis=1)
    )
    return value * cos + moved * sin if sign > 0 else value * cos - moved * sin


def attention(block, q_s, k_s, v_s, d_s, dq_s, dk_s, cos_ref, sin_ref, mask, g_ref):
    scale = 1.0 / math.sqrt(HDIM)
    toks = pl.ds(pl.multiple_of(block * 128, 128), 128)
    cos = cos_ref[...]
    sin = sin_ref[...]
    first = lax.broadcasted_iota(jnp.int32, (128, HALF), 1) % HDIM < HDIM // 2
    q_s[toks] = turn(q_s[toks].astype(F32), cos, sin, first, 1).astype(BF)
    k_s[toks] = turn(k_s[toks].astype(F32), cos, sin, first, 1).astype(BF)
    cols = [slice(h * HDIM, (h + 1) * HDIM) for h in range(HEADS // 2)]
    q = [q_s[toks, c] for c in cols]
    k = [k_s[toks, c] for c in cols]
    v = [v_s[toks, c] for c in cols]
    d_o = [d_s[toks, c] for c in cols]
    scores = [dot_nt(a, b) * scale for a, b in zip(q, k)]
    d_p = [dot_nt(a, b) for a, b in zip(d_o, v)]
    if mask is not None:
        scores = [s + mask for s in scores]
    expo = [jnp.exp(s - jnp.max(s, axis=-1, keepdims=True)) for s in scores]
    prob = [e * (1.0 / jnp.sum(e, axis=-1, keepdims=True)) for e in expo]
    prob_b = [p.astype(BF) for p in prob]
    d_s_b = [
        (p * (x - jnp.sum(p * x, axis=-1, keepdims=True)) * scale).astype(BF)
        for p, x in zip(prob, d_p)
    ]
    for h, c in enumerate(cols):
        g_ref[toks, slice(3 * HALF + c.start, 3 * HALF + c.stop)] = dot(prob_b[h], v[h]).astype(BF)
    for h, c in enumerate(cols):
        g_ref[toks, slice(2 * HALF + c.start, 2 * HALF + c.stop)] = dot_tn(
            prob_b[h], d_o[h]
        ).astype(BF)
    for h, c in enumerate(cols):
        dq_s[:, c] = dot(d_s_b[h], k[h])
    for h, c in enumerate(cols):
        dk_s[:, c] = dot_tn(d_s_b[h], q[h])
    g_ref[toks, slice(0, HALF)] = turn(dq_s[...], cos, sin, first, -1).astype(BF)
    g_ref[toks, slice(HALF, 2 * HALF)] = turn(dk_s[...], cos, sin, first, -1).astype(BF)


def row_kernel(
    y_ref, c_ref, wq_ref, wk_ref, wv_ref, wo_ref, cos_ref, sin_ref,
    g_ref, out_ref, dy_ref, q_s, k_s, v_s, d_s, dq_s, dk_s,
):
    y = y_ref[...]
    cot = c_ref[...]
    q_s[...] = dot(y, wq_ref[...]).astype(BF)
    k_s[...] = dot(y, wk_ref[...]).astype(BF)
    v_s[...] = dot(y, wv_ref[...]).astype(BF)
    d_s[...] = dot_nt(cot, wo_ref[...]).astype(BF)

    @pl.loop(0, TOK // 128)
    def _(block):
        attention(block, q_s, k_s, v_s, d_s, dq_s, dk_s, cos_ref, sin_ref, None, g_ref)

    out_ref[...] = y.astype(F32) + dot(g_ref[:, 3 * HALF :], wo_ref[...])
    dy_ref[...] = (
        cot.astype(F32)
        + dot_nt(g_ref[:, :HALF], wq_ref[...])
        + dot_nt(g_ref[:, HALF : 2 * HALF], wk_ref[...])
        + dot_nt(g_ref[:, 2 * HALF : 3 * HALF], wv_ref[...])
    )


def col_kernel(
    pair_ref, wq_ref, wk_ref, wv_ref, wo_ref, cos_ref, sin_ref, mask_ref, perm_ref,
    yp_ref, cp_ref, g_ref, back_ref, q_s, k_s, v_s, d_s, dq_s, dk_s,
):
    yp_ref[...] = dot(perm_ref[...], pair_ref[:, 0].reshape(TOK, D)).astype(BF)
    cp_ref[...] = dot(perm_ref[...], pair_ref[:, 1].reshape(TOK, D)).astype(BF)
    y = yp_ref[...]
    q_s[...] = dot(y, wq_ref[...]).astype(BF)
    k_s[...] = dot(y, wk_ref[...]).astype(BF)
    v_s[...] = dot(y, wv_ref[...]).astype(BF)
    d_s[...] = dot_nt(cp_ref[...], wo_ref[...]).astype(BF)

    @pl.loop(0, TOK // 128)
    def _(block):
        attention(
            block, q_s, k_s, v_s, d_s, dq_s, dk_s, cos_ref, sin_ref, mask_ref[...], g_ref
        )

    part = (
        dot_nt(g_ref[:, :HALF], wq_ref[...])
        + dot_nt(g_ref[:, HALF : 2 * HALF], wk_ref[...])
        + dot_nt(g_ref[:, 2 * HALF : 3 * HALF], wv_ref[...])
    ).astype(BF)
    back_ref[:, :HALF] = dot_tn(perm_ref[...], g_ref[:, 3 * HALF :]).astype(BF)
    back_ref[:, HALF:] = dot_tn(perm_ref[...], part).astype(BF)


def whole(shape):
    return pl.BlockSpec(shape, lambda i: (0,) * len(shape))


def attention_call(kernel, half, tokens, w_qkv, w_out, tables, outs):
    def columns(which):
        return pl.BlockSpec((D, HALF), lambda i: (0, 2 * which + half))

    return pl.pallas_call(
        kernel,
        grid=(1,),
        in_specs=[whole(t.shape) for t in tokens]
        + [
            columns(0),
            columns(1),
            columns(2),
            pl.BlockSpec((HALF, D), lambda i: (half, 0)),
        ]
        + [whole(t.shape) for t in tables],
        out_specs=[whole(s) for s, _ in outs],
        out_shape=[jax.ShapeDtypeStruct(s, t) for s, t in outs],
        scratch_shapes=[pltpu.VMEM((TOK, HALF), BF)] * 4 + [pltpu.VMEM((128, HALF), F32)] * 2,
        compiler_params=params(60),
        cost_estimate=cost(30),
    )(*tokens, w_qkv, w_qkv, w_qkv, w_out, *tables)


def angle_tables(positions):
    half = HDIM // 2
    base = 10000.0 * 4.0 ** (HDIM / (HDIM - 2.0))
    steps = np.arange(half, dtype=np.float32)
    freq = np.exp(-(2.0 * steps / HDIM) * np.float32(math.log(base))).astype(np.float32)
    angle = positions.astype(np.float32)[:, None] * freq[None, :]
    cos = np.cos(angle).astype(np.float32)
    sin = np.sin(angle).astype(np.float32)
    cos = np.tile(np.concatenate([cos, cos], 1), (1, HEADS // 2))
    sin = np.tile(np.concatenate([-sin, sin], 1), (1, HEADS // 2))
    return jnp.asarray(cos), jnp.asarray(sin)


def col_order():
    order = np.zeros((TOK, TOK), np.float32)
    for pair in range(4):
        for src in range(16):
            for c in range(2):
                for r in range(ROWS):
                    order[pair * 128 + src * 8 + c * 4 + r, src * 32 + r * 8 + pair * 2 + c] = 1.0
    token = np.arange(128)
    positions = (token // 8) * 4 + token % 4
    column = (token // 4) % 2
    mask = np.where(column[:, None] == column[None, :], 0.0, -1e30).astype(np.float32)
    return jnp.asarray(order, BF), positions, jnp.asarray(mask)


def grads_kernel(*refs):
    pick_ref, pick_o_ref, out_ref = refs[-3:]
    sides = (refs[:6], refs[6:12])
    step = pl.program_id(0)

    def both(first, second, pick, cols):
        return jnp.concatenate(
            [dot_nt(pick, ref[:, cols]).astype(BF) for ref in (first, second)], axis=1
        )

    def product(left, first, second):
        return dot(left[:, :TOK], first[...]) + dot(left[:, TOK:], second[...])

    for z in range(4):

        @pl.when(step == z)
        def _():
            lefts = ([], [])
            rows = ([], [])
            for sub in range(4):
                lo, hi = 240 * (z * 4 + sub), 240 * (z * 4 + sub) + 240
                for which in range(3):
                    for half in range(2):
                        base = which * D + half * HALF
                        a, b = max(lo, base), min(hi, base + HALF)
                        if a >= b:
                            continue
                        shift = which * HALF - base
                        lefts[half].append(
                            both(
                                sides[half][2],
                                sides[half][3],
                                pick_ref[:, a - lo : b - lo],
                                slice(a + shift, b + shift),
                            )
                        )
                        rows[half].append(sub)
            totals = [None] * 4
            extra = []
            for half in range(2):
                y0, y1, g0, g1, c0, c1 = sides[half]
                result = product(jnp.concatenate(lefts[half], axis=0), y0, y1)
                for i, sub in enumerate(rows[half]):
                    term = result[128 * i : 128 * i + 128]
                    totals[sub] = term if totals[sub] is None else totals[sub] + term
                left = [
                    both(c0, c1, pick_o_ref[...], slice(320 * z + 80 * s, 320 * z + 80 * s + 80))
                    for s in range(4)
                ]
                left = jnp.concatenate(left, axis=0)
                extra.append(
                    product(left, g0.at[:, 3 * HALF : 4 * HALF], g1.at[:, 3 * HALF : 4 * HALF])
                )
            extra = jnp.concatenate(extra, axis=1)
            for sub in range(4):
                for j in range(4):
                    main = totals[sub][32 * j : 32 * j + 32]
                    more = extra[64 * sub + 16 * j : 64 * sub + 16 * j + 16]
                    block = jnp.concatenate([main[:24], main[24:] + more[:8], more[8:]], axis=0)
                    block = block.astype(BF)
                    for t in range(10):
                        out_ref[4 * sub + j, CHUNK * t : CHUNK * t + CHUNK] = block[
                            :, 128 * t : 128 * t + 128
                        ]


def weight_grads(row, col):
    core = lax.axis_index("sp") % 2
    lane = jnp.arange(128)[:, None]
    source = (lane // 32) * 2 + core
    pick = ((jnp.arange(240)[None, :] == source * 30 + lane % 32) & (lane % 32 < 30)).astype(BF)
    lane = jnp.arange(64)[:, None]
    source = (lane // 16) * 2 + core
    pick_o = (
        (jnp.arange(80)[None, :] == source * 10 + lane % 16 - 6) & (lane % 16 >= 6)
    ).astype(BF)
    ins = (*row, *col, pick, pick_o)
    return pl.pallas_call(
        grads_kernel,
        grid=(4,),
        in_specs=[
            pl.BlockSpec(v.shape, lambda z: (0, 0), pipeline_mode=pl.Buffered(1)) for v in ins
        ],
        out_specs=pl.BlockSpec((CHIPS // 4, CHUNK * 10, 128), lambda z: (z, 0, 0)),
        out_shape=jax.ShapeDtypeStruct((CHIPS, CHUNK * 10, 128), BF),
        compiler_params=params(60),
        cost_estimate=cost(16),
    )(*ins)


def other_core(value):
    return lax.ppermute(value, "sp", [(i, i ^ 1) for i in range(16)])


def reduce_scatter(chip, gconv):
    core = lax.axis_index("sp") % 2
    small = gconv.reshape(9, CHIPS, 2, 10).transpose(2, 1, 0, 3).reshape(2, CHIPS, 90)
    mine = lax.dynamic_index_in_dim(small, core, 0, keepdims=False)
    small = mine + other_core(lax.dynamic_index_in_dim(small, 1 - core, 0, keepdims=False))
    high = small.astype(BF)
    low = (small - high.astype(F32)).astype(BF)
    small = jnp.pad(jnp.stack([high, low], axis=1), ((0, 0), (0, 6), (0, 38)))
    same_core = [[2 * i + core for i in range(CHIPS)] for core in range(2)]

    def exchange(value):
        return lax.all_to_all(
            value, AXES, split_axis=0, concat_axis=0, axis_index_groups=same_core, tiled=True
        )

    got = exchange(jnp.concatenate([chip, small], axis=1))
    total = jnp.sum(got.astype(F32), axis=0)
    return total[: CHUNK * 10], (total[CHUNK * 10] + total[CHUNK * 10 + 1])[:90]


def join_kernel(back_ref, part_ref, dpart_ref, wo_ref, out_ref, dy_ref):
    wo = wo_ref[...]
    for r in range(ROWS):
        toks = slice(r * WIDTH, (r + 1) * WIDTH)
        back = back_ref[:, r].reshape(WIDTH, 3 * HALF)
        out_ref[toks] = (part_ref[toks] + dot(back[:, :HALF], wo)).astype(BF)
        dy_ref[toks] = (dpart_ref[toks] + back[:, HALF:].astype(F32)).astype(BF)


def join(back, part, dpart, w_out):
    return pl.pallas_call(
        join_kernel,
        grid=(1,),
        in_specs=[
            whole((16, ROWS, 8, 3 * HALF)),
            whole((TOK, D)),
            whole((TOK, D)),
            pl.BlockSpec((HALF, D), lambda i: (1, 0)),
        ],
        out_specs=[whole((TOK, D))] * 2,
        out_shape=[jax.ShapeDtypeStruct((TOK, D), BF)] * 2,
        compiler_params=params(60),
        cost_estimate=cost(6),
    )(back, part, dpart, w_out)


def neighbours(cells):
    last = lax.axis_size("sp") - 1
    down = [(i, i + 1) for i in range(last)]
    up = [(i + 1, i) for i in range(last)]
    return (lax.ppermute(cells[ROWS - 1 :], "sp", down), lax.ppermute(cells[:1], "sp", up))


def spread(value):
    return lax.all_to_all(value, "sp", split_axis=0, concat_axis=0, tiled=True)


def shards(patches, conv_w, w_qkv, w_out, cotangent):
    x = patches[0]
    cot = cotangent[0]
    taps = conv_w.reshape(9, D)
    cot_flat = cot.reshape(TOK, D)
    top, bot = neighbours(x)
    y, pair = conv_forward(x, top, bot, cot, taps)
    y_flat = y.reshape(TOK, D)
    pair = spread(pair.reshape(16, 2 * ROWS * 8, D)).reshape(16, 2, ROWS * 8, D)

    cos_w, sin_w = angle_tables(np.arange(WIDTH))
    g_row, part, dpart = attention_call(
        row_kernel, 0, (y_flat, cot_flat), w_qkv, w_out, (cos_w, sin_w),
        [((TOK, 4 * HALF), BF), ((TOK, D), F32), ((TOK, D), F32)],
    )
    pair, g_row = lax.optimization_barrier((pair, g_row))
    row = []
    for value in (y_flat, g_row, cot_flat):
        row += [value, other_core(value)]
    order, positions, mask = col_order()
    cos_h, sin_h = angle_tables(positions)
    y_col, c_col, g_col, back = attention_call(
        col_kernel, 1, (pair,), w_qkv, w_out, (cos_h, sin_h, mask, order),
        [((TOK, D), BF), ((TOK, D), BF), ((TOK, 4 * HALF), BF), ((TOK, 3 * HALF), BF)],
    )
    returned = spread(back.reshape(16, ROWS * 8, 3 * HALF)).reshape(16, ROWS, 8, 3 * HALF)
    col = []
    for value in (y_col, g_col, c_col):
        col += [value, other_core(value)]
    chip = weight_grads(row, col)
    returned, chip = lax.optimization_barrier((returned, chip))
    layer_out, dy = join(returned, part, dpart, w_out)
    dy = dy.reshape(ROWS, WIDTH, D)
    dtop, dbot = neighbours(dy)
    grad_x, gconv = conv_backward(x, top, bot, dy, dtop, dbot, taps)
    factor = 1.0 / math.sqrt(8 * 64 * 128)
    total, gconv = reduce_scatter(chip, gconv)
    total = total.reshape(10, CHUNK, 128).transpose(0, 2, 1).reshape(D, CHUNK) * factor
    return (
        layer_out.reshape(1, ROWS, WIDTH, D),
        grad_x[None],
        total[:, :30],
        total[:, 30:],
        (gconv * factor).reshape(3, 3, 10),
    )


def solution(mesh):
    slab = P("grp", "sp", None, None)
    return jax.shard_map(
        shards,
        mesh=mesh,
        in_specs=(slab, P(), P(), P(), slab),
        out_specs=(slab, slab, P(None, AXES), P(None, AXES), P(None, None, AXES)),
        check_vma=False,
    )
```

```python
import functools
import math

import jax
import jax.numpy as jnp
import numpy as np
from jax import lax
from jax.experimental import pallas as pl
from jax.experimental.pallas import tpu as pltpu
from jax.sharding import PartitionSpec as P

HEADS = 16
HDIM = 80
D = 1280
HALF = 640
ROWS = 4
WIDTH = 128
TOK = ROWS * WIDTH
AXES = ("grp", "sp")
BF = jnp.bfloat16
F32 = jnp.float32
MIB = 1024 * 1024

CHUNK = 40
CHIPS = 64
SPARE = 8


def dot(a, b):
    return lax.dot_general(a, b, (((1,), (0,)), ((), ())), preferred_element_type=F32)


def dot_nt(a, b):
    return lax.dot_general(a, b, (((1,), (1,)), ((), ())), preferred_element_type=F32)


def dot_tn(a, b):
    return lax.dot_general(a, b, (((0,), (0,)), ((), ())), preferred_element_type=F32)


def params(limit):
    return pltpu.CompilerParams(vmem_limit_bytes=limit * MIB)


def cost(micros):
    return pl.CostEstimate(flops=int(micros * 1.1535e9), bytes_accessed=0, transcendentals=0)


def shifted(value, step):
    index = lax.broadcasted_iota(jnp.int32, value.shape, 0)
    moved = pltpu.roll(value, step % WIDTH, axis=0)
    edge = 0 if step == 1 else WIDTH - 1
    return jnp.where(index == edge, 0.0, moved)


def conv_kernel(x_ref, top_ref, bot_ref, c_ref, k_ref, y_ref, send_ref):
    taps = k_ref[...].astype(F32)
    rows = [top_ref[0].astype(F32)]
    rows += [x_ref[r].astype(F32) for r in range(ROWS)]
    rows += [bot_ref[0].astype(F32)]
    for r in range(ROWS):
        sums = []
        for b in range(3):
            total = taps[b : b + 1] * rows[r]
            total += taps[3 + b : 4 + b] * rows[r + 1]
            total += taps[6 + b : 7 + b] * rows[r + 2]
            sums.append(total)
        out = rows[r + 1] + sums[1] + shifted(sums[0], 1) + shifted(sums[2], -1)
        y_ref[r] = out.astype(BF)
        send_ref[:, 0, r] = out.reshape(16, 8, out.shape[-1]).astype(BF)
        send_ref[:, 1, r] = c_ref[r].reshape(16, 8, out.shape[-1])


def conv_forward(x, top, bot, cot, taps):
    block = 256
    grid = (D // block,)
    row = pl.BlockSpec((1, WIDTH, block), lambda i: (0, 0, i))
    return pl.pallas_call(
        conv_kernel,
        grid=grid,
        in_specs=[
            pl.BlockSpec((ROWS, WIDTH, block), lambda i: (0, 0, i)),
            row,
            row,
            pl.BlockSpec((ROWS, WIDTH, block), lambda i: (0, 0, i)),
            pl.BlockSpec((9, block), lambda i: (0, i)),
        ],
        out_specs=[
            pl.BlockSpec((ROWS, WIDTH, block), lambda i: (0, 0, i)),
            pl.BlockSpec((16, 2, ROWS, 8, block), lambda i: (0, 0, 0, 0, i)),
        ],
        out_shape=[
            jax.ShapeDtypeStruct((ROWS, WIDTH, D), BF),
            jax.ShapeDtypeStruct((16, 2, ROWS, 8, D), BF),
        ],
        compiler_params=params(32),
        cost_estimate=cost(5),
    )(x, top, bot, cot, taps)


def conv_back_kernel(x_ref, top_ref, bot_ref, dy_ref, dtop_ref, dbot_ref, k_ref, gx_ref, gk_ref):
    taps = k_ref[...].astype(F32)
    rows = [top_ref[0].astype(F32)]
    rows += [x_ref[r].astype(F32) for r in range(ROWS)]
    rows += [bot_ref[0].astype(F32)]
    grads = [dtop_ref[0].astype(F32)]
    grads += [dy_ref[r].astype(F32) for r in range(ROWS)]
    grads += [dbot_ref[0].astype(F32)]
    gains = [None] * 9
    for r in range(ROWS):
        sums = []
        for b in range(3):
            total = taps[b : b + 1] * grads[r + 2]
            total += taps[3 + b : 4 + b] * grads[r + 1]
            total += taps[6 + b : 7 + b] * grads[r]
            sums.append(total)
        mid = grads[r + 1]
        gx_ref[r] = (mid + sums[1] + shifted(sums[0], -1) + shifted(sums[2], 1)).astype(BF)
        near = (shifted(mid, -1), mid, shifted(mid, 1))
        for a in range(3):
            for b in range(3):
                term = rows[r + a] * near[b]
                slot = a * 3 + b
                gains[slot] = term if gains[slot] is None else gains[slot] + term
    for slot in range(9):
        gk_ref[slot : slot + 1] = jnp.sum(gains[slot], axis=0, keepdims=True)


def conv_backward(x, top, bot, dy, dtop, dbot, taps):
    block = 128
    grid = (D // block,)
    row = pl.BlockSpec((1, WIDTH, block), lambda i: (0, 0, i))
    slab = pl.BlockSpec((ROWS, WIDTH, block), lambda i: (0, 0, i))
    small = pl.BlockSpec((9, block), lambda i: (0, i))
    return pl.pallas_call(
        conv_back_kernel,
        grid=grid,
        in_specs=[slab, row, row, slab, row, row, small],
        out_specs=[slab, small],
        out_shape=[
            jax.ShapeDtypeStruct((ROWS, WIDTH, D), BF),
            jax.ShapeDtypeStruct((9, D), F32),
        ],
        compiler_params=params(32),
        cost_estimate=cost(7),
    )(x, top, bot, dy, dtop, dbot, taps)


def turn(value, cos, sin, first, sign):
    moved = jnp.where(
        first, pltpu.roll(value, HALF - HDIM // 2, axis=1), pltpu.roll(value, HDIM // 2, axis=1)
    )
    return value * cos + moved * sin if sign > 0 else value * cos - moved * sin


def attention(block, q_s, k_s, v_s, d_s, dq_s, dk_s, cos_ref, sin_ref, mask, g_ref):
    scale = 1.0 / math.sqrt(HDIM)
    toks = pl.ds(pl.multiple_of(block * 128, 128), 128)
    cos = cos_ref[...]
    sin = sin_ref[...]
    first = lax.broadcasted_iota(jnp.int32, (128, HALF), 1) % HDIM < HDIM // 2
    q_s[toks] = turn(q_s[toks].astype(F32), cos, sin, first, 1).astype(BF)
    k_s[toks] = turn(k_s[toks].astype(F32), cos, sin, first, 1).astype(BF)
    cols = [slice(h * HDIM, (h + 1) * HDIM) for h in range(HEADS // 2)]
    q = [q_s[toks, c] for c in cols]
    k = [k_s[toks, c] for c in cols]
    v = [v_s[toks, c] for c in cols]
    d_o = [d_s[toks, c] for c in cols]
    scores = [dot_nt(a, b) * scale for a, b in zip(q, k)]
    d_p = [dot_nt(a, b) for a, b in zip(d_o, v)]
    if mask is not None:
        scores = [s + mask for s in scores]
    expo = [jnp.exp(s - jnp.max(s, axis=-1, keepdims=True)) for s in scores]
    prob = [e * (1.0 / jnp.sum(e, axis=-1, keepdims=True)) for e in expo]
    prob_b = [p.astype(BF) for p in prob]
    d_s_b = [
        (p * (x - jnp.sum(p * x, axis=-1, keepdims=True)) * scale).astype(BF)
        for p, x in zip(prob, d_p)
    ]
    for h, c in enumerate(cols):
        g_ref[toks, slice(3 * HALF + c.start, 3 * HALF + c.stop)] = dot(prob_b[h], v[h]).astype(BF)
    for h, c in enumerate(cols):
        g_ref[toks, slice(2 * HALF + c.start, 2 * HALF + c.stop)] = dot_tn(
            prob_b[h], d_o[h]
        ).astype(BF)
    for h, c in enumerate(cols):
        dq_s[:, c] = dot(d_s_b[h], k[h])
    for h, c in enumerate(cols):
        dk_s[:, c] = dot_tn(d_s_b[h], q[h])
    g_ref[toks, slice(0, HALF)] = turn(dq_s[...], cos, sin, first, -1).astype(BF)
    g_ref[toks, slice(HALF, 2 * HALF)] = turn(dk_s[...], cos, sin, first, -1).astype(BF)


def row_kernel(
    y_ref, c_ref, wq_ref, wk_ref, wv_ref, wo_ref, cos_ref, sin_ref,
    g_ref, out_ref, dy_ref, q_s, k_s, v_s, d_s, dq_s, dk_s,
):
    y = y_ref[...]
    cot = c_ref[...]
    q_s[...] = dot(y, wq_ref[...]).astype(BF)
    k_s[...] = dot(y, wk_ref[...]).astype(BF)
    v_s[...] = dot(y, wv_ref[...]).astype(BF)
    d_s[...] = dot_nt(cot, wo_ref[...]).astype(BF)

    @pl.loop(0, TOK // 128)
    def _(block):
        attention(block, q_s, k_s, v_s, d_s, dq_s, dk_s, cos_ref, sin_ref, None, g_ref)

    out_ref[...] = y.astype(F32) + dot(g_ref[:, 3 * HALF :], wo_ref[...])
    dy_ref[...] = (
        cot.astype(F32)
        + dot_nt(g_ref[:, :HALF], wq_ref[...])
        + dot_nt(g_ref[:, HALF : 2 * HALF], wk_ref[...])
        + dot_nt(g_ref[:, 2 * HALF : 3 * HALF], wv_ref[...])
    )


def col_kernel(
    pair_ref, wq_ref, wk_ref, wv_ref, wo_ref, cos_ref, sin_ref, mask_ref, perm_ref,
    yp_ref, cp_ref, g_ref, back_ref, q_s, k_s, v_s, d_s, dq_s, dk_s,
):
    yp_ref[...] = dot(perm_ref[...], pair_ref[:, 0].reshape(TOK, D)).astype(BF)
    cp_ref[...] = dot(perm_ref[...], pair_ref[:, 1].reshape(TOK, D)).astype(BF)
    y = yp_ref[...]
    q_s[...] = dot(y, wq_ref[...]).astype(BF)
    k_s[...] = dot(y, wk_ref[...]).astype(BF)
    v_s[...] = dot(y, wv_ref[...]).astype(BF)
    d_s[...] = dot_nt(cp_ref[...], wo_ref[...]).astype(BF)

    @pl.loop(0, TOK // 128)
    def _(block):
        attention(
            block, q_s, k_s, v_s, d_s, dq_s, dk_s, cos_ref, sin_ref, mask_ref[...], g_ref
        )

    part = (
        dot_nt(g_ref[:, :HALF], wq_ref[...])
        + dot_nt(g_ref[:, HALF : 2 * HALF], wk_ref[...])
        + dot_nt(g_ref[:, 2 * HALF : 3 * HALF], wv_ref[...])
    ).astype(BF)
    back_ref[:, :HALF] = dot_tn(perm_ref[...], g_ref[:, 3 * HALF :]).astype(BF)
    back_ref[:, HALF:] = dot_tn(perm_ref[...], part).astype(BF)


def whole(shape):
    return pl.BlockSpec(shape, lambda i: (0,) * len(shape))


def attention_call(kernel, half, tokens, w_qkv, w_out, tables, outs):
    def columns(which):
        return pl.BlockSpec((D, HALF), lambda i: (0, 2 * which + half))

    return pl.pallas_call(
        kernel,
        grid=(1,),
        in_specs=[whole(t.shape) for t in tokens]
        + [
            columns(0),
            columns(1),
            columns(2),
            pl.BlockSpec((HALF, D), lambda i: (half, 0)),
        ]
        + [whole(t.shape) for t in tables],
        out_specs=[whole(s) for s, _ in outs],
        out_shape=[jax.ShapeDtypeStruct(s, t) for s, t in outs],
        scratch_shapes=[pltpu.VMEM((TOK, HALF), BF)] * 4 + [pltpu.VMEM((128, HALF), F32)] * 2,
        compiler_params=params(60),
        cost_estimate=cost(30),
    )(*tokens, w_qkv, w_qkv, w_qkv, w_out, *tables)


def angle_tables(positions):
    half = HDIM // 2
    base = 10000.0 * 4.0 ** (HDIM / (HDIM - 2.0))
    steps = np.arange(half, dtype=np.float32)
    freq = np.exp(-(2.0 * steps / HDIM) * np.float32(math.log(base))).astype(np.float32)
    angle = positions.astype(np.float32)[:, None] * freq[None, :]
    cos = np.cos(angle).astype(np.float32)
    sin = np.sin(angle).astype(np.float32)
    cos = np.tile(np.concatenate([cos, cos], 1), (1, HEADS // 2))
    sin = np.tile(np.concatenate([-sin, sin], 1), (1, HEADS // 2))
    return jnp.asarray(cos), jnp.asarray(sin)


def col_order():
    order = np.zeros((TOK, TOK), np.float32)
    for pair in range(4):
        for src in range(16):
            for c in range(2):
                for r in range(ROWS):
                    order[pair * 128 + src * 8 + c * 4 + r, src * 32 + r * 8 + pair * 2 + c] = 1.0
    token = np.arange(128)
    positions = (token // 8) * 4 + token % 4
    column = (token // 4) % 2
    mask = np.where(column[:, None] == column[None, :], 0.0, -1e30).astype(np.float32)
    return jnp.asarray(order, BF), positions, jnp.asarray(mask)


def grads_kernel(*refs):
    pick_ref, pick_o_ref, out_ref = refs[-3:]
    sides = (refs[:6], refs[6:12])
    step = pl.program_id(0)

    def both(first, second, pick, cols):
        return jnp.concatenate(
            [dot_nt(pick, ref[:, cols]).astype(BF) for ref in (first, second)], axis=1
        )

    def product(left, first, second):
        return dot(left[:, :TOK], first[...]) + dot(left[:, TOK:], second[...])

    out_ref[:, CHUNK * 10 :] = jnp.zeros((CHIPS // 4, SPARE, 128), BF)
    for z in range(4):

        @pl.when(step == z)
        def _():
            lefts = ([], [])
            rows = ([], [])
            for sub in range(4):
                lo, hi = 240 * (z * 4 + sub), 240 * (z * 4 + sub) + 240
                for which in range(3):
                    for half in range(2):
                        base = which * D + half * HALF
                        a, b = max(lo, base), min(hi, base + HALF)
                        if a >= b:
                            continue
                        shift = which * HALF - base
                        lefts[half].append(
                            both(
                                sides[half][2],
                                sides[half][3],
                                pick_ref[:, a - lo : b - lo],
                                slice(a + shift, b + shift),
                            )
                        )
                        rows[half].append(sub)
            totals = [None] * 4
            extra = []
            for half in range(2):
                y0, y1, g0, g1, c0, c1 = sides[half]
                result = product(jnp.concatenate(lefts[half], axis=0), y0, y1)
                for i, sub in enumerate(rows[half]):
                    term = result[128 * i : 128 * i + 128]
                    totals[sub] = term if totals[sub] is None else totals[sub] + term
                left = [
                    both(c0, c1, pick_o_ref[...], slice(320 * z + 80 * s, 320 * z + 80 * s + 80))
                    for s in range(4)
                ]
                left = jnp.concatenate(left, axis=0)
                extra.append(
                    product(left, g0.at[:, 3 * HALF : 4 * HALF], g1.at[:, 3 * HALF : 4 * HALF])
                )
            extra = jnp.concatenate(extra, axis=1)
            for sub in range(4):
                for j in range(4):
                    main = totals[sub][32 * j : 32 * j + 32]
                    more = extra[64 * sub + 16 * j : 64 * sub + 16 * j + 16]
                    block = jnp.concatenate([main[:24], main[24:] + more[:8], more[8:]], axis=0)
                    block = block.astype(BF)
                    for t in range(10):
                        out_ref[4 * sub + j, CHUNK * t : CHUNK * t + CHUNK] = block[
                            :, 128 * t : 128 * t + 128
                        ]


def pickers():
    core = lax.axis_index("sp") % 2
    lane = jnp.arange(128)[:, None]
    source = (lane // 32) * 2 + core
    pick = ((jnp.arange(240)[None, :] == source * 30 + lane % 32) & (lane % 32 < 30)).astype(BF)
    lane = jnp.arange(64)[:, None]
    source = (lane // 16) * 2 + core
    pick_o = (
        (jnp.arange(80)[None, :] == source * 10 + lane % 16 - 6) & (lane % 16 >= 6)
    ).astype(BF)
    return pick, pick_o


def weight_grads(row, col, picks):
    ins = (*row, *col, *picks)
    return pl.pallas_call(
        grads_kernel,
        grid=(4,),
        in_specs=[
            pl.BlockSpec(v.shape, lambda z: (0, 0), pipeline_mode=pl.Buffered(1)) for v in ins
        ],
        out_specs=pl.BlockSpec((CHIPS // 4, CHUNK * 10 + SPARE, 128), lambda z: (z, 0, 0)),
        out_shape=jax.ShapeDtypeStruct((CHIPS, CHUNK * 10 + SPARE, 128), BF),
        compiler_params=params(60),
        cost_estimate=cost(16),
    )(*ins)


def other_core(value):
    return lax.ppermute(value, "sp", [(i, i ^ 1) for i in range(16)])


def reduce_scatter(chip, gconv):
    small = gconv.reshape(9, CHIPS, 2, 10).transpose(1, 2, 0, 3).reshape(CHIPS, 2, 90)
    high = small.astype(BF)
    low = (small - high.astype(F32)).astype(BF)
    small = jnp.pad(jnp.concatenate([high, low], axis=1), ((0, 0), (0, SPARE - 4), (0, 38)))
    chip = lax.dynamic_update_slice(chip, small, (0, CHUNK * 10, 0))
    same_core = [[2 * i + core for i in range(CHIPS)] for core in range(2)]
    got = lax.all_to_all(
        chip, AXES, split_axis=0, concat_axis=0, axis_index_groups=same_core, tiled=True
    )
    total = jnp.sum(got.astype(F32), axis=0)
    small = total[CHUNK * 10 : CHUNK * 10 + 2] + total[CHUNK * 10 + 2 : CHUNK * 10 + 4]
    core = lax.axis_index("sp") % 2
    mine = lax.dynamic_slice_in_dim(small, core, 1, axis=0)
    mine = mine + other_core(lax.dynamic_slice_in_dim(small, 1 - core, 1, axis=0))
    return total[: CHUNK * 10], mine[0, :90]


def join_kernel(back_ref, part_ref, dpart_ref, wo_ref, out_ref, dy_ref):
    back = back_ref[:, 0].reshape(WIDTH, 3 * HALF)
    out_ref[...] = (part_ref[...] + dot(back[:, :HALF], wo_ref[...])).astype(BF)
    dy_ref[...] = (dpart_ref[...] + back[:, HALF:].astype(F32)).astype(BF)


def join(back, part, dpart, w_out):
    row = pl.BlockSpec((WIDTH, D), lambda r: (r, 0))
    return pl.pallas_call(
        join_kernel,
        grid=(ROWS,),
        in_specs=[
            pl.BlockSpec((16, 1, 8, 3 * HALF), lambda r: (0, r, 0, 0)),
            row,
            row,
            pl.BlockSpec((HALF, D), lambda r: (1, 0)),
        ],
        out_specs=[row] * 2,
        out_shape=[jax.ShapeDtypeStruct((TOK, D), BF)] * 2,
        compiler_params=params(40),
        cost_estimate=cost(5),
    )(back, part, dpart, w_out)


def neighbours(cells):
    last = lax.axis_size("sp") - 1
    down = [(i, i + 1) for i in range(last)]
    up = [(i + 1, i) for i in range(last)]
    return (lax.ppermute(cells[ROWS - 1 :], "sp", down), lax.ppermute(cells[:1], "sp", up))


def spread(value):
    return lax.all_to_all(value, "sp", split_axis=0, concat_axis=0, tiled=True)


def shards(patches, conv_w, w_qkv, w_out, cotangent):
    x = patches[0]
    cot = cotangent[0]
    taps = conv_w.reshape(9, D)
    cot_flat = cot.reshape(TOK, D)
    top, bot = neighbours(x)
    y, pair = conv_forward(x, top, bot, cot, taps)
    y_flat = y.reshape(TOK, D)
    pair = spread(pair.reshape(16, 2 * ROWS * 8, D)).reshape(16, 2, ROWS * 8, D)

    cos_w, sin_w = angle_tables(np.arange(WIDTH))
    g_row, part, dpart = attention_call(
        row_kernel, 0, (y_flat, cot_flat), w_qkv, w_out, (cos_w, sin_w),
        [((TOK, 4 * HALF), BF), ((TOK, D), F32), ((TOK, D), F32)],
    )
    pair, g_row, y_late, cot_late, picks = lax.optimization_barrier(
        (pair, g_row, y_flat, cot_flat, pickers())
    )
    row = []
    for value in (y_late, g_row, cot_late):
        row += [value, other_core(value)]
    order, positions, mask = col_order()
    cos_h, sin_h = angle_tables(positions)
    y_col, c_col, g_col, back = attention_call(
        col_kernel, 1, (pair,), w_qkv, w_out, (cos_h, sin_h, mask, order),
        [((TOK, D), BF), ((TOK, D), BF), ((TOK, 4 * HALF), BF), ((TOK, 3 * HALF), BF)],
    )
    returned = spread(back.reshape(16, ROWS * 8, 3 * HALF)).reshape(16, ROWS, 8, 3 * HALF)
    col = []
    for value in (y_col, g_col, c_col):
        col += [value, other_core(value)]
    chip = weight_grads(row, col, picks)
    returned, chip = lax.optimization_barrier((returned, chip))
    layer_out, dy = join(returned, part, dpart, w_out)
    dy = dy.reshape(ROWS, WIDTH, D)
    dtop, dbot = neighbours(dy)
    grad_x, gconv = conv_backward(x, top, bot, dy, dtop, dbot, taps)
    factor = 1.0 / math.sqrt(8 * 64 * 128)
    total, gconv = reduce_scatter(chip, gconv)
    total = total.reshape(10, CHUNK, 128).transpose(0, 2, 1).reshape(D, CHUNK) * factor
    return (
        layer_out.reshape(1, ROWS, WIDTH, D),
        grad_x[None],
        total[:, :30],
        total[:, 30:],
        (gconv * factor).reshape(3, 3, 10),
    )


def solution(mesh):
    slab = P("grp", "sp", None, None)
    return jax.shard_map(
        shards,
        mesh=mesh,
        in_specs=(slab, P(), P(), P(), slab),
        out_specs=(slab, slab, P(None, AXES), P(None, AXES), P(None, None, AXES)),
        check_vma=False,
    )
```

```python
import functools
import math

import jax
import jax.numpy as jnp
import numpy as np
from jax import lax
from jax.experimental import pallas as pl
from jax.experimental.pallas import tpu as pltpu
from jax.sharding import PartitionSpec as P

HEADS = 16
HDIM = 80
D = 1280
HALF = 640
ROWS = 4
WIDTH = 128
TOK = ROWS * WIDTH
AXES = ("grp", "sp")
BF = jnp.bfloat16
F32 = jnp.float32
MIB = 1024 * 1024

CHUNK = 40
CHIPS = 64
SPARE = 8


def dot(a, b):
    return lax.dot_general(a, b, (((1,), (0,)), ((), ())), preferred_element_type=F32)


def dot_nt(a, b):
    return lax.dot_general(a, b, (((1,), (1,)), ((), ())), preferred_element_type=F32)


def dot_tn(a, b):
    return lax.dot_general(a, b, (((0,), (0,)), ((), ())), preferred_element_type=F32)


def params(limit):
    return pltpu.CompilerParams(vmem_limit_bytes=limit * MIB)


def cost(micros):
    return pl.CostEstimate(flops=int(micros * 1.1535e9), bytes_accessed=0, transcendentals=0)


def shifted(value, step):
    index = lax.broadcasted_iota(jnp.int32, value.shape, 0)
    moved = pltpu.roll(value, step % WIDTH, axis=0)
    edge = 0 if step == 1 else WIDTH - 1
    return jnp.where(index == edge, 0.0, moved)


def conv_kernel(x_ref, top_ref, bot_ref, c_ref, k_ref, y_ref, send_ref):
    taps = k_ref[...].astype(F32)
    rows = [top_ref[0].astype(F32)]
    rows += [x_ref[r].astype(F32) for r in range(ROWS)]
    rows += [bot_ref[0].astype(F32)]
    for r in range(ROWS):
        sums = []
        for b in range(3):
            total = taps[b : b + 1] * rows[r]
            total += taps[3 + b : 4 + b] * rows[r + 1]
            total += taps[6 + b : 7 + b] * rows[r + 2]
            sums.append(total)
        out = rows[r + 1] + sums[1] + shifted(sums[0], 1) + shifted(sums[2], -1)
        y_ref[r] = out.astype(BF)
        send_ref[:, 0, r] = out.reshape(16, 8, out.shape[-1]).astype(BF)
        send_ref[:, 1, r] = c_ref[r].reshape(16, 8, out.shape[-1])


def conv_forward(x, top, bot, cot, taps):
    block = 256
    grid = (D // block,)
    row = pl.BlockSpec((1, WIDTH, block), lambda i: (0, 0, i))
    return pl.pallas_call(
        conv_kernel,
        grid=grid,
        in_specs=[
            pl.BlockSpec((ROWS, WIDTH, block), lambda i: (0, 0, i)),
            row,
            row,
            pl.BlockSpec((ROWS, WIDTH, block), lambda i: (0, 0, i)),
            pl.BlockSpec((9, block), lambda i: (0, i)),
        ],
        out_specs=[
            pl.BlockSpec((ROWS, WIDTH, block), lambda i: (0, 0, i)),
            pl.BlockSpec((16, 2, ROWS, 8, block), lambda i: (0, 0, 0, 0, i)),
        ],
        out_shape=[
            jax.ShapeDtypeStruct((ROWS, WIDTH, D), BF),
            jax.ShapeDtypeStruct((16, 2, ROWS, 8, D), BF),
        ],
        compiler_params=params(32),
        cost_estimate=cost(5),
    )(x, top, bot, cot, taps)


def conv_back_kernel(dy_ref, dtop_ref, dbot_ref, k_ref, gx_ref):
    taps = k_ref[...].astype(F32)
    grads = [dtop_ref[0].astype(F32)]
    grads += [dy_ref[r].astype(F32) for r in range(ROWS)]
    grads += [dbot_ref[0].astype(F32)]
    for r in range(ROWS):
        sums = []
        for b in range(3):
            total = taps[b : b + 1] * grads[r + 2]
            total += taps[3 + b : 4 + b] * grads[r + 1]
            total += taps[6 + b : 7 + b] * grads[r]
            sums.append(total)
        mid = grads[r + 1]
        gx_ref[r] = (mid + sums[1] + shifted(sums[0], -1) + shifted(sums[2], 1)).astype(BF)


def conv_gain_kernel(x_ref, top_ref, bot_ref, dy_ref, gk_ref):
    rows = [top_ref[0].astype(F32)]
    rows += [x_ref[r].astype(F32) for r in range(ROWS)]
    rows += [bot_ref[0].astype(F32)]
    gains = [None] * 9
    for r in range(ROWS):
        mid = dy_ref[r].astype(F32)
        near = (shifted(mid, -1), mid, shifted(mid, 1))
        for a in range(3):
            for b in range(3):
                term = rows[r + a] * near[b]
                slot = a * 3 + b
                gains[slot] = term if gains[slot] is None else gains[slot] + term
    for slot in range(9):
        gk_ref[slot : slot + 1] = jnp.sum(gains[slot], axis=0, keepdims=True)


def blocks(block):
    row = pl.BlockSpec((1, WIDTH, block), lambda i: (0, 0, i))
    slab = pl.BlockSpec((ROWS, WIDTH, block), lambda i: (0, 0, i))
    small = pl.BlockSpec((9, block), lambda i: (0, i))
    return row, slab, small


def conv_backward(dy, dtop, dbot, taps):
    row, slab, small = blocks(256)
    return pl.pallas_call(
        conv_back_kernel,
        grid=(D // 256,),
        in_specs=[slab, row, row, small],
        out_specs=slab,
        out_shape=jax.ShapeDtypeStruct((ROWS, WIDTH, D), BF),
        compiler_params=params(60),
        cost_estimate=cost(4),
    )(dy, dtop, dbot, taps)


def conv_gain(x, top, bot, dy):
    row, slab, small = blocks(128)
    return pl.pallas_call(
        conv_gain_kernel,
        grid=(D // 128,),
        in_specs=[slab, row, row, slab],
        out_specs=small,
        out_shape=jax.ShapeDtypeStruct((9, D), F32),
        compiler_params=params(60),
        cost_estimate=cost(4),
    )(x, top, bot, dy)


def turn(value, cos, sin, first, sign):
    moved = jnp.where(
        first, pltpu.roll(value, HALF - HDIM // 2, axis=1), pltpu.roll(value, HDIM // 2, axis=1)
    )
    return value * cos + moved * sin if sign > 0 else value * cos - moved * sin


def attention(block, q_s, k_s, v_s, d_s, dq_s, dk_s, cos_ref, sin_ref, mask, g_ref):
    scale = 1.0 / math.sqrt(HDIM)
    toks = pl.ds(pl.multiple_of(block * 128, 128), 128)
    cos = cos_ref[...]
    sin = sin_ref[...]
    first = lax.broadcasted_iota(jnp.int32, (128, HALF), 1) % HDIM < HDIM // 2
    q_s[toks] = turn(q_s[toks].astype(F32), cos, sin, first, 1).astype(BF)
    k_s[toks] = turn(k_s[toks].astype(F32), cos, sin, first, 1).astype(BF)
    cols = [slice(h * HDIM, (h + 1) * HDIM) for h in range(HEADS // 2)]
    q = [q_s[toks, c] for c in cols]
    k = [k_s[toks, c] for c in cols]
    v = [v_s[toks, c] for c in cols]
    d_o = [d_s[toks, c] for c in cols]
    scores = [dot_nt(a, b) * scale for a, b in zip(q, k)]
    d_p = [dot_nt(a, b) for a, b in zip(d_o, v)]
    if mask is not None:
        scores = [s + mask for s in scores]
    expo = [jnp.exp(s - jnp.max(s, axis=-1, keepdims=True)) for s in scores]
    prob = [e * (1.0 / jnp.sum(e, axis=-1, keepdims=True)) for e in expo]
    prob_b = [p.astype(BF) for p in prob]
    d_s_b = [
        (p * (x - jnp.sum(p * x, axis=-1, keepdims=True)) * scale).astype(BF)
        for p, x in zip(prob, d_p)
    ]
    for h, c in enumerate(cols):
        g_ref[toks, slice(3 * HALF + c.start, 3 * HALF + c.stop)] = dot(prob_b[h], v[h]).astype(BF)
    for h, c in enumerate(cols):
        g_ref[toks, slice(2 * HALF + c.start, 2 * HALF + c.stop)] = dot_tn(
            prob_b[h], d_o[h]
        ).astype(BF)
    for h, c in enumerate(cols):
        dq_s[:, c] = dot(d_s_b[h], k[h])
    for h, c in enumerate(cols):
        dk_s[:, c] = dot_tn(d_s_b[h], q[h])
    g_ref[toks, slice(0, HALF)] = turn(dq_s[...], cos, sin, first, -1).astype(BF)
    g_ref[toks, slice(HALF, 2 * HALF)] = turn(dk_s[...], cos, sin, first, -1).astype(BF)


def row_kernel(
    y_ref, c_ref, wq_ref, wk_ref, wv_ref, wo_ref, cos_ref, sin_ref,
    g_ref, out_ref, dy_ref, q_s, k_s, v_s, d_s, dq_s, dk_s,
):
    y = y_ref[...]
    cot = c_ref[...]
    q_s[...] = dot(y, wq_ref[...]).astype(BF)
    k_s[...] = dot(y, wk_ref[...]).astype(BF)
    v_s[...] = dot(y, wv_ref[...]).astype(BF)
    d_s[...] = dot_nt(cot, wo_ref[...]).astype(BF)

    @pl.loop(0, TOK // 128)
    def _(block):
        attention(block, q_s, k_s, v_s, d_s, dq_s, dk_s, cos_ref, sin_ref, None, g_ref)

    out_ref[...] = y.astype(F32) + dot(g_ref[:, 3 * HALF :], wo_ref[...])
    dy_ref[...] = (
        cot.astype(F32)
        + dot_nt(g_ref[:, :HALF], wq_ref[...])
        + dot_nt(g_ref[:, HALF : 2 * HALF], wk_ref[...])
        + dot_nt(g_ref[:, 2 * HALF : 3 * HALF], wv_ref[...])
    )


def col_kernel(
    pair_ref, wq_ref, wk_ref, wv_ref, wo_ref, cos_ref, sin_ref, mask_ref, perm_ref,
    yp_ref, cp_ref, g_ref, back_ref, q_s, k_s, v_s, d_s, dq_s, dk_s,
):
    yp_ref[...] = dot(perm_ref[...], pair_ref[:, 0].reshape(TOK, D)).astype(BF)
    cp_ref[...] = dot(perm_ref[...], pair_ref[:, 1].reshape(TOK, D)).astype(BF)
    y = yp_ref[...]
    q_s[...] = dot(y, wq_ref[...]).astype(BF)
    k_s[...] = dot(y, wk_ref[...]).astype(BF)
    v_s[...] = dot(y, wv_ref[...]).astype(BF)
    d_s[...] = dot_nt(cp_ref[...], wo_ref[...]).astype(BF)

    @pl.loop(0, TOK // 128)
    def _(block):
        attention(
            block, q_s, k_s, v_s, d_s, dq_s, dk_s, cos_ref, sin_ref, mask_ref[...], g_ref
        )

    part = (
        dot_nt(g_ref[:, :HALF], wq_ref[...])
        + dot_nt(g_ref[:, HALF : 2 * HALF], wk_ref[...])
        + dot_nt(g_ref[:, 2 * HALF : 3 * HALF], wv_ref[...])
    ).astype(BF)
    back_ref[:, :HALF] = dot_tn(perm_ref[...], g_ref[:, 3 * HALF :]).astype(BF)
    back_ref[:, HALF:] = dot_tn(perm_ref[...], part).astype(BF)


def whole(shape):
    return pl.BlockSpec(shape, lambda i: (0,) * len(shape))


def attention_call(kernel, half, tokens, w_qkv, w_out, tables, outs):
    def columns(which):
        return pl.BlockSpec((D, HALF), lambda i: (0, 2 * which + half))

    return pl.pallas_call(
        kernel,
        grid=(1,),
        in_specs=[whole(t.shape) for t in tokens]
        + [
            columns(0),
            columns(1),
            columns(2),
            pl.BlockSpec((HALF, D), lambda i: (half, 0)),
        ]
        + [whole(t.shape) for t in tables],
        out_specs=[whole(s) for s, _ in outs],
        out_shape=[jax.ShapeDtypeStruct(s, t) for s, t in outs],
        scratch_shapes=[pltpu.VMEM((TOK, HALF), BF)] * 4 + [pltpu.VMEM((128, HALF), F32)] * 2,
        compiler_params=params(60),
        cost_estimate=cost(30),
    )(*tokens, w_qkv, w_qkv, w_qkv, w_out, *tables)


def angle_tables(positions):
    half = HDIM // 2
    base = 10000.0 * 4.0 ** (HDIM / (HDIM - 2.0))
    steps = np.arange(half, dtype=np.float32)
    freq = np.exp(-(2.0 * steps / HDIM) * np.float32(math.log(base))).astype(np.float32)
    angle = positions.astype(np.float32)[:, None] * freq[None, :]
    cos = np.cos(angle).astype(np.float32)
    sin = np.sin(angle).astype(np.float32)
    cos = np.tile(np.concatenate([cos, cos], 1), (1, HEADS // 2))
    sin = np.tile(np.concatenate([-sin, sin], 1), (1, HEADS // 2))
    return jnp.asarray(cos), jnp.asarray(sin)


def col_order():
    order = np.zeros((TOK, TOK), np.float32)
    for pair in range(4):
        for src in range(16):
            for c in range(2):
                for r in range(ROWS):
                    order[pair * 128 + src * 8 + c * 4 + r, src * 32 + r * 8 + pair * 2 + c] = 1.0
    token = np.arange(128)
    positions = (token // 8) * 4 + token % 4
    column = (token // 4) % 2
    mask = np.where(column[:, None] == column[None, :], 0.0, -1e30).astype(np.float32)
    return jnp.asarray(order, BF), positions, jnp.asarray(mask)


def grads_kernel(*refs):
    pick_ref, pick_o_ref, out_ref = refs[-3:]
    sides = (refs[:6], refs[6:12])
    step = pl.program_id(0)

    def both(first, second, pick, cols):
        return jnp.concatenate(
            [dot_nt(pick, ref[:, cols]).astype(BF) for ref in (first, second)], axis=1
        )

    def product(left, first, second):
        return dot(left[:, :TOK], first[...]) + dot(left[:, TOK:], second[...])

    out_ref[:, CHUNK * 10 :] = jnp.zeros((CHIPS // 4, SPARE, 128), BF)
    for z in range(4):

        @pl.when(step == z)
        def _():
            lefts = ([], [])
            rows = ([], [])
            for sub in range(4):
                lo, hi = 240 * (z * 4 + sub), 240 * (z * 4 + sub) + 240
                for which in range(3):
                    for half in range(2):
                        base = which * D + half * HALF
                        a, b = max(lo, base), min(hi, base + HALF)
                        if a >= b:
                            continue
                        shift = which * HALF - base
                        lefts[half].append(
                            both(
                                sides[half][2],
                                sides[half][3],
                                pick_ref[:, a - lo : b - lo],
                                slice(a + shift, b + shift),
                            )
                        )
                        rows[half].append(sub)
            totals = [None] * 4
            extra = []
            for half in range(2):
                y0, y1, g0, g1, c0, c1 = sides[half]
                result = product(jnp.concatenate(lefts[half], axis=0), y0, y1)
                for i, sub in enumerate(rows[half]):
                    term = result[128 * i : 128 * i + 128]
                    totals[sub] = term if totals[sub] is None else totals[sub] + term
                left = [
                    both(c0, c1, pick_o_ref[...], slice(320 * z + 80 * s, 320 * z + 80 * s + 80))
                    for s in range(4)
                ]
                left = jnp.concatenate(left, axis=0)
                extra.append(
                    product(left, g0.at[:, 3 * HALF : 4 * HALF], g1.at[:, 3 * HALF : 4 * HALF])
                )
            extra = jnp.concatenate(extra, axis=1)
            for sub in range(4):
                for j in range(4):
                    main = totals[sub][32 * j : 32 * j + 32]
                    more = extra[64 * sub + 16 * j : 64 * sub + 16 * j + 16]
                    block = jnp.concatenate([main[:24], main[24:] + more[:8], more[8:]], axis=0)
                    block = block.astype(BF)
                    for t in range(10):
                        out_ref[4 * sub + j, CHUNK * t : CHUNK * t + CHUNK] = block[
                            :, 128 * t : 128 * t + 128
                        ]


def pickers():
    core = lax.axis_index("sp") % 2
    lane = jnp.arange(128)[:, None]
    source = (lane // 32) * 2 + core
    pick = ((jnp.arange(240)[None, :] == source * 30 + lane % 32) & (lane % 32 < 30)).astype(BF)
    lane = jnp.arange(64)[:, None]
    source = (lane // 16) * 2 + core
    pick_o = (
        (jnp.arange(80)[None, :] == source * 10 + lane % 16 - 6) & (lane % 16 >= 6)
    ).astype(BF)
    return pick, pick_o


def weight_grads(row, col, picks):
    ins = (*row, *col, *picks)
    return pl.pallas_call(
        grads_kernel,
        grid=(4,),
        in_specs=[
            pl.BlockSpec(v.shape, lambda z: (0, 0), pipeline_mode=pl.Buffered(1)) for v in ins
        ],
        out_specs=pl.BlockSpec((CHIPS // 4, CHUNK * 10 + SPARE, 128), lambda z: (z, 0, 0)),
        out_shape=jax.ShapeDtypeStruct((CHIPS, CHUNK * 10 + SPARE, 128), BF),
        compiler_params=params(60),
        cost_estimate=cost(16),
    )(*ins)


def other_core(value):
    return lax.ppermute(value, "sp", [(i, i ^ 1) for i in range(16)])


def reduce_scatter(chip, gconv):
    small = gconv.reshape(9, CHIPS, 2, 10).transpose(1, 2, 0, 3).reshape(CHIPS, 2, 90)
    high = small.astype(BF)
    low = (small - high.astype(F32)).astype(BF)
    small = jnp.pad(jnp.concatenate([high, low], axis=1), ((0, 0), (0, SPARE - 4), (0, 38)))
    chip = lax.dynamic_update_slice(chip, small, (0, CHUNK * 10, 0))
    same_core = [[2 * i + core for i in range(CHIPS)] for core in range(2)]
    got = lax.all_to_all(
        chip, AXES, split_axis=0, concat_axis=0, axis_index_groups=same_core, tiled=True
    )
    total = jnp.sum(got.astype(F32), axis=0)
    small = total[CHUNK * 10 : CHUNK * 10 + 2] + total[CHUNK * 10 + 2 : CHUNK * 10 + 4]
    core = lax.axis_index("sp") % 2
    mine = lax.dynamic_slice_in_dim(small, core, 1, axis=0)
    mine = mine + other_core(lax.dynamic_slice_in_dim(small, 1 - core, 1, axis=0))
    return total[: CHUNK * 10], mine[0, :90]


def join_kernel(back_ref, part_ref, dpart_ref, wo_ref, out_ref, dy_ref):
    back = back_ref[:, 0].reshape(WIDTH, 3 * HALF)
    out_ref[...] = (part_ref[...] + dot(back[:, :HALF], wo_ref[...])).astype(BF)
    dy_ref[...] = (dpart_ref[...] + back[:, HALF:].astype(F32)).astype(BF)


def join(back, part, dpart, w_out):
    row = pl.BlockSpec((WIDTH, D), lambda r: (r, 0))
    return pl.pallas_call(
        join_kernel,
        grid=(ROWS,),
        in_specs=[
            pl.BlockSpec((16, 1, 8, 3 * HALF), lambda r: (0, r, 0, 0)),
            row,
            row,
            pl.BlockSpec((HALF, D), lambda r: (1, 0)),
        ],
        out_specs=[row] * 2,
        out_shape=[jax.ShapeDtypeStruct((TOK, D), BF)] * 2,
        compiler_params=params(60),
        cost_estimate=cost(5),
    )(back, part, dpart, w_out)


def neighbours(cells):
    last = lax.axis_size("sp") - 1
    down = [(i, i + 1) for i in range(last)]
    up = [(i + 1, i) for i in range(last)]
    return (lax.ppermute(cells[ROWS - 1 :], "sp", down), lax.ppermute(cells[:1], "sp", up))


def spread(value):
    return lax.all_to_all(value, "sp", split_axis=0, concat_axis=0, tiled=True)


def shards(patches, conv_w, w_qkv, w_out, cotangent):
    x = patches[0]
    cot = cotangent[0]
    taps = conv_w.reshape(9, D)
    cot_flat = cot.reshape(TOK, D)
    top, bot = neighbours(x)
    y, pair = conv_forward(x, top, bot, cot, taps)
    y_flat = y.reshape(TOK, D)
    pair = spread(pair.reshape(16, 2 * ROWS * 8, D)).reshape(16, 2, ROWS * 8, D)

    cos_w, sin_w = angle_tables(np.arange(WIDTH))
    g_row, part, dpart = attention_call(
        row_kernel, 0, (y_flat, cot_flat), w_qkv, w_out, (cos_w, sin_w),
        [((TOK, 4 * HALF), BF), ((TOK, D), F32), ((TOK, D), F32)],
    )
    pair, g_row, y_late, cot_late, picks = lax.optimization_barrier(
        (pair, g_row, y_flat, cot_flat, pickers())
    )
    row = []
    for value in (y_late, g_row, cot_late):
        row += [value, other_core(value)]
    order, positions, mask = col_order()
    cos_h, sin_h = angle_tables(positions)
    y_col, c_col, g_col, back = attention_call(
        col_kernel, 1, (pair,), w_qkv, w_out, (cos_h, sin_h, mask, order),
        [((TOK, D), BF), ((TOK, D), BF), ((TOK, 4 * HALF), BF), ((TOK, 3 * HALF), BF)],
    )
    returned = spread(back.reshape(16, ROWS * 8, 3 * HALF)).reshape(16, ROWS, 8, 3 * HALF)
    col = []
    for value in (y_col, g_col, c_col):
        col += [value, other_core(value)]
    chip = weight_grads(row, col, picks)
    returned, chip = lax.optimization_barrier((returned, chip))
    layer_out, dy = join(returned, part, dpart, w_out)
    dy = dy.reshape(ROWS, WIDTH, D)
    dtop, dbot = neighbours(dy)
    gconv = conv_gain(x, top, bot, dy)
    gconv, dtop, dbot = lax.optimization_barrier((gconv, dtop, dbot))
    grad_x = conv_backward(dy, dtop, dbot, taps)
    factor = 1.0 / math.sqrt(8 * 64 * 128)
    total, gconv = reduce_scatter(chip, gconv)
    total = total.reshape(10, CHUNK, 128).transpose(0, 2, 1).reshape(D, CHUNK) * factor
    return (
        layer_out.reshape(1, ROWS, WIDTH, D),
        grad_x[None],
        total[:, :30],
        total[:, 30:],
        (gconv * factor).reshape(3, 3, 10),
    )


def solution(mesh):
    slab = P("grp", "sp", None, None)
    return jax.shard_map(
        shards,
        mesh=mesh,
        in_specs=(slab, P(), P(), P(), slab),
        out_specs=(slab, slab, P(None, AXES), P(None, AXES), P(None, None, AXES)),
        check_vma=False,
    )
```

```python
import functools
import math

import jax
import jax.numpy as jnp
import numpy as np
from jax import lax
from jax.experimental import pallas as pl
from jax.experimental.pallas import tpu as pltpu
from jax.sharding import PartitionSpec as P

HEADS = 16
HDIM = 80
D = 1280
HALF = 640
ROWS = 4
WIDTH = 128
TOK = ROWS * WIDTH
AXES = ("grp", "sp")
BF = jnp.bfloat16
F32 = jnp.float32
MIB = 1024 * 1024

CHUNK = 40
CHIPS = 64
SPARE = 8


def dot(a, b):
    return lax.dot_general(a, b, (((1,), (0,)), ((), ())), preferred_element_type=F32)


def dot_nt(a, b):
    return lax.dot_general(a, b, (((1,), (1,)), ((), ())), preferred_element_type=F32)


def dot_tn(a, b):
    return lax.dot_general(a, b, (((0,), (0,)), ((), ())), preferred_element_type=F32)


def params(limit):
    return pltpu.CompilerParams(vmem_limit_bytes=limit * MIB)


def cost(micros):
    return pl.CostEstimate(flops=int(micros * 1.1535e9), bytes_accessed=0, transcendentals=0)


def shifted(value, step):
    index = lax.broadcasted_iota(jnp.int32, value.shape, 0)
    moved = pltpu.roll(value, step % WIDTH, axis=0)
    edge = 0 if step == 1 else WIDTH - 1
    return jnp.where(index == edge, 0.0, moved)


def conv_kernel(x_ref, top_ref, bot_ref, c_ref, k_ref, y_ref, send_ref):
    taps = k_ref[...].astype(F32)
    rows = [top_ref[0].astype(F32)]
    rows += [x_ref[r].astype(F32) for r in range(ROWS)]
    rows += [bot_ref[0].astype(F32)]
    for r in range(ROWS):
        sums = []
        for b in range(3):
            total = taps[b : b + 1] * rows[r]
            total += taps[3 + b : 4 + b] * rows[r + 1]
            total += taps[6 + b : 7 + b] * rows[r + 2]
            sums.append(total)
        out = rows[r + 1] + sums[1] + shifted(sums[0], 1) + shifted(sums[2], -1)
        y_ref[r] = out.astype(BF)
        send_ref[:, 0, r] = out.reshape(16, 8, out.shape[-1]).astype(BF)
        send_ref[:, 1, r] = c_ref[r].reshape(16, 8, out.shape[-1])


def conv_forward(x, top, bot, cot, taps):
    block = 256
    grid = (D // block,)
    row = pl.BlockSpec((1, WIDTH, block), lambda i: (0, 0, i))
    return pl.pallas_call(
        conv_kernel,
        grid=grid,
        in_specs=[
            pl.BlockSpec((ROWS, WIDTH, block), lambda i: (0, 0, i)),
            row,
            row,
            pl.BlockSpec((ROWS, WIDTH, block), lambda i: (0, 0, i)),
            pl.BlockSpec((9, block), lambda i: (0, i)),
        ],
        out_specs=[
            pl.BlockSpec((ROWS, WIDTH, block), lambda i: (0, 0, i)),
            pl.BlockSpec((16, 2, ROWS, 8, block), lambda i: (0, 0, 0, 0, i)),
        ],
        out_shape=[
            jax.ShapeDtypeStruct((ROWS, WIDTH, D), BF),
            jax.ShapeDtypeStruct((16, 2, ROWS, 8, D), BF),
        ],
        compiler_params=params(32),
        cost_estimate=cost(5),
    )(x, top, bot, cot, taps)


def conv_back_kernel(dy_ref, dtop_ref, dbot_ref, k_ref, gx_ref):
    taps = k_ref[...].astype(F32)
    grads = [dtop_ref[0].astype(F32)]
    grads += [dy_ref[r].astype(F32) for r in range(ROWS)]
    grads += [dbot_ref[0].astype(F32)]
    for r in range(ROWS):
        sums = []
        for b in range(3):
            total = taps[b : b + 1] * grads[r + 2]
            total += taps[3 + b : 4 + b] * grads[r + 1]
            total += taps[6 + b : 7 + b] * grads[r]
            sums.append(total)
        mid = grads[r + 1]
        gx_ref[r] = (mid + sums[1] + shifted(sums[0], -1) + shifted(sums[2], 1)).astype(BF)


def conv_gain_kernel(x_ref, top_ref, bot_ref, dy_ref, gk_ref):
    rows = [top_ref[0].astype(F32)]
    rows += [x_ref[r].astype(F32) for r in range(ROWS)]
    rows += [bot_ref[0].astype(F32)]
    gains = [None] * 9
    for r in range(ROWS):
        mid = dy_ref[r].astype(F32)
        near = (shifted(mid, -1), mid, shifted(mid, 1))
        for a in range(3):
            for b in range(3):
                term = rows[r + a] * near[b]
                slot = a * 3 + b
                gains[slot] = term if gains[slot] is None else gains[slot] + term
    for slot in range(9):
        gk_ref[slot : slot + 1] = jnp.sum(gains[slot], axis=0, keepdims=True)


def blocks(block):
    row = pl.BlockSpec((1, WIDTH, block), lambda i: (0, 0, i))
    slab = pl.BlockSpec((ROWS, WIDTH, block), lambda i: (0, 0, i))
    small = pl.BlockSpec((9, block), lambda i: (0, i))
    return row, slab, small


def conv_backward(dy, dtop, dbot, taps):
    row, slab, small = blocks(256)
    return pl.pallas_call(
        conv_back_kernel,
        grid=(D // 256,),
        in_specs=[slab, row, row, small],
        out_specs=slab,
        out_shape=jax.ShapeDtypeStruct((ROWS, WIDTH, D), BF),
        compiler_params=params(16),
        cost_estimate=cost(4),
    )(dy, dtop, dbot, taps)


def conv_gain(x, top, bot, dy):
    row, slab, small = blocks(128)
    return pl.pallas_call(
        conv_gain_kernel,
        grid=(D // 128,),
        in_specs=[slab, row, row, slab],
        out_specs=small,
        out_shape=jax.ShapeDtypeStruct((9, D), F32),
        compiler_params=params(60),
        cost_estimate=cost(4),
    )(x, top, bot, dy)


def turn(value, cos, sin, first, sign):
    moved = jnp.where(
        first, pltpu.roll(value, HALF - HDIM // 2, axis=1), pltpu.roll(value, HDIM // 2, axis=1)
    )
    return value * cos + moved * sin if sign > 0 else value * cos - moved * sin


def attention(block, q_s, k_s, v_s, d_s, dq_s, dk_s, cos_ref, sin_ref, mask, g_ref):
    scale = 1.0 / math.sqrt(HDIM)
    toks = pl.ds(pl.multiple_of(block * 128, 128), 128)
    cos = cos_ref[...]
    sin = sin_ref[...]
    first = lax.broadcasted_iota(jnp.int32, (128, HALF), 1) % HDIM < HDIM // 2
    q_s[toks] = turn(q_s[toks].astype(F32), cos, sin, first, 1).astype(BF)
    k_s[toks] = turn(k_s[toks].astype(F32), cos, sin, first, 1).astype(BF)
    cols = [slice(h * HDIM, (h + 1) * HDIM) for h in range(HEADS // 2)]
    q = [q_s[toks, c] for c in cols]
    k = [k_s[toks, c] for c in cols]
    v = [v_s[toks, c] for c in cols]
    d_o = [d_s[toks, c] for c in cols]
    scores = [dot_nt(a, b) * scale for a, b in zip(q, k)]
    d_p = [dot_nt(a, b) for a, b in zip(d_o, v)]
    if mask is not None:
        scores = [s + mask for s in scores]
    expo = [jnp.exp(s - jnp.max(s, axis=-1, keepdims=True)) for s in scores]
    prob = [e * (1.0 / jnp.sum(e, axis=-1, keepdims=True)) for e in expo]
    prob_b = [p.astype(BF) for p in prob]
    d_s_b = [
        (p * (x - jnp.sum(p * x, axis=-1, keepdims=True)) * scale).astype(BF)
        for p, x in zip(prob, d_p)
    ]
    for h, c in enumerate(cols):
        g_ref[toks, slice(3 * HALF + c.start, 3 * HALF + c.stop)] = dot(prob_b[h], v[h]).astype(BF)
    for h, c in enumerate(cols):
        g_ref[toks, slice(2 * HALF + c.start, 2 * HALF + c.stop)] = dot_tn(
            prob_b[h], d_o[h]
        ).astype(BF)
    for h, c in enumerate(cols):
        dq_s[:, c] = dot(d_s_b[h], k[h])
    for h, c in enumerate(cols):
        dk_s[:, c] = dot_tn(d_s_b[h], q[h])
    g_ref[toks, slice(0, HALF)] = turn(dq_s[...], cos, sin, first, -1).astype(BF)
    g_ref[toks, slice(HALF, 2 * HALF)] = turn(dk_s[...], cos, sin, first, -1).astype(BF)


def row_kernel(
    y_ref, c_ref, wq_ref, wk_ref, wv_ref, wo_ref, cos_ref, sin_ref,
    g_ref, out_ref, dy_ref, q_s, k_s, v_s, d_s, dq_s, dk_s,
):
    y = y_ref[...]
    cot = c_ref[...]
    q_s[...] = dot(y, wq_ref[...]).astype(BF)
    k_s[...] = dot(y, wk_ref[...]).astype(BF)
    v_s[...] = dot(y, wv_ref[...]).astype(BF)
    d_s[...] = dot_nt(cot, wo_ref[...]).astype(BF)

    @pl.loop(0, TOK // 128)
    def _(block):
        attention(block, q_s, k_s, v_s, d_s, dq_s, dk_s, cos_ref, sin_ref, None, g_ref)

    out_ref[...] = y.astype(F32) + dot(g_ref[:, 3 * HALF :], wo_ref[...])
    dy_ref[...] = (
        cot.astype(F32)
        + dot_nt(g_ref[:, :HALF], wq_ref[...])
        + dot_nt(g_ref[:, HALF : 2 * HALF], wk_ref[...])
        + dot_nt(g_ref[:, 2 * HALF : 3 * HALF], wv_ref[...])
    )


def col_kernel(
    pair_ref, wq_ref, wk_ref, wv_ref, wo_ref, cos_ref, sin_ref, mask_ref, perm_ref,
    yp_ref, cp_ref, g_ref, back_ref, q_s, k_s, v_s, d_s, dq_s, dk_s,
):
    yp_ref[...] = dot(perm_ref[...], pair_ref[:, 0].reshape(TOK, D)).astype(BF)
    cp_ref[...] = dot(perm_ref[...], pair_ref[:, 1].reshape(TOK, D)).astype(BF)
    y = yp_ref[...]
    q_s[...] = dot(y, wq_ref[...]).astype(BF)
    k_s[...] = dot(y, wk_ref[...]).astype(BF)
    v_s[...] = dot(y, wv_ref[...]).astype(BF)
    d_s[...] = dot_nt(cp_ref[...], wo_ref[...]).astype(BF)

    @pl.loop(0, TOK // 128)
    def _(block):
        attention(
            block, q_s, k_s, v_s, d_s, dq_s, dk_s, cos_ref, sin_ref, mask_ref[...], g_ref
        )

    part = (
        dot_nt(g_ref[:, :HALF], wq_ref[...])
        + dot_nt(g_ref[:, HALF : 2 * HALF], wk_ref[...])
        + dot_nt(g_ref[:, 2 * HALF : 3 * HALF], wv_ref[...])
    ).astype(BF)
    back_ref[:, :HALF] = dot_tn(perm_ref[...], g_ref[:, 3 * HALF :]).astype(BF)
    back_ref[:, HALF:] = dot_tn(perm_ref[...], part).astype(BF)


def whole(shape):
    return pl.BlockSpec(shape, lambda i: (0,) * len(shape))


def attention_call(kernel, half, tokens, w_qkv, w_out, tables, outs):
    def columns(which):
        return pl.BlockSpec((D, HALF), lambda i: (0, 2 * which + half))

    return pl.pallas_call(
        kernel,
        grid=(1,),
        in_specs=[whole(t.shape) for t in tokens]
        + [
            columns(0),
            columns(1),
            columns(2),
            pl.BlockSpec((HALF, D), lambda i: (half, 0)),
        ]
        + [whole(t.shape) for t in tables],
        out_specs=[whole(s) for s, _ in outs],
        out_shape=[jax.ShapeDtypeStruct(s, t) for s, t in outs],
        scratch_shapes=[pltpu.VMEM((TOK, HALF), BF)] * 4 + [pltpu.VMEM((128, HALF), F32)] * 2,
        compiler_params=params(60),
        cost_estimate=cost(30),
    )(*tokens, w_qkv, w_qkv, w_qkv, w_out, *tables)


def angle_tables(positions):
    half = HDIM // 2
    base = 10000.0 * 4.0 ** (HDIM / (HDIM - 2.0))
    steps = np.arange(half, dtype=np.float32)
    freq = np.exp(-(2.0 * steps / HDIM) * np.float32(math.log(base))).astype(np.float32)
    angle = positions.astype(np.float32)[:, None] * freq[None, :]
    cos = np.cos(angle).astype(np.float32)
    sin = np.sin(angle).astype(np.float32)
    cos = np.tile(np.concatenate([cos, cos], 1), (1, HEADS // 2))
    sin = np.tile(np.concatenate([-sin, sin], 1), (1, HEADS // 2))
    return jnp.asarray(cos), jnp.asarray(sin)


def col_order():
    order = np.zeros((TOK, TOK), np.float32)
    for pair in range(4):
        for src in range(16):
            for c in range(2):
                for r in range(ROWS):
                    order[pair * 128 + src * 8 + c * 4 + r, src * 32 + r * 8 + pair * 2 + c] = 1.0
    token = np.arange(128)
    positions = (token // 8) * 4 + token % 4
    column = (token // 4) % 2
    mask = np.where(column[:, None] == column[None, :], 0.0, -1e30).astype(np.float32)
    return jnp.asarray(order, BF), positions, jnp.asarray(mask)


def grads_kernel(*refs):
    pick_ref, pick_o_ref, out_ref = refs[-3:]
    sides = (refs[:6], refs[6:12])
    step = pl.program_id(0)

    def both(first, second, pick, cols):
        return jnp.concatenate(
            [dot_nt(pick, ref[:, cols]).astype(BF) for ref in (first, second)], axis=1
        )

    def product(left, first, second):
        return dot(left[:, :TOK], first[...]) + dot(left[:, TOK:], second[...])

    for z in range(4):

        @pl.when(step == z)
        def _():
            lefts = ([], [])
            rows = ([], [])
            for sub in range(4):
                lo, hi = 240 * (z * 4 + sub), 240 * (z * 4 + sub) + 240
                for which in range(3):
                    for half in range(2):
                        base = which * D + half * HALF
                        a, b = max(lo, base), min(hi, base + HALF)
                        if a >= b:
                            continue
                        shift = which * HALF - base
                        lefts[half].append(
                            both(
                                sides[half][2],
                                sides[half][3],
                                pick_ref[:, a - lo : b - lo],
                                slice(a + shift, b + shift),
                            )
                        )
                        rows[half].append(sub)
            totals = [None] * 4
            extra = []
            for half in range(2):
                y0, y1, g0, g1, c0, c1 = sides[half]
                result = product(jnp.concatenate(lefts[half], axis=0), y0, y1)
                for i, sub in enumerate(rows[half]):
                    term = result[128 * i : 128 * i + 128]
                    totals[sub] = term if totals[sub] is None else totals[sub] + term
                left = [
                    both(c0, c1, pick_o_ref[...], slice(320 * z + 80 * s, 320 * z + 80 * s + 80))
                    for s in range(4)
                ]
                left = jnp.concatenate(left, axis=0)
                extra.append(
                    product(left, g0.at[:, 3 * HALF : 4 * HALF], g1.at[:, 3 * HALF : 4 * HALF])
                )
            extra = jnp.concatenate(extra, axis=1)
            for sub in range(4):
                for j in range(4):
                    main = totals[sub][32 * j : 32 * j + 32]
                    more = extra[64 * sub + 16 * j : 64 * sub + 16 * j + 16]
                    block = jnp.concatenate([main[:24], main[24:] + more[:8], more[8:]], axis=0)
                    block = block.astype(BF)
                    for t in range(10):
                        out_ref[4 * sub + j, CHUNK * t : CHUNK * t + CHUNK] = block[
                            :, 128 * t : 128 * t + 128
                        ]


def pickers():
    core = lax.axis_index("sp") % 2
    lane = jnp.arange(128)[:, None]
    source = (lane // 32) * 2 + core
    pick = ((jnp.arange(240)[None, :] == source * 30 + lane % 32) & (lane % 32 < 30)).astype(BF)
    lane = jnp.arange(64)[:, None]
    source = (lane // 16) * 2 + core
    pick_o = (
        (jnp.arange(80)[None, :] == source * 10 + lane % 16 - 6) & (lane % 16 >= 6)
    ).astype(BF)
    return pick, pick_o


def weight_grads(row, col, picks):
    ins = (*row, *col, *picks)
    return pl.pallas_call(
        grads_kernel,
        grid=(4,),
        in_specs=[
            pl.BlockSpec(v.shape, lambda z: (0, 0), pipeline_mode=pl.Buffered(1)) for v in ins
        ],
        out_specs=pl.BlockSpec((CHIPS // 4, CHUNK * 10, 128), lambda z: (z, 0, 0)),
        out_shape=jax.ShapeDtypeStruct((CHIPS, CHUNK * 10, 128), BF),
        compiler_params=params(60),
        cost_estimate=cost(16),
    )(*ins)


def other_core(value):
    return lax.ppermute(value, "sp", [(i, i ^ 1) for i in range(16)])


def reduce_scatter(chip, gconv, mask):
    small = gconv.reshape(9, CHIPS, 2, 10).transpose(1, 2, 0, 3).reshape(CHIPS, 2, 90)
    high = small.astype(BF)
    low = (small - high.astype(F32)).astype(BF)
    small = jnp.pad(jnp.concatenate([high, low], axis=1), ((0, 0), (0, SPARE - 4), (0, 38)))
    chip = jnp.concatenate([chip, small], axis=1)
    same_core = [[2 * i + core for i in range(CHIPS)] for core in range(2)]
    got = lax.all_to_all(
        chip, AXES, split_axis=0, concat_axis=0, axis_index_groups=same_core, tiled=True
    )
    total = jnp.sum(got.astype(F32), axis=0)
    small = total[CHUNK * 10 : CHUNK * 10 + 2] + total[CHUNK * 10 + 2 : CHUNK * 10 + 4]
    own, other = mask
    mine = jnp.sum(small * own, axis=0, keepdims=True)
    mine = mine + other_core(jnp.sum(small * other, axis=0, keepdims=True))
    return total[: CHUNK * 10], mine[0, :90]


def join_kernel(back_ref, part_ref, dpart_ref, wo_ref, out_ref, dy_ref):
    back = back_ref[:, 0].reshape(WIDTH, 3 * HALF)
    out_ref[...] = (part_ref[...] + dot(back[:, :HALF], wo_ref[...])).astype(BF)
    dy_ref[...] = (dpart_ref[...] + back[:, HALF:].astype(F32)).astype(BF)


def join(back, part, dpart, w_out):
    row = pl.BlockSpec((WIDTH, D), lambda r: (r, 0))
    return pl.pallas_call(
        join_kernel,
        grid=(ROWS,),
        in_specs=[
            pl.BlockSpec((16, 1, 8, 3 * HALF), lambda r: (0, r, 0, 0)),
            row,
            row,
            pl.BlockSpec((HALF, D), lambda r: (1, 0)),
        ],
        out_specs=[row] * 2,
        out_shape=[jax.ShapeDtypeStruct((TOK, D), BF)] * 2,
        compiler_params=params(60),
        cost_estimate=cost(5),
    )(back, part, dpart, w_out)


def neighbours(cells):
    last = lax.axis_size("sp") - 1
    down = [(i, i + 1) for i in range(last)]
    up = [(i + 1, i) for i in range(last)]
    return (lax.ppermute(cells[ROWS - 1 :], "sp", down), lax.ppermute(cells[:1], "sp", up))


def spread(value):
    return lax.all_to_all(value, "sp", split_axis=0, concat_axis=0, tiled=True)


def shards(patches, conv_w, w_qkv, w_out, cotangent):
    x = patches[0]
    cot = cotangent[0]
    taps = conv_w.reshape(9, D)
    cot_flat = cot.reshape(TOK, D)
    top, bot = neighbours(x)
    y, pair = conv_forward(x, top, bot, cot, taps)
    y_flat = y.reshape(TOK, D)
    pair = spread(pair.reshape(16, 2 * ROWS * 8, D)).reshape(16, 2, ROWS * 8, D)

    cos_w, sin_w = angle_tables(np.arange(WIDTH))
    g_row, part, dpart = attention_call(
        row_kernel, 0, (y_flat, cot_flat), w_qkv, w_out, (cos_w, sin_w),
        [((TOK, 4 * HALF), BF), ((TOK, D), F32), ((TOK, D), F32)],
    )
    pair, g_row, y_late, cot_late, picks = lax.optimization_barrier(
        (pair, g_row, y_flat, cot_flat, pickers())
    )
    row = []
    for value in (y_late, g_row, cot_late):
        row += [value, other_core(value)]
    order, positions, mask = col_order()
    cos_h, sin_h = angle_tables(positions)
    y_col, c_col, g_col, back = attention_call(
        col_kernel, 1, (pair,), w_qkv, w_out, (cos_h, sin_h, mask, order),
        [((TOK, D), BF), ((TOK, D), BF), ((TOK, 4 * HALF), BF), ((TOK, 3 * HALF), BF)],
    )
    returned = spread(back.reshape(16, ROWS * 8, 3 * HALF)).reshape(16, ROWS, 8, 3 * HALF)
    col = []
    for value in (y_col, g_col, c_col):
        col += [value, other_core(value)]
    chip = weight_grads(row, col, picks)
    returned, chip = lax.optimization_barrier((returned, chip))
    layer_out, dy = join(returned, part, dpart, w_out)
    dy = dy.reshape(ROWS, WIDTH, D)
    dtop, dbot = neighbours(dy)
    gconv = conv_gain(x, top, bot, dy)
    gconv, dtop, dbot = lax.optimization_barrier((gconv, dtop, dbot))
    grad_x = conv_backward(dy, dtop, dbot, taps)
    core = lax.axis_index("sp") % 2
    own = (jnp.arange(2)[:, None] == core).astype(F32) * jnp.ones((2, 128), F32)
    gconv, grad_x, mask = lax.optimization_barrier((gconv, grad_x, (own, 1.0 - own)))
    factor = 1.0 / math.sqrt(8 * 64 * 128)
    total, gconv = reduce_scatter(chip, gconv, mask)
    total = total.reshape(10, CHUNK, 128).transpose(0, 2, 1).reshape(D, CHUNK) * factor
    return (
        layer_out.reshape(1, ROWS, WIDTH, D),
        grad_x[None],
        total[:, :30],
        total[:, 30:],
        (gconv * factor).reshape(3, 3, 10),
    )


def solution(mesh):
    slab = P("grp", "sp", None, None)
    return jax.shard_map(
        shards,
        mesh=mesh,
        in_specs=(slab, P(), P(), P(), slab),
        out_specs=(slab, slab, P(None, AXES), P(None, AXES), P(None, None, AXES)),
        check_vma=False,
    )
```

```python
import functools
import math

import jax
import jax.numpy as jnp
import numpy as np
from jax import lax
from jax.experimental import pallas as pl
from jax.experimental.pallas import tpu as pltpu
from jax.sharding import PartitionSpec as P

HEADS = 16
HDIM = 80
D = 1280
HALF = 640
ROWS = 4
WIDTH = 128
TOK = ROWS * WIDTH
AXES = ("grp", "sp")
BF = jnp.bfloat16
F32 = jnp.float32
MIB = 1024 * 1024

CHUNK = 40
CHIPS = 64
SPARE = 8


def dot(a, b):
    return lax.dot_general(a, b, (((1,), (0,)), ((), ())), preferred_element_type=F32)


def dot_nt(a, b):
    return lax.dot_general(a, b, (((1,), (1,)), ((), ())), preferred_element_type=F32)


def dot_tn(a, b):
    return lax.dot_general(a, b, (((0,), (0,)), ((), ())), preferred_element_type=F32)


def params(limit):
    return pltpu.CompilerParams(vmem_limit_bytes=limit * MIB)


def cost(micros):
    return pl.CostEstimate(flops=int(micros * 1.1535e9), bytes_accessed=0, transcendentals=0)


def shifted(value, step):
    index = lax.broadcasted_iota(jnp.int32, value.shape, 0)
    moved = pltpu.roll(value, step % WIDTH, axis=0)
    edge = 0 if step == 1 else WIDTH - 1
    return jnp.where(index == edge, 0.0, moved)


def conv_kernel(x_ref, top_ref, bot_ref, c_ref, k_ref, y_ref, send_ref):
    taps = k_ref[...].astype(F32)
    rows = [top_ref[0].astype(F32)]
    rows += [x_ref[r].astype(F32) for r in range(ROWS)]
    rows += [bot_ref[0].astype(F32)]
    for r in range(ROWS):
        sums = []
        for b in range(3):
            total = taps[b : b + 1] * rows[r]
            total += taps[3 + b : 4 + b] * rows[r + 1]
            total += taps[6 + b : 7 + b] * rows[r + 2]
            sums.append(total)
        out = rows[r + 1] + sums[1] + shifted(sums[0], 1) + shifted(sums[2], -1)
        y_ref[r] = out.astype(BF)
        send_ref[:, 0, r] = out.reshape(16, 8, out.shape[-1]).astype(BF)
        send_ref[:, 1, r] = c_ref[r].reshape(16, 8, out.shape[-1])


def conv_forward(x, top, bot, cot, taps):
    block = 256
    grid = (D // block,)
    row = pl.BlockSpec((1, WIDTH, block), lambda i: (0, 0, i))
    return pl.pallas_call(
        conv_kernel,
        grid=grid,
        in_specs=[
            pl.BlockSpec((ROWS, WIDTH, block), lambda i: (0, 0, i)),
            row,
            row,
            pl.BlockSpec((ROWS, WIDTH, block), lambda i: (0, 0, i)),
            pl.BlockSpec((9, block), lambda i: (0, i)),
        ],
        out_specs=[
            pl.BlockSpec((ROWS, WIDTH, block), lambda i: (0, 0, i)),
            pl.BlockSpec((16, 2, ROWS, 8, block), lambda i: (0, 0, 0, 0, i)),
        ],
        out_shape=[
            jax.ShapeDtypeStruct((ROWS, WIDTH, D), BF),
            jax.ShapeDtypeStruct((16, 2, ROWS, 8, D), BF),
        ],
        compiler_params=params(60),
        cost_estimate=cost(5),
    )(x, top, bot, cot, taps)


def conv_back_kernel(dy_ref, dtop_ref, dbot_ref, k_ref, gx_ref):
    taps = k_ref[...].astype(F32)
    grads = [dtop_ref[0].astype(F32)]
    grads += [dy_ref[r].astype(F32) for r in range(ROWS)]
    grads += [dbot_ref[0].astype(F32)]
    for r in range(ROWS):
        sums = []
        for b in range(3):
            total = taps[b : b + 1] * grads[r + 2]
            total += taps[3 + b : 4 + b] * grads[r + 1]
            total += taps[6 + b : 7 + b] * grads[r]
            sums.append(total)
        mid = grads[r + 1]
        gx_ref[r] = (mid + sums[1] + shifted(sums[0], -1) + shifted(sums[2], 1)).astype(BF)


def conv_gain_kernel(x_ref, top_ref, bot_ref, dy_ref, gk_ref):
    rows = [top_ref[0].astype(F32)]
    rows += [x_ref[r].astype(F32) for r in range(ROWS)]
    rows += [bot_ref[0].astype(F32)]
    gains = [None] * 9
    for r in range(ROWS):
        mid = dy_ref[r].astype(F32)
        near = (shifted(mid, -1), mid, shifted(mid, 1))
        for a in range(3):
            for b in range(3):
                term = rows[r + a] * near[b]
                term = jnp.sum(term.reshape(WIDTH // 8, 8, term.shape[-1]), axis=0)
                slot = a * 3 + b
                gains[slot] = term if gains[slot] is None else gains[slot] + term
    for slot in range(9):
        gk_ref[slot : slot + 1] = jnp.sum(gains[slot], axis=0, keepdims=True)


def blocks(block):
    row = pl.BlockSpec((1, WIDTH, block), lambda i: (0, 0, i))
    slab = pl.BlockSpec((ROWS, WIDTH, block), lambda i: (0, 0, i))
    small = pl.BlockSpec((9, block), lambda i: (0, i))
    return row, slab, small


def conv_backward(dy, dtop, dbot, taps):
    row, slab, small = blocks(256)
    return pl.pallas_call(
        conv_back_kernel,
        grid=(D // 256,),
        in_specs=[slab, row, row, small],
        out_specs=slab,
        out_shape=jax.ShapeDtypeStruct((ROWS, WIDTH, D), BF),
        compiler_params=params(16),
        cost_estimate=cost(4),
    )(dy, dtop, dbot, taps)


def conv_gain(x, top, bot, dy):
    row, slab, small = blocks(256)
    return pl.pallas_call(
        conv_gain_kernel,
        grid=(D // 256,),
        in_specs=[slab, row, row, slab],
        out_specs=small,
        out_shape=jax.ShapeDtypeStruct((9, D), F32),
        compiler_params=params(60),
        cost_estimate=cost(4),
    )(x, top, bot, dy)


def turn(value, cos, sin, first, sign):
    moved = jnp.where(
        first, pltpu.roll(value, HALF - HDIM // 2, axis=1), pltpu.roll(value, HDIM // 2, axis=1)
    )
    return value * cos + moved * sin if sign > 0 else value * cos - moved * sin


def attention(block, q_s, k_s, v_s, d_s, dq_s, dk_s, cos_ref, sin_ref, mask, g_ref):
    scale = 1.0 / math.sqrt(HDIM)
    toks = pl.ds(pl.multiple_of(block * 128, 128), 128)
    cos = cos_ref[...]
    sin = sin_ref[...]
    first = lax.broadcasted_iota(jnp.int32, (128, HALF), 1) % HDIM < HDIM // 2
    q_s[toks] = turn(q_s[toks].astype(F32), cos, sin, first, 1).astype(BF)
    k_s[toks] = turn(k_s[toks].astype(F32), cos, sin, first, 1).astype(BF)
    cols = [slice(h * HDIM, (h + 1) * HDIM) for h in range(HEADS // 2)]
    q = [q_s[toks, c] for c in cols]
    k = [k_s[toks, c] for c in cols]
    v = [v_s[toks, c] for c in cols]
    d_o = [d_s[toks, c] for c in cols]
    scores = [dot_nt(a, b) * scale for a, b in zip(q, k)]
    d_p = [dot_nt(a, b) for a, b in zip(d_o, v)]
    if mask is not None:
        scores = [s + mask for s in scores]
    expo = [jnp.exp(s - jnp.max(s, axis=-1, keepdims=True)) for s in scores]
    prob = [e * (1.0 / jnp.sum(e, axis=-1, keepdims=True)) for e in expo]
    prob_b = [p.astype(BF) for p in prob]
    d_s_b = [
        (p * (x - jnp.sum(p * x, axis=-1, keepdims=True)) * scale).astype(BF)
        for p, x in zip(prob, d_p)
    ]
    for h, c in enumerate(cols):
        g_ref[toks, slice(3 * HALF + c.start, 3 * HALF + c.stop)] = dot(prob_b[h], v[h]).astype(BF)
    for h, c in enumerate(cols):
        g_ref[toks, slice(2 * HALF + c.start, 2 * HALF + c.stop)] = dot_tn(
            prob_b[h], d_o[h]
        ).astype(BF)
    for h, c in enumerate(cols):
        dq_s[:, c] = dot(d_s_b[h], k[h])
    for h, c in enumerate(cols):
        dk_s[:, c] = dot_tn(d_s_b[h], q[h])
    g_ref[toks, slice(0, HALF)] = turn(dq_s[...], cos, sin, first, -1).astype(BF)
    g_ref[toks, slice(HALF, 2 * HALF)] = turn(dk_s[...], cos, sin, first, -1).astype(BF)


def row_kernel(
    y_ref, c_ref, wq_ref, wk_ref, wv_ref, wo_ref, cos_ref, sin_ref,
    g_ref, out_ref, dy_ref, q_s, k_s, v_s, d_s, dq_s, dk_s,
):
    y = y_ref[...]
    cot = c_ref[...]
    q_s[...] = dot(y, wq_ref[...]).astype(BF)
    k_s[...] = dot(y, wk_ref[...]).astype(BF)
    v_s[...] = dot(y, wv_ref[...]).astype(BF)
    d_s[...] = dot_nt(cot, wo_ref[...]).astype(BF)

    @pl.loop(0, TOK // 128)
    def _(block):
        attention(block, q_s, k_s, v_s, d_s, dq_s, dk_s, cos_ref, sin_ref, None, g_ref)

    out_ref[...] = y.astype(F32) + dot(g_ref[:, 3 * HALF :], wo_ref[...])
    dy_ref[...] = (
        cot.astype(F32)
        + dot_nt(g_ref[:, :HALF], wq_ref[...])
        + dot_nt(g_ref[:, HALF : 2 * HALF], wk_ref[...])
        + dot_nt(g_ref[:, 2 * HALF : 3 * HALF], wv_ref[...])
    )


def col_kernel(
    pair_ref, wq_ref, wk_ref, wv_ref, wo_ref, cos_ref, sin_ref, mask_ref, perm_ref,
    yp_ref, cp_ref, g_ref, back_ref, q_s, k_s, v_s, d_s, dq_s, dk_s,
):
    yp_ref[...] = dot(perm_ref[...], pair_ref[:, 0].reshape(TOK, D)).astype(BF)
    cp_ref[...] = dot(perm_ref[...], pair_ref[:, 1].reshape(TOK, D)).astype(BF)
    y = yp_ref[...]
    q_s[...] = dot(y, wq_ref[...]).astype(BF)
    k_s[...] = dot(y, wk_ref[...]).astype(BF)
    v_s[...] = dot(y, wv_ref[...]).astype(BF)
    d_s[...] = dot_nt(cp_ref[...], wo_ref[...]).astype(BF)

    @pl.loop(0, TOK // 128)
    def _(block):
        attention(
            block, q_s, k_s, v_s, d_s, dq_s, dk_s, cos_ref, sin_ref, mask_ref[...], g_ref
        )

    part = (
        dot_nt(g_ref[:, :HALF], wq_ref[...])
        + dot_nt(g_ref[:, HALF : 2 * HALF], wk_ref[...])
        + dot_nt(g_ref[:, 2 * HALF : 3 * HALF], wv_ref[...])
    ).astype(BF)
    back_ref[:, :HALF] = dot_tn(perm_ref[...], g_ref[:, 3 * HALF :]).astype(BF)
    back_ref[:, HALF:] = dot_tn(perm_ref[...], part).astype(BF)


def whole(shape):
    return pl.BlockSpec(shape, lambda i: (0,) * len(shape))


def attention_call(kernel, half, tokens, w_qkv, w_out, tables, outs):
    def columns(which):
        return pl.BlockSpec((D, HALF), lambda i: (0, 2 * which + half))

    return pl.pallas_call(
        kernel,
        grid=(1,),
        in_specs=[whole(t.shape) for t in tokens]
        + [
            columns(0),
            columns(1),
            columns(2),
            pl.BlockSpec((HALF, D), lambda i: (half, 0)),
        ]
        + [whole(t.shape) for t in tables],
        out_specs=[whole(s) for s, _ in outs],
        out_shape=[jax.ShapeDtypeStruct(s, t) for s, t in outs],
        scratch_shapes=[pltpu.VMEM((TOK, HALF), BF)] * 4 + [pltpu.VMEM((128, HALF), F32)] * 2,
        compiler_params=params(60),
        cost_estimate=cost(30),
    )(*tokens, w_qkv, w_qkv, w_qkv, w_out, *tables)


def angle_tables(positions):
    half = HDIM // 2
    base = 10000.0 * 4.0 ** (HDIM / (HDIM - 2.0))
    steps = np.arange(half, dtype=np.float32)
    freq = np.exp(-(2.0 * steps / HDIM) * np.float32(math.log(base))).astype(np.float32)
    angle = positions.astype(np.float32)[:, None] * freq[None, :]
    cos = np.cos(angle).astype(np.float32)
    sin = np.sin(angle).astype(np.float32)
    cos = np.tile(np.concatenate([cos, cos], 1), (1, HEADS // 2))
    sin = np.tile(np.concatenate([-sin, sin], 1), (1, HEADS // 2))
    return jnp.asarray(cos), jnp.asarray(sin)


def col_order():
    order = np.zeros((TOK, TOK), np.float32)
    for pair in range(4):
        for src in range(16):
            for c in range(2):
                for r in range(ROWS):
                    order[pair * 128 + src * 8 + c * 4 + r, src * 32 + r * 8 + pair * 2 + c] = 1.0
    token = np.arange(128)
    positions = (token // 8) * 4 + token % 4
    column = (token // 4) % 2
    mask = np.where(column[:, None] == column[None, :], 0.0, -1e30).astype(np.float32)
    return jnp.asarray(order, BF), positions, jnp.asarray(mask)


def grads_kernel(*refs):
    pick_ref, pick_o_ref, out_ref = refs[-3:]
    sides = (refs[:6], refs[6:12])
    step = pl.program_id(0)

    def both(first, second, pick, cols):
        return jnp.concatenate(
            [dot_nt(pick, ref[:, cols]).astype(BF) for ref in (first, second)], axis=1
        )

    def product(left, first, second):
        return dot(left[:, :TOK], first[...]) + dot(left[:, TOK:], second[...])

    for z in range(4):

        @pl.when(step == z)
        def _():
            lefts = ([], [])
            rows = ([], [])
            for sub in range(4):
                lo, hi = 240 * (z * 4 + sub), 240 * (z * 4 + sub) + 240
                for which in range(3):
                    for half in range(2):
                        base = which * D + half * HALF
                        a, b = max(lo, base), min(hi, base + HALF)
                        if a >= b:
                            continue
                        shift = which * HALF - base
                        lefts[half].append(
                            both(
                                sides[half][2],
                                sides[half][3],
                                pick_ref[:, a - lo : b - lo],
                                slice(a + shift, b + shift),
                            )
                        )
                        rows[half].append(sub)
            totals = [None] * 4
            extra = []
            for half in range(2):
                y0, y1, g0, g1, c0, c1 = sides[half]
                result = product(jnp.concatenate(lefts[half], axis=0), y0, y1)
                for i, sub in enumerate(rows[half]):
                    term = result[128 * i : 128 * i + 128]
                    totals[sub] = term if totals[sub] is None else totals[sub] + term
                left = [
                    both(c0, c1, pick_o_ref[...], slice(320 * z + 80 * s, 320 * z + 80 * s + 80))
                    for s in range(4)
                ]
                left = jnp.concatenate(left, axis=0)
                extra.append(
                    product(left, g0.at[:, 3 * HALF : 4 * HALF], g1.at[:, 3 * HALF : 4 * HALF])
                )
            extra = jnp.concatenate(extra, axis=1)
            for sub in range(4):
                for j in range(4):
                    main = totals[sub][32 * j : 32 * j + 32]
                    more = extra[64 * sub + 16 * j : 64 * sub + 16 * j + 16]
                    block = jnp.concatenate([main[:24], main[24:] + more[:8], more[8:]], axis=0)
                    block = block.astype(BF)
                    for t in range(10):
                        out_ref[4 * sub + j, CHUNK * t : CHUNK * t + CHUNK] = block[
                            :, 128 * t : 128 * t + 128
                        ]


def pickers():
    core = lax.axis_index("sp") % 2
    lane = jnp.arange(128)[:, None]
    source = (lane // 32) * 2 + core
    pick = ((jnp.arange(240)[None, :] == source * 30 + lane % 32) & (lane % 32 < 30)).astype(BF)
    lane = jnp.arange(64)[:, None]
    source = (lane // 16) * 2 + core
    pick_o = (
        (jnp.arange(80)[None, :] == source * 10 + lane % 16 - 6) & (lane % 16 >= 6)
    ).astype(BF)
    return pick, pick_o


def weight_grads(row, col, picks):
    ins = (*row, *col, *picks)
    return pl.pallas_call(
        grads_kernel,
        grid=(4,),
        in_specs=[
            pl.BlockSpec(v.shape, lambda z: (0, 0), pipeline_mode=pl.Buffered(1)) for v in ins
        ],
        out_specs=pl.BlockSpec((CHIPS // 4, CHUNK * 10, 128), lambda z: (z, 0, 0)),
        out_shape=jax.ShapeDtypeStruct((CHIPS, CHUNK * 10, 128), BF),
        compiler_params=params(60),
        cost_estimate=cost(16),
    )(*ins)


def other_core(value):
    return lax.ppermute(value, "sp", [(i, i ^ 1) for i in range(16)])


def reduce_scatter(chip, gconv, mask):
    small = gconv.reshape(9, CHIPS, 2, 10).transpose(1, 2, 0, 3).reshape(CHIPS, 2, 90)
    high = small.astype(BF)
    low = (small - high.astype(F32)).astype(BF)
    small = jnp.pad(jnp.concatenate([high, low], axis=1), ((0, 0), (0, SPARE - 4), (0, 38)))
    chip = jnp.concatenate([chip, small], axis=1)
    same_core = [[2 * i + core for i in range(CHIPS)] for core in range(2)]
    got = lax.all_to_all(
        chip, AXES, split_axis=0, concat_axis=0, axis_index_groups=same_core, tiled=True
    )
    total = jnp.sum(got.astype(F32), axis=0)
    small = total[CHUNK * 10 : CHUNK * 10 + 2] + total[CHUNK * 10 + 2 : CHUNK * 10 + 4]
    own, other = mask
    mine = jnp.sum(small * own, axis=0, keepdims=True)
    mine = mine + other_core(jnp.sum(small * other, axis=0, keepdims=True))
    return total[: CHUNK * 10], mine[0, :90]


def join_kernel(back_ref, part_ref, dpart_ref, wo_ref, out_ref, dy_ref, first_ref, last_ref):
    back = back_ref[:, 0].reshape(WIDTH, 3 * HALF)
    out_ref[...] = (part_ref[...] + dot(back[:, :HALF], wo_ref[...])).astype(BF)
    dy = (dpart_ref[...] + back[:, HALF:].astype(F32)).astype(BF)
    dy_ref[...] = dy

    @pl.when(pl.program_id(0) == 0)
    def _():
        first_ref[...] = dy

    @pl.when(pl.program_id(0) == ROWS - 1)
    def _():
        last_ref[...] = dy


def join(back, part, dpart, w_out):
    row = pl.BlockSpec((WIDTH, D), lambda r: (r, 0))
    return pl.pallas_call(
        join_kernel,
        grid=(ROWS,),
        in_specs=[
            pl.BlockSpec((16, 1, 8, 3 * HALF), lambda r: (0, r, 0, 0)),
            row,
            row,
            pl.BlockSpec((HALF, D), lambda r: (1, 0)),
        ],
        out_specs=[row] * 2 + [pl.BlockSpec((WIDTH, D), lambda r: (0, 0))] * 2,
        out_shape=[jax.ShapeDtypeStruct((TOK, D), BF)] * 2
        + [jax.ShapeDtypeStruct((WIDTH, D), BF)] * 2,
        compiler_params=params(60),
        cost_estimate=cost(5),
    )(back, part, dpart, w_out)


def neighbours(head, tail):
    last = lax.axis_size("sp") - 1
    down = [(i, i + 1) for i in range(last)]
    up = [(i + 1, i) for i in range(last)]
    return (lax.ppermute(tail, "sp", down), lax.ppermute(head, "sp", up))


def spread(value):
    return lax.all_to_all(value, "sp", split_axis=0, concat_axis=0, tiled=True)


def shards(patches, conv_w, w_qkv, w_out, cotangent):
    x = patches[0]
    cot = cotangent[0]
    taps = conv_w.reshape(9, D)
    cot_flat = cot.reshape(TOK, D)
    top, bot = neighbours(x[:1], x[ROWS - 1 :])
    y, pair = conv_forward(x, top, bot, cot, taps)
    y_flat = y.reshape(TOK, D)
    pair = spread(pair.reshape(16, 2 * ROWS * 8, D)).reshape(16, 2, ROWS * 8, D)

    cos_w, sin_w = angle_tables(np.arange(WIDTH))
    g_row, part, dpart = attention_call(
        row_kernel, 0, (y_flat, cot_flat), w_qkv, w_out, (cos_w, sin_w),
        [((TOK, 4 * HALF), BF), ((TOK, D), F32), ((TOK, D), F32)],
    )
    own = (jnp.arange(2)[:, None] == lax.axis_index("sp") % 2).astype(F32)
    own = own * jnp.ones((2, 128), F32)
    pair, g_row, y_late, cot_late, picks, masks = lax.optimization_barrier(
        (pair, g_row, y_flat, cot_flat, pickers(), (own, 1.0 - own))
    )
    row = []
    for value in (y_late, g_row, cot_late):
        row += [value, other_core(value)]
    order, positions, mask = col_order()
    cos_h, sin_h = angle_tables(positions)
    y_col, c_col, g_col, back = attention_call(
        col_kernel, 1, (pair,), w_qkv, w_out, (cos_h, sin_h, mask, order),
        [((TOK, D), BF), ((TOK, D), BF), ((TOK, 4 * HALF), BF), ((TOK, 3 * HALF), BF)],
    )
    returned = spread(back.reshape(16, ROWS * 8, 3 * HALF)).reshape(16, ROWS, 8, 3 * HALF)
    col = []
    for value in (y_col, g_col, c_col):
        col += [value, other_core(value)]
    chip = weight_grads(row, col, picks)
    returned, chip = lax.optimization_barrier((returned, chip))
    layer_out, dy, head, tail = join(returned, part, dpart, w_out)
    dy = dy.reshape(ROWS, WIDTH, D)
    edge = (1, WIDTH, D)
    dtop, dbot = neighbours(head.reshape(edge), tail.reshape(edge))
    gconv = conv_gain(x, top, bot, dy)
    gconv, dtop, dbot = lax.optimization_barrier((gconv, dtop, dbot))
    grad_x = conv_backward(dy, dtop, dbot, taps)
    gconv, grad_x, masks = lax.optimization_barrier((gconv, grad_x, masks))
    factor = 1.0 / math.sqrt(8 * 64 * 128)
    total, gconv = reduce_scatter(chip, gconv, masks)
    total = total.reshape(10, CHUNK, 128).transpose(0, 2, 1).reshape(D, CHUNK) * factor
    return (
        layer_out.reshape(1, ROWS, WIDTH, D),
        grad_x[None],
        total[:, :30],
        total[:, 30:],
        (gconv * factor).reshape(3, 3, 10),
    )


def solution(mesh):
    slab = P("grp", "sp", None, None)
    return jax.shard_map(
        shards,
        mesh=mesh,
        in_specs=(slab, P(), P(), P(), slab),
        out_specs=(slab, slab, P(None, AXES), P(None, AXES), P(None, None, AXES)),
        check_vma=False,
    )
```

```python
import functools
import math

import jax
import jax.numpy as jnp
import numpy as np
from jax import lax
from jax.experimental import pallas as pl
from jax.experimental.pallas import tpu as pltpu
from jax.sharding import PartitionSpec as P

HEADS = 16
HDIM = 80
D = 1280
HALF = 640
ROWS = 4
WIDTH = 128
TOK = ROWS * WIDTH
AXES = ("grp", "sp")
BF = jnp.bfloat16
F32 = jnp.float32
MIB = 1024 * 1024

CHUNK = 40
CHIPS = 64
SPARE = 8


def dot(a, b):
    return lax.dot_general(a, b, (((1,), (0,)), ((), ())), preferred_element_type=F32)


def dot_nt(a, b):
    return lax.dot_general(a, b, (((1,), (1,)), ((), ())), preferred_element_type=F32)


def dot_tn(a, b):
    return lax.dot_general(a, b, (((0,), (0,)), ((), ())), preferred_element_type=F32)


def params(limit):
    return pltpu.CompilerParams(vmem_limit_bytes=limit * MIB)


def cost(micros):
    return pl.CostEstimate(flops=int(micros * 1.1535e9), bytes_accessed=0, transcendentals=0)


def shifted(value, step):
    index = lax.broadcasted_iota(jnp.int32, value.shape, 0)
    moved = pltpu.roll(value, step % WIDTH, axis=0)
    edge = 0 if step == 1 else WIDTH - 1
    return jnp.where(index == edge, 0.0, moved)


def conv_kernel(x_ref, top_ref, bot_ref, c_ref, k_ref, y_ref, send_ref):
    taps = k_ref[...].astype(F32)
    rows = [top_ref[0].astype(F32)]
    rows += [x_ref[r].astype(F32) for r in range(ROWS)]
    rows += [bot_ref[0].astype(F32)]
    for r in range(ROWS):
        sums = []
        for b in range(3):
            total = taps[b : b + 1] * rows[r]
            total += taps[3 + b : 4 + b] * rows[r + 1]
            total += taps[6 + b : 7 + b] * rows[r + 2]
            sums.append(total)
        out = rows[r + 1] + sums[1] + shifted(sums[0], 1) + shifted(sums[2], -1)
        y_ref[r] = out.astype(BF)
        send_ref[:, 0, r] = out.reshape(16, 8, out.shape[-1]).astype(BF)
        send_ref[:, 1, r] = c_ref[r].reshape(16, 8, out.shape[-1])


def conv_forward(x, top, bot, cot, taps):
    block = 640
    grid = (D // block,)
    row = pl.BlockSpec((1, WIDTH, block), lambda i: (0, 0, i))
    return pl.pallas_call(
        conv_kernel,
        grid=grid,
        in_specs=[
            pl.BlockSpec((ROWS, WIDTH, block), lambda i: (0, 0, i)),
            row,
            row,
            pl.BlockSpec((ROWS, WIDTH, block), lambda i: (0, 0, i)),
            pl.BlockSpec((9, block), lambda i: (0, i)),
        ],
        out_specs=[
            pl.BlockSpec((ROWS, WIDTH, block), lambda i: (0, 0, i)),
            pl.BlockSpec((16, 2, ROWS, 8, block), lambda i: (0, 0, 0, 0, i)),
        ],
        out_shape=[
            jax.ShapeDtypeStruct((ROWS, WIDTH, D), BF),
            jax.ShapeDtypeStruct((16, 2, ROWS, 8, D), BF),
        ],
        compiler_params=params(60),
        cost_estimate=cost(5),
    )(x, top, bot, cot, taps)


def conv_back_kernel(dy_ref, dtop_ref, dbot_ref, k_ref, gx_ref):
    taps = k_ref[...].astype(F32)
    grads = [dtop_ref[0].astype(F32)]
    grads += [dy_ref[r].astype(F32) for r in range(ROWS)]
    grads += [dbot_ref[0].astype(F32)]
    for r in range(ROWS):
        sums = []
        for b in range(3):
            total = taps[b : b + 1] * grads[r + 2]
            total += taps[3 + b : 4 + b] * grads[r + 1]
            total += taps[6 + b : 7 + b] * grads[r]
            sums.append(total)
        mid = grads[r + 1]
        gx_ref[r] = (mid + sums[1] + shifted(sums[0], -1) + shifted(sums[2], 1)).astype(BF)


def conv_gain_kernel(x_ref, top_ref, bot_ref, dy_ref, gk_ref):
    rows = [top_ref[0].astype(F32)]
    rows += [x_ref[r].astype(F32) for r in range(ROWS)]
    rows += [bot_ref[0].astype(F32)]
    gains = [None] * 9
    for r in range(ROWS):
        mid = dy_ref[r].astype(F32)
        near = (shifted(mid, -1), mid, shifted(mid, 1))
        for a in range(3):
            for b in range(3):
                term = rows[r + a] * near[b]
                term = jnp.sum(term.reshape(WIDTH // 8, 8, term.shape[-1]), axis=0)
                slot = a * 3 + b
                gains[slot] = term if gains[slot] is None else gains[slot] + term
    for slot in range(9):
        gk_ref[slot : slot + 1] = jnp.sum(gains[slot], axis=0, keepdims=True)


def blocks(block):
    row = pl.BlockSpec((1, WIDTH, block), lambda i: (0, 0, i))
    slab = pl.BlockSpec((ROWS, WIDTH, block), lambda i: (0, 0, i))
    small = pl.BlockSpec((9, block), lambda i: (0, i))
    return row, slab, small


def conv_backward(dy, dtop, dbot, taps):
    row, slab, small = blocks(256)
    return pl.pallas_call(
        conv_back_kernel,
        grid=(D // 256,),
        in_specs=[slab, row, row, small],
        out_specs=slab,
        out_shape=jax.ShapeDtypeStruct((ROWS, WIDTH, D), BF),
        compiler_params=params(16),
        cost_estimate=cost(4),
    )(dy, dtop, dbot, taps)


def conv_gain(x, top, bot, dy):
    row, slab, small = blocks(640)
    return pl.pallas_call(
        conv_gain_kernel,
        grid=(D // 640,),
        in_specs=[slab, row, row, slab],
        out_specs=small,
        out_shape=jax.ShapeDtypeStruct((9, D), F32),
        compiler_params=params(60),
        cost_estimate=cost(4),
    )(x, top, bot, dy)


def turn(value, cos, sin, first, sign):
    moved = jnp.where(
        first, pltpu.roll(value, HALF - HDIM // 2, axis=1), pltpu.roll(value, HDIM // 2, axis=1)
    )
    return value * cos + moved * sin if sign > 0 else value * cos - moved * sin


def attention(block, q_s, k_s, v_s, d_s, dq_s, dk_s, cos_ref, sin_ref, mask, g_ref):
    scale = 1.0 / math.sqrt(HDIM)
    toks = pl.ds(pl.multiple_of(block * 128, 128), 128)
    cos = cos_ref[...]
    sin = sin_ref[...]
    first = lax.broadcasted_iota(jnp.int32, (128, HALF), 1) % HDIM < HDIM // 2
    q_s[toks] = turn(q_s[toks].astype(F32), cos, sin, first, 1).astype(BF)
    k_s[toks] = turn(k_s[toks].astype(F32), cos, sin, first, 1).astype(BF)
    cols = [slice(h * HDIM, (h + 1) * HDIM) for h in range(HEADS // 2)]
    q = [q_s[toks, c] for c in cols]
    k = [k_s[toks, c] for c in cols]
    v = [v_s[toks, c] for c in cols]
    d_o = [d_s[toks, c] for c in cols]
    scores = [dot_nt(a, b) * scale for a, b in zip(q, k)]
    d_p = [dot_nt(a, b) for a, b in zip(d_o, v)]
    if mask is not None:
        scores = [s + mask for s in scores]
    expo = [jnp.exp(s - jnp.max(s, axis=-1, keepdims=True)) for s in scores]
    prob = [e * (1.0 / jnp.sum(e, axis=-1, keepdims=True)) for e in expo]
    prob_b = [p.astype(BF) for p in prob]
    d_s_b = [
        (p * (x - jnp.sum(p * x, axis=-1, keepdims=True)) * scale).astype(BF)
        for p, x in zip(prob, d_p)
    ]
    for h, c in enumerate(cols):
        g_ref[toks, slice(3 * HALF + c.start, 3 * HALF + c.stop)] = dot(prob_b[h], v[h]).astype(BF)
    for h, c in enumerate(cols):
        g_ref[toks, slice(2 * HALF + c.start, 2 * HALF + c.stop)] = dot_tn(
            prob_b[h], d_o[h]
        ).astype(BF)
    for h, c in enumerate(cols):
        dq_s[:, c] = dot(d_s_b[h], k[h])
    for h, c in enumerate(cols):
        dk_s[:, c] = dot_tn(d_s_b[h], q[h])
    g_ref[toks, slice(0, HALF)] = turn(dq_s[...], cos, sin, first, -1).astype(BF)
    g_ref[toks, slice(HALF, 2 * HALF)] = turn(dk_s[...], cos, sin, first, -1).astype(BF)


def row_kernel(
    y_ref, c_ref, wq_ref, wk_ref, wv_ref, wo_ref, cos_ref, sin_ref,
    g_ref, out_ref, dy_ref, q_s, k_s, v_s, d_s, dq_s, dk_s,
):
    y = y_ref[...]
    cot = c_ref[...]
    q_s[...] = dot(y, wq_ref[...]).astype(BF)
    k_s[...] = dot(y, wk_ref[...]).astype(BF)
    v_s[...] = dot(y, wv_ref[...]).astype(BF)
    d_s[...] = dot_nt(cot, wo_ref[...]).astype(BF)

    @pl.loop(0, TOK // 128)
    def _(block):
        attention(block, q_s, k_s, v_s, d_s, dq_s, dk_s, cos_ref, sin_ref, None, g_ref)

    out_ref[...] = y.astype(F32) + dot(g_ref[:, 3 * HALF :], wo_ref[...])
    dy_ref[...] = (
        cot.astype(F32)
        + dot_nt(g_ref[:, :HALF], wq_ref[...])
        + dot_nt(g_ref[:, HALF : 2 * HALF], wk_ref[...])
        + dot_nt(g_ref[:, 2 * HALF : 3 * HALF], wv_ref[...])
    )


def col_kernel(
    pair_ref, wq_ref, wk_ref, wv_ref, wo_ref, cos_ref, sin_ref, mask_ref, perm_ref,
    yp_ref, cp_ref, g_ref, back_ref, q_s, k_s, v_s, d_s, dq_s, dk_s,
):
    yp_ref[...] = dot(perm_ref[...], pair_ref[:, 0].reshape(TOK, D)).astype(BF)
    cp_ref[...] = dot(perm_ref[...], pair_ref[:, 1].reshape(TOK, D)).astype(BF)
    y = yp_ref[...]
    q_s[...] = dot(y, wq_ref[...]).astype(BF)
    k_s[...] = dot(y, wk_ref[...]).astype(BF)
    v_s[...] = dot(y, wv_ref[...]).astype(BF)
    d_s[...] = dot_nt(cp_ref[...], wo_ref[...]).astype(BF)

    @pl.loop(0, TOK // 128)
    def _(block):
        attention(
            block, q_s, k_s, v_s, d_s, dq_s, dk_s, cos_ref, sin_ref, mask_ref[...], g_ref
        )

    part = (
        dot_nt(g_ref[:, :HALF], wq_ref[...])
        + dot_nt(g_ref[:, HALF : 2 * HALF], wk_ref[...])
        + dot_nt(g_ref[:, 2 * HALF : 3 * HALF], wv_ref[...])
    ).astype(BF)
    back_ref[:, :HALF] = dot_tn(perm_ref[...], g_ref[:, 3 * HALF :]).astype(BF)
    back_ref[:, HALF:] = dot_tn(perm_ref[...], part).astype(BF)


def whole(shape):
    return pl.BlockSpec(shape, lambda i: (0,) * len(shape))


def attention_call(kernel, half, tokens, w_qkv, w_out, tables, outs):
    def columns(which):
        return pl.BlockSpec((D, HALF), lambda i: (0, 2 * which + half))

    return pl.pallas_call(
        kernel,
        grid=(1,),
        in_specs=[whole(t.shape) for t in tokens]
        + [
            columns(0),
            columns(1),
            columns(2),
            pl.BlockSpec((HALF, D), lambda i: (half, 0)),
        ]
        + [whole(t.shape) for t in tables],
        out_specs=[whole(s) for s, _ in outs],
        out_shape=[jax.ShapeDtypeStruct(s, t) for s, t in outs],
        scratch_shapes=[pltpu.VMEM((TOK, HALF), BF)] * 4 + [pltpu.VMEM((128, HALF), F32)] * 2,
        compiler_params=params(60),
        cost_estimate=cost(30),
    )(*tokens, w_qkv, w_qkv, w_qkv, w_out, *tables)


def angle_tables(positions):
    half = HDIM // 2
    base = 10000.0 * 4.0 ** (HDIM / (HDIM - 2.0))
    steps = np.arange(half, dtype=np.float32)
    freq = np.exp(-(2.0 * steps / HDIM) * np.float32(math.log(base))).astype(np.float32)
    angle = positions.astype(np.float32)[:, None] * freq[None, :]
    cos = np.cos(angle).astype(np.float32)
    sin = np.sin(angle).astype(np.float32)
    cos = np.tile(np.concatenate([cos, cos], 1), (1, HEADS // 2))
    sin = np.tile(np.concatenate([-sin, sin], 1), (1, HEADS // 2))
    return jnp.asarray(cos), jnp.asarray(sin)


def col_order():
    order = np.zeros((TOK, TOK), np.float32)
    for pair in range(4):
        for src in range(16):
            for c in range(2):
                for r in range(ROWS):
                    order[pair * 128 + src * 8 + c * 4 + r, src * 32 + r * 8 + pair * 2 + c] = 1.0
    token = np.arange(128)
    positions = (token // 8) * 4 + token % 4
    column = (token // 4) % 2
    mask = np.where(column[:, None] == column[None, :], 0.0, -1e30).astype(np.float32)
    return jnp.asarray(order, BF), positions, jnp.asarray(mask)


def grads_kernel(*refs):
    pick_ref, pick_o_ref, out_ref = refs[-3:]
    sides = (refs[:6], refs[6:12])
    step = pl.program_id(0)

    def both(first, second, pick, cols):
        return jnp.concatenate(
            [dot_nt(pick, ref[:, cols]).astype(BF) for ref in (first, second)], axis=1
        )

    def product(left, first, second):
        return dot(left[:, :TOK], first[...]) + dot(left[:, TOK:], second[...])

    for z in range(4):

        @pl.when(step == z)
        def _():
            lefts = ([], [])
            rows = ([], [])
            for sub in range(4):
                lo, hi = 240 * (z * 4 + sub), 240 * (z * 4 + sub) + 240
                for which in range(3):
                    for half in range(2):
                        base = which * D + half * HALF
                        a, b = max(lo, base), min(hi, base + HALF)
                        if a >= b:
                            continue
                        shift = which * HALF - base
                        lefts[half].append(
                            both(
                                sides[half][2],
                                sides[half][3],
                                pick_ref[:, a - lo : b - lo],
                                slice(a + shift, b + shift),
                            )
                        )
                        rows[half].append(sub)
            totals = [None] * 4
            extra = []
            for half in range(2):
                y0, y1, g0, g1, c0, c1 = sides[half]
                result = product(jnp.concatenate(lefts[half], axis=0), y0, y1)
                for i, sub in enumerate(rows[half]):
                    term = result[128 * i : 128 * i + 128]
                    totals[sub] = term if totals[sub] is None else totals[sub] + term
                left = [
                    both(c0, c1, pick_o_ref[...], slice(320 * z + 80 * s, 320 * z + 80 * s + 80))
                    for s in range(4)
                ]
                left = jnp.concatenate(left, axis=0)
                extra.append(
                    product(left, g0.at[:, 3 * HALF : 4 * HALF], g1.at[:, 3 * HALF : 4 * HALF])
                )
            extra = jnp.concatenate(extra, axis=1)
            for sub in range(4):
                for j in range(4):
                    main = totals[sub][32 * j : 32 * j + 32]
                    more = extra[64 * sub + 16 * j : 64 * sub + 16 * j + 16]
                    block = jnp.concatenate([main[:24], main[24:] + more[:8], more[8:]], axis=0)
                    block = block.astype(BF)
                    for t in range(10):
                        out_ref[4 * sub + j, CHUNK * t : CHUNK * t + CHUNK] = block[
                            :, 128 * t : 128 * t + 128
                        ]


def pickers():
    core = lax.axis_index("sp") % 2
    lane = jnp.arange(128)[:, None]
    source = (lane // 32) * 2 + core
    pick = ((jnp.arange(240)[None, :] == source * 30 + lane % 32) & (lane % 32 < 30)).astype(BF)
    lane = jnp.arange(64)[:, None]
    source = (lane // 16) * 2 + core
    pick_o = (
        (jnp.arange(80)[None, :] == source * 10 + lane % 16 - 6) & (lane % 16 >= 6)
    ).astype(BF)
    return pick, pick_o


def weight_grads(row, col, picks):
    ins = (*row, *col, *picks)
    return pl.pallas_call(
        grads_kernel,
        grid=(4,),
        in_specs=[
            pl.BlockSpec(v.shape, lambda z: (0, 0), pipeline_mode=pl.Buffered(1)) for v in ins
        ],
        out_specs=pl.BlockSpec((CHIPS // 4, CHUNK * 10, 128), lambda z: (z, 0, 0)),
        out_shape=jax.ShapeDtypeStruct((CHIPS, CHUNK * 10, 128), BF),
        compiler_params=params(60),
        cost_estimate=cost(16),
    )(*ins)


def other_core(value):
    return lax.ppermute(value, "sp", [(i, i ^ 1) for i in range(16)])


def reduce_scatter(chip, gconv, mask):
    small = gconv.reshape(9, CHIPS, 2, 10).transpose(1, 2, 0, 3).reshape(CHIPS, 2, 90)
    high = small.astype(BF)
    low = (small - high.astype(F32)).astype(BF)
    small = jnp.pad(jnp.concatenate([high, low], axis=1), ((0, 0), (0, SPARE - 4), (0, 38)))
    chip = jnp.concatenate([chip, small], axis=1)
    same_core = [[2 * i + core for i in range(CHIPS)] for core in range(2)]
    got = lax.all_to_all(
        chip, AXES, split_axis=0, concat_axis=0, axis_index_groups=same_core, tiled=True
    )
    total = jnp.sum(got.astype(F32), axis=0)
    small = total[CHUNK * 10 : CHUNK * 10 + 2] + total[CHUNK * 10 + 2 : CHUNK * 10 + 4]
    own, other = mask
    mine = jnp.sum(small * own, axis=0, keepdims=True)
    mine = mine + other_core(jnp.sum(small * other, axis=0, keepdims=True))
    return total[: CHUNK * 10], mine[0, :90]


def join_kernel(back_ref, part_ref, dpart_ref, wo_ref, out_ref, dy_ref, first_ref, last_ref):
    back = back_ref[:, 0].reshape(WIDTH, 3 * HALF)
    out_ref[...] = (part_ref[...] + dot(back[:, :HALF], wo_ref[...])).astype(BF)
    dy = (dpart_ref[...] + back[:, HALF:].astype(F32)).astype(BF)
    dy_ref[...] = dy

    @pl.when(pl.program_id(0) == 0)
    def _():
        first_ref[...] = dy

    @pl.when(pl.program_id(0) == ROWS - 1)
    def _():
        last_ref[...] = dy


def join(back, part, dpart, w_out):
    row = pl.BlockSpec((WIDTH, D), lambda r: (r, 0))
    return pl.pallas_call(
        join_kernel,
        grid=(ROWS,),
        in_specs=[
            pl.BlockSpec((16, 1, 8, 3 * HALF), lambda r: (0, r, 0, 0)),
            row,
            row,
            pl.BlockSpec((HALF, D), lambda r: (1, 0)),
        ],
        out_specs=[row] * 2 + [pl.BlockSpec((WIDTH, D), lambda r: (0, 0))] * 2,
        out_shape=[jax.ShapeDtypeStruct((TOK, D), BF)] * 2
        + [jax.ShapeDtypeStruct((WIDTH, D), BF)] * 2,
        compiler_params=params(60),
        cost_estimate=cost(5),
    )(back, part, dpart, w_out)


def neighbours(head, tail):
    last = lax.axis_size("sp") - 1
    down = [(i, i + 1) for i in range(last)]
    up = [(i + 1, i) for i in range(last)]
    return (lax.ppermute(tail, "sp", down), lax.ppermute(head, "sp", up))


def spread(value):
    return lax.all_to_all(value, "sp", split_axis=0, concat_axis=0, tiled=True)


def shards(patches, conv_w, w_qkv, w_out, cotangent):
    x = patches[0]
    cot = cotangent[0]
    taps = conv_w.reshape(9, D)
    cot_flat = cot.reshape(TOK, D)
    top, bot = neighbours(x[:1], x[ROWS - 1 :])
    y, pair = conv_forward(x, top, bot, cot, taps)
    y_flat = y.reshape(TOK, D)
    pair = spread(pair.reshape(16, 2 * ROWS * 8, D)).reshape(16, 2, ROWS * 8, D)

    cos_w, sin_w = angle_tables(np.arange(WIDTH))
    g_row, part, dpart = attention_call(
        row_kernel, 0, (y_flat, cot_flat), w_qkv, w_out, (cos_w, sin_w),
        [((TOK, 4 * HALF), BF), ((TOK, D), F32), ((TOK, D), F32)],
    )
    own = (jnp.arange(2)[:, None] == lax.axis_index("sp") % 2).astype(F32)
    own = own * jnp.ones((2, 128), F32)
    pair, g_row, y_late, cot_late, picks, masks = lax.optimization_barrier(
        (pair, g_row, y_flat, cot_flat, pickers(), (own, 1.0 - own))
    )
    row = []
    for value in (y_late, g_row, cot_late):
        row += [value, other_core(value)]
    order, positions, mask = col_order()
    cos_h, sin_h = angle_tables(positions)
    y_col, c_col, g_col, back = attention_call(
        col_kernel, 1, (pair,), w_qkv, w_out, (cos_h, sin_h, mask, order),
        [((TOK, D), BF), ((TOK, D), BF), ((TOK, 4 * HALF), BF), ((TOK, 3 * HALF), BF)],
    )
    returned = spread(back.reshape(16, ROWS * 8, 3 * HALF)).reshape(16, ROWS, 8, 3 * HALF)
    col = []
    for value in (y_col, g_col, c_col):
        col += [value, other_core(value)]
    chip = weight_grads(row, col, picks)
    returned, chip = lax.optimization_barrier((returned, chip))
    layer_out, dy, head, tail = join(returned, part, dpart, w_out)
    dy = dy.reshape(ROWS, WIDTH, D)
    edge = (1, WIDTH, D)
    dtop, dbot = neighbours(head.reshape(edge), tail.reshape(edge))
    gconv = conv_gain(x, top, bot, dy)
    gconv, dtop, dbot = lax.optimization_barrier((gconv, dtop, dbot))
    grad_x = conv_backward(dy, dtop, dbot, taps)
    gconv, grad_x, masks = lax.optimization_barrier((gconv, grad_x, masks))
    factor = 1.0 / math.sqrt(8 * 64 * 128)
    total, gconv = reduce_scatter(chip, gconv, masks)
    total = total.reshape(10, CHUNK, 128).transpose(0, 2, 1).reshape(D, CHUNK) * factor
    return (
        layer_out.reshape(1, ROWS, WIDTH, D),
        grad_x[None],
        total[:, :30],
        total[:, 30:],
        (gconv * factor).reshape(3, 3, 10),
    )


def solution(mesh):
    slab = P("grp", "sp", None, None)
    return jax.shard_map(
        shards,
        mesh=mesh,
        in_specs=(slab, P(), P(), P(), slab),
        out_specs=(slab, slab, P(None, AXES), P(None, AXES), P(None, None, AXES)),
        check_vma=False,
    )
```

```python
import functools
import math

import jax
import jax.numpy as jnp
import numpy as np
from jax import lax
from jax.experimental import pallas as pl
from jax.experimental.pallas import tpu as pltpu
from jax.sharding import PartitionSpec as P

HEADS = 16
HDIM = 80
D = 1280
HALF = 640
ROWS = 4
WIDTH = 128
TOK = ROWS * WIDTH
AXES = ("grp", "sp")
BF = jnp.bfloat16
F32 = jnp.float32
MIB = 1024 * 1024

CHUNK = 40
CHIPS = 64
SPARE = 8


def dot(a, b):
    return lax.dot_general(a, b, (((1,), (0,)), ((), ())), preferred_element_type=F32)


def dot_nt(a, b):
    return lax.dot_general(a, b, (((1,), (1,)), ((), ())), preferred_element_type=F32)


def dot_tn(a, b):
    return lax.dot_general(a, b, (((0,), (0,)), ((), ())), preferred_element_type=F32)


def params(limit):
    return pltpu.CompilerParams(vmem_limit_bytes=limit * MIB)


def cost(micros):
    return pl.CostEstimate(flops=int(micros * 1.1535e9), bytes_accessed=0, transcendentals=0)


def shifted(value, step):
    index = lax.broadcasted_iota(jnp.int32, value.shape, 0)
    moved = pltpu.roll(value, step % WIDTH, axis=0)
    edge = 0 if step == 1 else WIDTH - 1
    return jnp.where(index == edge, 0.0, moved)


def conv_kernel(x_ref, top_ref, bot_ref, c_ref, k_ref, y_ref, send_ref):
    taps = k_ref[...].astype(F32)
    rows = [top_ref[0].astype(F32)]
    rows += [x_ref[r].astype(F32) for r in range(ROWS)]
    rows += [bot_ref[0].astype(F32)]
    for r in range(ROWS):
        sums = []
        for b in range(3):
            total = taps[b : b + 1] * rows[r]
            total += taps[3 + b : 4 + b] * rows[r + 1]
            total += taps[6 + b : 7 + b] * rows[r + 2]
            sums.append(total)
        out = rows[r + 1] + sums[1] + shifted(sums[0], 1) + shifted(sums[2], -1)
        y_ref[r] = out.astype(BF)
        send_ref[:, 0, r] = out.reshape(16, 8, out.shape[-1]).astype(BF)
        send_ref[:, 1, r] = c_ref[r].reshape(16, 8, out.shape[-1])


def conv_forward(x, top, bot, cot, taps):
    block = 640
    grid = (D // block,)
    row = pl.BlockSpec((1, WIDTH, block), lambda i: (0, 0, i))
    return pl.pallas_call(
        conv_kernel,
        grid=grid,
        in_specs=[
            pl.BlockSpec((ROWS, WIDTH, block), lambda i: (0, 0, i)),
            row,
            row,
            pl.BlockSpec((ROWS, WIDTH, block), lambda i: (0, 0, i)),
            pl.BlockSpec((9, block), lambda i: (0, i)),
        ],
        out_specs=[
            pl.BlockSpec((ROWS, WIDTH, block), lambda i: (0, 0, i)),
            pl.BlockSpec((16, 2, ROWS, 8, block), lambda i: (0, 0, 0, 0, i)),
        ],
        out_shape=[
            jax.ShapeDtypeStruct((ROWS, WIDTH, D), BF),
            jax.ShapeDtypeStruct((16, 2, ROWS, 8, D), BF),
        ],
        compiler_params=params(60),
        cost_estimate=cost(5),
    )(x, top, bot, cot, taps)


def conv_back_kernel(dy_ref, dtop_ref, dbot_ref, k_ref, gx_ref):
    taps = k_ref[...].astype(F32)
    grads = [dtop_ref[0].astype(F32)]
    grads += [dy_ref[r].astype(F32) for r in range(ROWS)]
    grads += [dbot_ref[0].astype(F32)]
    for r in range(ROWS):
        sums = []
        for b in range(3):
            total = taps[b : b + 1] * grads[r + 2]
            total += taps[3 + b : 4 + b] * grads[r + 1]
            total += taps[6 + b : 7 + b] * grads[r]
            sums.append(total)
        mid = grads[r + 1]
        gx_ref[r] = (mid + sums[1] + shifted(sums[0], -1) + shifted(sums[2], 1)).astype(BF)


def conv_gain_kernel(x_ref, top_ref, bot_ref, dy_ref, gk_ref):
    rows = [top_ref[0].astype(F32)]
    rows += [x_ref[r].astype(F32) for r in range(ROWS)]
    rows += [bot_ref[0].astype(F32)]
    gains = [None] * 9
    for r in range(ROWS):
        mid = dy_ref[r].astype(F32)
        near = (shifted(mid, -1), mid, shifted(mid, 1))
        for a in range(3):
            for b in range(3):
                term = rows[r + a] * near[b]
                term = jnp.sum(term.reshape(WIDTH // 8, 8, term.shape[-1]), axis=0)
                slot = a * 3 + b
                gains[slot] = term if gains[slot] is None else gains[slot] + term
    for slot in range(9):
        gk_ref[slot : slot + 1] = jnp.sum(gains[slot], axis=0, keepdims=True)


def blocks(block):
    row = pl.BlockSpec((1, WIDTH, block), lambda i: (0, 0, i))
    slab = pl.BlockSpec((ROWS, WIDTH, block), lambda i: (0, 0, i))
    small = pl.BlockSpec((9, block), lambda i: (0, i))
    return row, slab, small


def conv_backward(dy, dtop, dbot, taps):
    row, slab, small = blocks(256)
    return pl.pallas_call(
        conv_back_kernel,
        grid=(D // 256,),
        in_specs=[slab, row, row, small],
        out_specs=slab,
        out_shape=jax.ShapeDtypeStruct((ROWS, WIDTH, D), BF),
        compiler_params=params(16),
        cost_estimate=cost(4),
    )(dy, dtop, dbot, taps)


def conv_gain(x, top, bot, dy):
    row, slab, small = blocks(640)
    return pl.pallas_call(
        conv_gain_kernel,
        grid=(D // 640,),
        in_specs=[slab, row, row, slab],
        out_specs=small,
        out_shape=jax.ShapeDtypeStruct((9, D), F32),
        compiler_params=params(60),
        cost_estimate=cost(4),
    )(x, top, bot, dy)


def turn(value, cos, sin, first, sign):
    moved = jnp.where(
        first, pltpu.roll(value, HALF - HDIM // 2, axis=1), pltpu.roll(value, HDIM // 2, axis=1)
    )
    return value * cos + moved * sin if sign > 0 else value * cos - moved * sin


def attention(block, q_s, k_s, v_s, d_s, dq_s, dk_s, cos_ref, sin_ref, mask, g_ref):
    scale = 1.0 / math.sqrt(HDIM)
    toks = pl.ds(pl.multiple_of(block * 128, 128), 128)
    cos = cos_ref[...]
    sin = sin_ref[...]
    first = lax.broadcasted_iota(jnp.int32, (128, HALF), 1) % HDIM < HDIM // 2
    q_s[toks] = turn(q_s[toks].astype(F32), cos, sin, first, 1).astype(BF)
    k_s[toks] = turn(k_s[toks].astype(F32), cos, sin, first, 1).astype(BF)
    cols = [slice(h * HDIM, (h + 1) * HDIM) for h in range(HEADS // 2)]
    q = [q_s[toks, c] for c in cols]
    k = [k_s[toks, c] for c in cols]
    v = [v_s[toks, c] for c in cols]
    d_o = [d_s[toks, c] for c in cols]
    scores = [dot_nt(a, b) * scale for a, b in zip(q, k)]
    d_p = [dot_nt(a, b) for a, b in zip(d_o, v)]
    if mask is not None:
        scores = [s + mask for s in scores]
    expo = [jnp.exp(s - jnp.max(s, axis=-1, keepdims=True)) for s in scores]
    prob = [e * (1.0 / jnp.sum(e, axis=-1, keepdims=True)) for e in expo]
    prob_b = [p.astype(BF) for p in prob]
    d_s_b = [
        (p * (x - jnp.sum(p * x, axis=-1, keepdims=True)) * scale).astype(BF)
        for p, x in zip(prob, d_p)
    ]
    for h, c in enumerate(cols):
        g_ref[toks, slice(3 * HALF + c.start, 3 * HALF + c.stop)] = dot(prob_b[h], v[h]).astype(BF)
    for h, c in enumerate(cols):
        g_ref[toks, slice(2 * HALF + c.start, 2 * HALF + c.stop)] = dot_tn(
            prob_b[h], d_o[h]
        ).astype(BF)
    for h, c in enumerate(cols):
        dq_s[:, c] = dot(d_s_b[h], k[h])
    for h, c in enumerate(cols):
        dk_s[:, c] = dot_tn(d_s_b[h], q[h])
    g_ref[toks, slice(0, HALF)] = turn(dq_s[...], cos, sin, first, -1).astype(BF)
    g_ref[toks, slice(HALF, 2 * HALF)] = turn(dk_s[...], cos, sin, first, -1).astype(BF)


def row_kernel(
    y_ref, c_ref, wq_ref, wk_ref, wv_ref, wo_ref, cos_ref, sin_ref,
    g_ref, out_ref, dy_ref, q_s, k_s, v_s, d_s, dq_s, dk_s,
):
    y = y_ref[...]
    cot = c_ref[...]
    q_s[...] = dot(y, wq_ref[...]).astype(BF)
    k_s[...] = dot(y, wk_ref[...]).astype(BF)
    v_s[...] = dot(y, wv_ref[...]).astype(BF)
    d_s[...] = dot_nt(cot, wo_ref[...]).astype(BF)

    @pl.loop(0, TOK // 128)
    def _(block):
        attention(block, q_s, k_s, v_s, d_s, dq_s, dk_s, cos_ref, sin_ref, None, g_ref)

    out_ref[...] = y.astype(F32) + dot(g_ref[:, 3 * HALF :], wo_ref[...])
    dy_ref[...] = (
        cot.astype(F32)
        + dot_nt(g_ref[:, :HALF], wq_ref[...])
        + dot_nt(g_ref[:, HALF : 2 * HALF], wk_ref[...])
        + dot_nt(g_ref[:, 2 * HALF : 3 * HALF], wv_ref[...])
    )


def col_kernel(
    pair_ref, wq_ref, wk_ref, wv_ref, wo_ref, cos_ref, sin_ref, mask_ref, perm_ref,
    yp_ref, cp_ref, g_ref, back_ref, q_s, k_s, v_s, d_s, dq_s, dk_s,
):
    yp_ref[...] = dot(perm_ref[...], pair_ref[:, 0].reshape(TOK, D)).astype(BF)
    cp_ref[...] = dot(perm_ref[...], pair_ref[:, 1].reshape(TOK, D)).astype(BF)
    y = yp_ref[...]
    q_s[...] = dot(y, wq_ref[...]).astype(BF)
    k_s[...] = dot(y, wk_ref[...]).astype(BF)
    v_s[...] = dot(y, wv_ref[...]).astype(BF)
    d_s[...] = dot_nt(cp_ref[...], wo_ref[...]).astype(BF)

    @pl.loop(0, TOK // 128)
    def _(block):
        attention(
            block, q_s, k_s, v_s, d_s, dq_s, dk_s, cos_ref, sin_ref, mask_ref[...], g_ref
        )

    part = (
        dot_nt(g_ref[:, :HALF], wq_ref[...])
        + dot_nt(g_ref[:, HALF : 2 * HALF], wk_ref[...])
        + dot_nt(g_ref[:, 2 * HALF : 3 * HALF], wv_ref[...])
    ).astype(BF)
    back_ref[:, :HALF] = dot_tn(perm_ref[...], g_ref[:, 3 * HALF :]).astype(BF)
    back_ref[:, HALF:] = dot_tn(perm_ref[...], part).astype(BF)


def whole(shape):
    return pl.BlockSpec(shape, lambda i: (0,) * len(shape))


def attention_call(kernel, half, tokens, w_qkv, w_out, tables, outs):
    def columns(which):
        return pl.BlockSpec((D, HALF), lambda i: (0, 2 * which + half))

    return pl.pallas_call(
        kernel,
        grid=(1,),
        in_specs=[whole(t.shape) for t in tokens]
        + [
            columns(0),
            columns(1),
            columns(2),
            pl.BlockSpec((HALF, D), lambda i: (half, 0)),
        ]
        + [whole(t.shape) for t in tables],
        out_specs=[whole(s) for s, _ in outs],
        out_shape=[jax.ShapeDtypeStruct(s, t) for s, t in outs],
        scratch_shapes=[pltpu.VMEM((TOK, HALF), BF)] * 4 + [pltpu.VMEM((128, HALF), F32)] * 2,
        compiler_params=params(60),
        cost_estimate=cost(30),
    )(*tokens, w_qkv, w_qkv, w_qkv, w_out, *tables)


def angle_tables(positions):
    half = HDIM // 2
    base = 10000.0 * 4.0 ** (HDIM / (HDIM - 2.0))
    steps = np.arange(half, dtype=np.float32)
    freq = np.exp(-(2.0 * steps / HDIM) * np.float32(math.log(base))).astype(np.float32)
    angle = positions.astype(np.float32)[:, None] * freq[None, :]
    cos = np.cos(angle).astype(np.float32)
    sin = np.sin(angle).astype(np.float32)
    cos = np.tile(np.concatenate([cos, cos], 1), (1, HEADS // 2))
    sin = np.tile(np.concatenate([-sin, sin], 1), (1, HEADS // 2))
    return jnp.asarray(cos), jnp.asarray(sin)


def col_order():
    order = np.zeros((TOK, TOK), np.float32)
    for pair in range(4):
        for src in range(16):
            for c in range(2):
                for r in range(ROWS):
                    order[pair * 128 + src * 8 + c * 4 + r, src * 32 + r * 8 + pair * 2 + c] = 1.0
    token = np.arange(128)
    positions = (token // 8) * 4 + token % 4
    column = (token // 4) % 2
    mask = np.where(column[:, None] == column[None, :], 0.0, -1e30).astype(np.float32)
    return jnp.asarray(order, BF), positions, jnp.asarray(mask)


def grads_kernel(*refs):
    pick_ref, pick_o_ref, out_ref = refs[-3:]
    sides = (refs[:6], refs[6:12])
    step = pl.program_id(0)

    def both(first, second, pick, cols):
        return jnp.concatenate(
            [dot_nt(pick, ref[:, cols]).astype(BF) for ref in (first, second)], axis=1
        )

    def product(left, first, second):
        return dot(left[:, :TOK], first[...]) + dot(left[:, TOK:], second[...])

    for z in range(4):

        @pl.when(step == z)
        def _():
            lefts = ([], [])
            rows = ([], [])
            for sub in range(4):
                lo, hi = 240 * (z * 4 + sub), 240 * (z * 4 + sub) + 240
                for which in range(3):
                    for half in range(2):
                        base = which * D + half * HALF
                        a, b = max(lo, base), min(hi, base + HALF)
                        if a >= b:
                            continue
                        shift = which * HALF - base
                        lefts[half].append(
                            both(
                                sides[half][2],
                                sides[half][3],
                                pick_ref[:, a - lo : b - lo],
                                slice(a + shift, b + shift),
                            )
                        )
                        rows[half].append(sub)
            totals = [None] * 4
            extra = []
            for half in range(2):
                y0, y1, g0, g1, c0, c1 = sides[half]
                result = product(jnp.concatenate(lefts[half], axis=0), y0, y1)
                for i, sub in enumerate(rows[half]):
                    term = result[128 * i : 128 * i + 128]
                    totals[sub] = term if totals[sub] is None else totals[sub] + term
                left = [
                    both(c0, c1, pick_o_ref[...], slice(320 * z + 80 * s, 320 * z + 80 * s + 80))
                    for s in range(4)
                ]
                left = jnp.concatenate(left, axis=0)
                extra.append(
                    product(left, g0.at[:, 3 * HALF : 4 * HALF], g1.at[:, 3 * HALF : 4 * HALF])
                )
            extra = jnp.concatenate(extra, axis=1)
            for sub in range(4):
                for j in range(4):
                    main = totals[sub][32 * j : 32 * j + 32]
                    more = extra[64 * sub + 16 * j : 64 * sub + 16 * j + 16]
                    block = jnp.concatenate([main[:24], main[24:] + more[:8], more[8:]], axis=0)
                    block = block.astype(BF)
                    for t in range(10):
                        out_ref[4 * sub + j, CHUNK * t : CHUNK * t + CHUNK] = block[
                            :, 128 * t : 128 * t + 128
                        ]


def pickers():
    core = lax.axis_index("sp") % 2
    lane = jnp.arange(128)[:, None]
    source = (lane // 32) * 2 + core
    pick = ((jnp.arange(240)[None, :] == source * 30 + lane % 32) & (lane % 32 < 30)).astype(BF)
    lane = jnp.arange(64)[:, None]
    source = (lane // 16) * 2 + core
    pick_o = (
        (jnp.arange(80)[None, :] == source * 10 + lane % 16 - 6) & (lane % 16 >= 6)
    ).astype(BF)
    return pick, pick_o


def weight_grads(row, col, picks):
    ins = (*row, *col, *picks)
    return pl.pallas_call(
        grads_kernel,
        grid=(4,),
        in_specs=[
            pl.BlockSpec(v.shape, lambda z: (0, 0), pipeline_mode=pl.Buffered(1)) for v in ins
        ],
        out_specs=pl.BlockSpec((CHIPS // 4, CHUNK * 10, 128), lambda z: (z, 0, 0)),
        out_shape=jax.ShapeDtypeStruct((CHIPS, CHUNK * 10, 128), BF),
        compiler_params=params(60),
        cost_estimate=cost(16),
    )(*ins)


def other_core(value):
    return lax.ppermute(value, "sp", [(i, i ^ 1) for i in range(16)])


def reduce_scatter(chip, gconv, mask):
    small = gconv.reshape(9, CHIPS, 2, 10).transpose(1, 2, 0, 3).reshape(CHIPS, 2, 90)
    high = small.astype(BF)
    low = (small - high.astype(F32)).astype(BF)
    small = jnp.pad(jnp.concatenate([high, low], axis=1), ((0, 0), (0, SPARE - 4), (0, 38)))
    chip = jnp.concatenate([chip, small], axis=1)
    same_core = [[2 * i + core for i in range(CHIPS)] for core in range(2)]
    got = lax.all_to_all(
        chip, AXES, split_axis=0, concat_axis=0, axis_index_groups=same_core, tiled=True
    )
    total = jnp.sum(got.astype(F32), axis=0)
    small = total[CHUNK * 10 : CHUNK * 10 + 2] + total[CHUNK * 10 + 2 : CHUNK * 10 + 4]
    own, other = mask
    mine = jnp.sum(small * own, axis=0, keepdims=True)
    mine = mine + other_core(jnp.sum(small * other, axis=0, keepdims=True))
    return total[: CHUNK * 10], mine[0, :90]


def join_kernel(back_ref, part_ref, dpart_ref, wo_ref, out_ref, dy_ref, first_ref, last_ref):
    back = back_ref[:, 0].reshape(WIDTH, 3 * HALF)
    out_ref[...] = (part_ref[...] + dot(back[:, :HALF], wo_ref[...])).astype(BF)
    dy = (dpart_ref[...] + back[:, HALF:].astype(F32)).astype(BF)
    dy_ref[...] = dy

    @pl.when(pl.program_id(0) == 0)
    def _():
        first_ref[...] = dy

    @pl.when(pl.program_id(0) == ROWS - 1)
    def _():
        last_ref[...] = dy


def join(back, part, dpart, w_out):
    row = pl.BlockSpec((WIDTH, D), lambda r: (r, 0))
    return pl.pallas_call(
        join_kernel,
        grid=(ROWS,),
        in_specs=[
            pl.BlockSpec((16, 1, 8, 3 * HALF), lambda r: (0, r, 0, 0)),
            row,
            row,
            pl.BlockSpec((HALF, D), lambda r: (1, 0)),
        ],
        out_specs=[row] * 2 + [pl.BlockSpec((WIDTH, D), lambda r: (0, 0))] * 2,
        out_shape=[jax.ShapeDtypeStruct((TOK, D), BF)] * 2
        + [jax.ShapeDtypeStruct((WIDTH, D), BF)] * 2,
        compiler_params=params(48),
        cost_estimate=cost(5),
    )(back, part, dpart, w_out)


def neighbours(head, tail):
    last = lax.axis_size("sp") - 1
    down = [(i, i + 1) for i in range(last)]
    up = [(i + 1, i) for i in range(last)]
    return (lax.ppermute(tail, "sp", down), lax.ppermute(head, "sp", up))


def spread(value):
    return lax.all_to_all(value, "sp", split_axis=0, concat_axis=0, tiled=True)


def shards(patches, conv_w, w_qkv, w_out, cotangent):
    x = patches[0]
    cot = cotangent[0]
    taps = conv_w.reshape(9, D)
    cot_flat = cot.reshape(TOK, D)
    top, bot = neighbours(x[:1], x[ROWS - 1 :])
    y, pair = conv_forward(x, top, bot, cot, taps)
    y_flat = y.reshape(TOK, D)
    pair = spread(pair.reshape(16, 2 * ROWS * 8, D)).reshape(16, 2, ROWS * 8, D)

    cos_w, sin_w = angle_tables(np.arange(WIDTH))
    g_row, part, dpart = attention_call(
        row_kernel, 0, (y_flat, cot_flat), w_qkv, w_out, (cos_w, sin_w),
        [((TOK, 4 * HALF), BF), ((TOK, D), F32), ((TOK, D), F32)],
    )
    own = (jnp.arange(2)[:, None] == lax.axis_index("sp") % 2).astype(F32)
    own = own * jnp.ones((2, 128), F32)
    pair, g_row, y_late, cot_late, picks, masks = lax.optimization_barrier(
        (pair, g_row, y_flat, cot_flat, pickers(), (own, 1.0 - own))
    )
    row = []
    for value in (y_late, g_row, cot_late):
        row += [value, other_core(value)]
    order, positions, mask = col_order()
    cos_h, sin_h = angle_tables(positions)
    y_col, c_col, g_col, back = attention_call(
        col_kernel, 1, (pair,), w_qkv, w_out, (cos_h, sin_h, mask, order),
        [((TOK, D), BF), ((TOK, D), BF), ((TOK, 4 * HALF), BF), ((TOK, 3 * HALF), BF)],
    )
    returned = spread(back.reshape(16, ROWS * 8, 3 * HALF)).reshape(16, ROWS, 8, 3 * HALF)
    col = []
    for value in (y_col, g_col, c_col):
        col += [value, other_core(value)]
    chip = weight_grads(row, col, picks)
    returned, chip = lax.optimization_barrier((returned, chip))
    layer_out, dy, head, tail = join(returned, part, dpart, w_out)
    dy = dy.reshape(ROWS, WIDTH, D)
    edge = (1, WIDTH, D)
    dtop, dbot = neighbours(head.reshape(edge), tail.reshape(edge))
    gconv = conv_gain(x, top, bot, dy)
    gconv, dtop, dbot = lax.optimization_barrier((gconv, dtop, dbot))
    grad_x = conv_backward(dy, dtop, dbot, taps)
    gconv, grad_x, masks = lax.optimization_barrier((gconv, grad_x, masks))
    factor = 1.0 / math.sqrt(8 * 64 * 128)
    total, gconv = reduce_scatter(chip, gconv, masks)
    total = total.reshape(10, CHUNK, 128).transpose(0, 2, 1).reshape(D, CHUNK) * factor
    return (
        layer_out.reshape(1, ROWS, WIDTH, D),
        grad_x[None],
        total[:, :30],
        total[:, 30:],
        (gconv * factor).reshape(3, 3, 10),
    )


def solution(mesh):
    slab = P("grp", "sp", None, None)
    return jax.shard_map(
        shards,
        mesh=mesh,
        in_specs=(slab, P(), P(), P(), slab),
        out_specs=(slab, slab, P(None, AXES), P(None, AXES), P(None, None, AXES)),
        check_vma=False,
    )
```
